32 devices in a mesh: row: 8 (over z, y), col: 4 (over x, core).
Axes of the slice: x: 2, y: 2, z: 4, core: 2. Of those that a mesh axis runs over, the one named last changes fastest.
Arguments:
- tokens: bfloat16 [2, 8192, 2048], P(None, ('row', 'col')), may hold values from -6 to 6
- cotangent: bfloat16 [2, 8192, 2048], P(None, ('row', 'col')), may hold values from -6 to 6
- segment_of: int32 [2, 8192], P(None, 'row'), may hold values from 0 to 12, as said below
- leaf_parent: int32 [2, 64], P(None, 'row'), may hold values from 0 to 3
- w_qkv: float32 [2048, 8, 384], P('row', 'col'), may hold values from -0.4375 to 0.4375
- mom_qkv: float32 [2, 2048, 8, 384], P(None, 'row', 'col'), as said below
- w_out: float32 [2048, 2048], P('col', 'row'), may hold values from -0.5 to 0.5
- mom_out: float32 [2, 2048, 2048], P(None, 'col', 'row'), as said below
- w_gu: float32 [2, 2048, 8192], P(None, 'row', 'col'), may hold values from -0.125 to 0.125
- mom_gu: float32 [2, 2, 2048, 8192], P(None, None, 'row', 'col'), as said below
- w_down: float32 [8192, 2048], P('col', 'row')
- mom_down: float32 [2, 8192, 2048], P(None, 'col', 'row'), as said below
- gains: float32 [2, 2048], replicated, may hold values from 0.25 to 3, as said below
- mom_gains: float32 [2, 2, 2048], replicated, as said below
Outputs:
- mixed: bfloat16 [2, 8192, 2048], P(None, ('row', 'col'))
- d_tokens: float32 [2, 8192, 2048], P(None, ('row', 'col'))
- grad_norm: float32 [], replicated
- new_qkv: float32 [2048, 8, 384], P('row', 'col')
- moments_qkv: float32 [2, 2048, 8, 384], P(None, 'row', 'col')
- copy_qkv: bfloat16 [2048, 8, 384], P('row', 'col')
- new_out: float32 [2048, 2048], P('col', 'row')
- moments_out: float32 [2, 2048, 2048], P(None, 'col', 'row')
- copy_out: bfloat16 [2048, 2048], P('col', 'row')
- new_gu: float32 [2, 2048, 8192], P(None, 'row', 'col')
- moments_gu: float32 [2, 2, 2048, 8192], P(None, None, 'row', 'col')
- copy_gu: bfloat16 [2, 2048, 8192], P(None, 'row', 'col')
- new_down: float32 [8192, 2048], P('col', 'row')
- moments_down: float32 [2, 8192, 2048], P(None, 'col', 'row')
- copy_down: bfloat16 [8192, 2048], P('col', 'row')
- new_gains: float32 [2, 2048], replicated
- moments_gains: float32 [2, 2, 2048], replicated
The draws below stay inside these ranges and needn't reach their ends.
Inputs may be any that keep to these rules, and one draw needn't show every extreme that they name: `segment_of`: in each tree (1024 tokens of one micro-batch that one index of row holds) the segments stand as runs in order: the trunk (0) of 256 tokens, branches 1 to 4, leaves 4 + 1 to 12. A branch holds 32 to 96 tokens, branches 1 and 2, and 3 and 4, 128 together; a leaf 64 // 2 to 96, consecutive pairs of leaves 2 * 64 together. `gains`: positive. `mom_qkv`: the second member of the first dimension is positive. `mom_out`: the second member of the first dimension is positive. `mom_gu`: the second member of the first dimension is positive. `mom_down`: the second member of the first dimension is positive. `mom_gains`: the second member of the first dimension is positive.
All inputs are finite; a program needn't handle non-finite values.
Results may differ from the reference program's by a relative error of at most 0.025.
Values may be sent and summed in bfloat16 or wider, within the bound.
A program may use at most 272 MiB of HBM per device.

```python
import math
import jax
import jax.numpy as jnp
from jax import lax

D = 2048
FF = 8192
HD = 64
KVH = 8
GROUP = 4
TRUNK = 256
BRANCH = 64
LEAF = 64
NBRANCH = 4
NLEAF = 8
MICRO = 2
STEP = 7
H = 32
QKVW = 384
TREE = 1024
TOKENS_M = 8192
N_ROW = 8
N_COL = 4


def draw_segment_of(key, part):
    trees = MICRO * (TOKENS_M // TREE)
    branch_key, leaf_key = jax.random.split(key)
    branch_half = BRANCH // 2
    branch_shift = jax.random.randint(branch_key, (trees, NBRANCH // 2), -branch_half, branch_half + 1)
    branch_lens = BRANCH + jnp.stack([branch_shift, -branch_shift], axis=-1).reshape(trees, NBRANCH)
    leaf_half = LEAF // 2
    leaf_shift = jax.random.randint(leaf_key, (trees, NLEAF // 2), -leaf_half, leaf_half + 1)
    leaf_lens = LEAF + jnp.stack([leaf_shift, -leaf_shift], axis=-1).reshape(trees, NLEAF)
    lengths = jnp.concatenate([TRUNK * jnp.ones((trees, 1), jnp.int32), branch_lens.astype(jnp.int32), leaf_lens.astype(jnp.int32)], axis=1)
    seg_ends = jnp.cumsum(lengths, axis=1).astype(jnp.int32)
    places = jnp.arange(TREE, dtype=jnp.int32)
    segments = jnp.sum((places[None, :, None] >= seg_ends[:, None, :]).astype(jnp.int32), axis=2)
    return segments.astype(jnp.int32).reshape(MICRO, TOKENS_M)


def rising(length, rise_ratio):
    return jnp.exp(jnp.arange(length, dtype=jnp.float32) * (math.log(rise_ratio) / length)) / math.sqrt(rise_ratio)


def draw_gains(key, part):
    rise_ratio = 3.0
    jitter = jnp.exp(jax.random.uniform(key, (2, D), jnp.float32, -0.22, 0.22))
    return rising(D, rise_ratio)[None, :] * jitter


def draw_w_down(key, part):
    rise_ratio = 3.0
    noise = jax.random.truncated_normal(key, -4.0, 4.0, (FF, D), jnp.float32)
    return noise * rising(FF, rise_ratio)[:, None] * max(FF // 64, 1) ** (-0.5)


def grad_size(kind_ratio):
    count_qkv = D * KVH * (GROUP + 2) * HD
    count_out = KVH * GROUP * HD * D
    count_gu = 2 * D * FF
    count_down = FF * D
    total_count = count_qkv + count_out + count_gu + count_down + 2 * D
    weighted = count_qkv * 0.64 + count_out * 0.01 + count_gu * 0.3025 + count_down * 0.0169 + 2 * D * 2.25
    return kind_ratio * math.sqrt(total_count / weighted)


def moment_pair(key, array_shape, kind_ratio):
    grad_scale = grad_size(kind_ratio)
    sign_key, size_key = jax.random.split(key)
    first_moment = grad_scale * jax.random.truncated_normal(sign_key, -4.0, 4.0, array_shape, jnp.float32)
    second_moment = grad_scale * grad_scale * jnp.exp(jax.random.uniform(size_key, array_shape, jnp.float32, 0.0, math.log(4.0)))
    return jnp.stack([first_moment, second_moment])


def draw_mom_qkv(key, part):
    return moment_pair(key, (D, KVH, (GROUP + 2) * HD), 0.8)


def draw_mom_out(key, part):
    return moment_pair(key, (KVH * GROUP * HD, D), 0.1)


def draw_mom_gu(key, part):
    return moment_pair(key, (2, D, FF), 0.55)


def draw_mom_down(key, part):
    return moment_pair(key, (FF, D), 0.13)


def draw_mom_gains(key, part):
    return moment_pair(key, (2, D), 1.5)


def touch_ends(entries, key, least, high):
    longest = entries.shape.index(max(entries.shape))
    spots = []
    for shift in (0, 1):
        where = [jax.random.randint(jax.random.fold_in(key, axis), (), 0, length) for axis, length in enumerate(entries.shape)]
        where[longest] = (where[longest] + shift) % entries.shape[longest]
        spots.append(tuple(where))
    return entries.at[spots[0]].set(least).at[spots[1]].set(high)


def level_of(rng, extent, pieces, low, top_value):
    def one(axis_at, shards_of):
        heights = jax.random.uniform(jax.random.fold_in(jax.random.fold_in(rng, 6), axis_at), (shards_of,), jnp.float32, low / len(pieces), top_value / len(pieces))
        return jnp.repeat(jnp.exp(heights), extent[axis_at] // shards_of).reshape((-1,) + (1,) * (len(extent) - axis_at - 1))

    factor_of = one(*pieces[0])
    for cut in pieces[1:]:
        factor_of = factor_of * one(*cut)
    return factor_of


def bell_draw(key, dims, width, most, shards=(), kind=jnp.bfloat16):
    drawn = jax.random.normal(key, dims, jnp.float32) * width
    if len(shards) > 0:
        drawn = level_of(key, dims, shards, -0.22, 0.18) * drawn
    return jnp.clip(drawn, min=-most, max=most).astype(kind)


def setup_inputs(seed: int = 0) -> dict:
    splits = jax.random.split(jax.random.key(seed), 15)
    return {
        "tokens": bell_draw(splits[0], (MICRO, TOKENS_M, D), 1.0, 6.0, ((1, 32),)),
        "cotangent": bell_draw(splits[1], (MICRO, TOKENS_M, D), 1.0, 6.0, ((1, 32),)),
        "segment_of": draw_segment_of(jax.random.fold_in(splits[14], 71), 0),
        "leaf_parent": touch_ends(jax.random.randint(splits[3], (MICRO, N_ROW * NLEAF), 0, NBRANCH), jax.random.fold_in(splits[3], 1), 0, NBRANCH - 1).astype(jnp.int32),
        "w_qkv": bell_draw(splits[4], (D, KVH, QKVW), (max(D // 12, 1)) ** -0.5, 0.4375, ((0, 8), (1, 4)), jnp.float32),
        "mom_qkv": draw_mom_qkv(jax.random.fold_in(splits[14], 71), 0),
        "w_out": bell_draw(splits[6], (H * HD, D), (max(D // 16, 1)) ** -0.5, 0.5, ((0, 4), (1, 8)), jnp.float32),
        "mom_out": draw_mom_out(jax.random.fold_in(splits[14], 71), 0),
        "w_gu": bell_draw(splits[8], (2, D, FF), D ** -0.5, 0.125, ((1, 8), (2, 4)), jnp.float32),
        "mom_gu": draw_mom_gu(jax.random.fold_in(splits[14], 71), 0),
        "w_down": draw_w_down(jax.random.fold_in(splits[14], 71), 0),
        "mom_down": draw_mom_down(jax.random.fold_in(splits[14], 71), 0),
        "gains": draw_gains(jax.random.fold_in(splits[14], 71), 0),
        "mom_gains": draw_mom_gains(jax.random.fold_in(splits[14], 71), 0),
    }


highest = lax.Precision.HIGHEST
norm_eps = 1e-05
residual_mult = 0.22
score_mult = 0.015625
rope_theta = 10000000.0
beta_one = 0.5
beta_two = 0.55
adam_eps = 1e-08
weight_decay = 0.1
masked_value = -1e+30

@jax.custom_vjp
def low(v):
    return lax.optimization_barrier(v.astype(jnp.bfloat16)).astype(jnp.float32)

@jax.custom_vjp
def low_back(v):
    return v

def low_keep(v):
    return (low(v), None)

def low_pass(kept, grad):
    return (grad,)

def back_keep(v):
    return (v, None)

def back_low(kept, grad):
    return (low(grad),)
low.defvjp(low_keep, low_pass)
low_back.defvjp(back_keep, back_low)

def param_count():
    return D * KVH * (GROUP + 2) * HD + KVH * GROUP * HD * D + 3 * D * FF + 2 * D

def clip_bound():
    return math.sqrt(param_count())

def step_rates():
    return (max(D // 12, 1) ** (-0.5), max(D // 16, 1) ** (-0.5), D ** (-0.5), max(FF // 64, 1) ** (-0.5), 0.3)

def tree_tables(segments, parents):
    seg_count = 1 + NBRANCH + NLEAF
    seg_ids = jnp.arange(seg_count, dtype=jnp.int32)
    member = (segments[:, None] == seg_ids[None, :]).astype(jnp.int32)
    seg_lengths = lax.optimization_barrier(jnp.sum(member, axis=0)).astype(jnp.int32)
    seg_starts = jnp.cumsum(seg_lengths).astype(jnp.int32) - seg_lengths
    branch_ids = jnp.arange(NBRANCH, dtype=jnp.int32)
    parent_pick = (parents[:, None] == branch_ids[None, :]).astype(jnp.int32)
    parent_len = lax.optimization_barrier(jnp.sum(parent_pick * seg_lengths[1:1 + NBRANCH][None, :], axis=1)).astype(jnp.int32)
    trunk_len = seg_lengths[0]
    base_depth = jnp.concatenate([jnp.zeros((1,), jnp.int32), trunk_len * jnp.ones((NBRANCH,), jnp.int32), trunk_len + parent_len])
    places = jnp.arange(segments.shape[0], dtype=jnp.int32)
    depth = places + lax.optimization_barrier(jnp.sum(member * (base_depth - seg_starts)[None, :], axis=1)).astype(jnp.int32)
    identity = (seg_ids[:, None] == seg_ids[None, :]).astype(jnp.int32)
    rooted = jnp.broadcast_to((seg_ids[None, :] == 0).astype(jnp.int32), (seg_count, seg_count))
    leaf_links = jnp.concatenate([jnp.zeros((NLEAF, 1), jnp.int32), parent_pick, jnp.zeros((NLEAF, NLEAF), jnp.int32)], axis=1)
    leaf_links = jnp.concatenate([jnp.zeros((1 + NBRANCH, seg_count), jnp.int32), leaf_links], axis=0)
    ancestry = jnp.minimum(identity + rooted + leaf_links, 1)
    token_path = jnp.dot(member, ancestry)
    allowed = (jnp.dot(token_path, member.T) > 0) & (depth[None, :] <= depth[:, None])
    freqs = jnp.exp(jnp.arange(HD // 2, dtype=jnp.float32) * (-2.0 * math.log(rope_theta) / HD))
    angles = depth.astype(jnp.float32)[:, None] * freqs[None, :]
    return (allowed, jnp.cos(angles), jnp.sin(angles))

def rotate(vectors, cosines, sines):
    half_width = vectors.shape[-1] // 2
    first_half = vectors[..., :half_width]
    second_half = vectors[..., half_width:]
    return jnp.concatenate([first_half * cosines - second_half * sines, second_half * cosines + first_half * sines], axis=-1)

def rms_norm(values, gain):
    return values * lax.rsqrt(lax.optimization_barrier(jnp.mean(values * values, axis=-1, keepdims=True)) + norm_eps) * gain

def block_forward(x_tree, w_a, w_b, w_c, w_d, gain_pair, cosines, sines, allowed):
    tree_len = x_tree.shape[0]
    attn_in = low(rms_norm(x_tree, gain_pair[0]))
    projected = low_back(jnp.einsum('td,dkf->tkf', attn_in, w_a, precision=highest))
    queries = low(rotate(projected[:, :, :GROUP * HD].reshape(tree_len, KVH, GROUP, HD), cosines[:, None, None, :], sines[:, None, None, :]))
    key_heads = low(rotate(projected[:, :, GROUP * HD:(GROUP + 1) * HD], cosines[:, None, :], sines[:, None, :]))
    values = low(projected[:, :, (GROUP + 1) * HD:])
    scores = low_back(jnp.einsum('tkgh,skh->kgts', queries, key_heads, precision=highest))
    logits = jnp.where(allowed[None, None], score_mult * scores, masked_value)
    attn_probs = low(jax.nn.softmax(logits, axis=-1))
    mixed_heads = low_back(low(jnp.einsum('kgts,skh->tkgh', attn_probs, values, precision=highest)))
    heads_flat = mixed_heads.reshape(tree_len, N_COL, -1)
    out_blocks = w_b.reshape(N_COL, -1, D)
    attn_sum = low_back(lax.optimization_barrier(jnp.sum(low(jnp.einsum('tcf,cfd->ctd', heads_flat, out_blocks, precision=highest)), axis=0)))
    residual_mid = x_tree + residual_mult * attn_sum
    ffn_in = low(rms_norm(residual_mid, gain_pair[1]))
    gate_up = low_back(jnp.einsum('td,edf->tef', ffn_in, w_c, precision=highest))
    hidden = low(jax.nn.silu(gate_up[:, 0]) * gate_up[:, 1])
    hidden_blocks = hidden.reshape(tree_len, N_COL, -1)
    down_blocks = w_d.reshape(N_COL, -1, D)
    mlp_sum = lax.optimization_barrier(jnp.sum(low(jnp.einsum('tcf,cfd->ctd', hidden_blocks, down_blocks, precision=highest)), axis=0))
    return residual_mid + residual_mult * mlp_sum

def adamw(master, moments, raw_grad, factor, step_rate):
    clipped = factor * raw_grad
    first_moment = beta_one * moments[0] + (1.0 - beta_one) * clipped
    second_moment = beta_two * moments[1] + (1.0 - beta_two) * clipped * clipped
    first_hat = first_moment / (1.0 - beta_one ** STEP)
    second_hat = second_moment / (1.0 - beta_two ** STEP)
    updated = master - step_rate * (first_hat / (jnp.sqrt(second_hat) + adam_eps) + weight_decay * master)
    return (updated, jnp.stack([first_moment, second_moment]))

def reference(tokens, cotangent, segment_of, leaf_parent, w_qkv, mom_qkv, w_out, mom_out, w_gu, mom_gu, w_down, mom_down, gains, mom_gains):
    trees = MICRO * N_ROW
    tree_tokens = tokens.reshape(trees, TREE, D).astype(jnp.float32)
    tree_cot = cotangent.reshape(trees, TREE, D).astype(jnp.float32)
    tree_segs = segment_of.reshape(trees, TREE)
    tree_parents = leaf_parent.reshape(trees, NLEAF)
    masters = (w_qkv, w_out, w_gu, w_down)
    used = tuple((matrix.astype(jnp.bfloat16).astype(jnp.float32) for matrix in masters))

    def one_tree(carry, inputs):
        x_tree, cot_tree, segments, parents = inputs
        allowed, cosines, sines = tree_tables(segments, parents)

        def forward(x_in, w_a, w_b, w_c, w_d, gain_pair):
            return block_forward(x_in, w_a, w_b, w_c, w_d, gain_pair, cosines, sines, allowed)
        output, pullback = jax.vjp(forward, x_tree, used[0], used[1], used[2], used[3], gains)
        grads = pullback(cot_tree)
        carry = tuple((running + addend for running, addend in zip(carry, grads[1:])))
        return (carry, (output.astype(jnp.bfloat16), grads[0]))
    zeros = tuple((jnp.zeros_like(matrix) for matrix in used)) + (jnp.zeros_like(gains),)
    totals, outputs = lax.scan(one_tree, zeros, (tree_tokens, tree_cot, tree_segs, tree_parents))
    mixed = outputs[0].reshape(MICRO, TOKENS_M, D)
    d_tokens = outputs[1].reshape(MICRO, TOKENS_M, D)
    squares = jnp.float32(0.0)
    for grad_piece in totals:
        squares = squares + jnp.sum(grad_piece * grad_piece)
    grad_norm = jnp.sqrt(squares)
    factor = jnp.minimum(1.0, clip_bound() / (grad_norm + 1e-06))
    rates = step_rates()
    states = (mom_qkv, mom_out, mom_gu, mom_down)
    results = []
    for index_w in range(4):
        updated, moments = adamw(masters[index_w], states[index_w], totals[index_w], factor, rates[index_w])
        results.append((updated, moments, updated.astype(jnp.bfloat16)))
    new_gains, moments_gains = adamw(gains, mom_gains, totals[4], factor, rates[4])
    return (mixed, d_tokens, grad_norm, results[0][0], results[0][1], results[0][2], results[1][0], results[1][1], results[1][2], results[2][0], results[2][1], results[2][2], results[3][0], results[3][1], results[3][2], new_gains, moments_gains)
```

```python
import functools
import math

import jax
import jax.numpy as jnp
from jax import lax
from jax.experimental import pallas as pl
from jax.experimental.pallas import tpu as pltpu
from jax.sharding import PartitionSpec as P

D = 2048
FF = 8192
HD = 64
KVH = 8
GROUP = 4
NBRANCH = 4
NLEAF = 8
STEP = 7


norm_eps = 1e-05
residual_mult = 0.22
score_mult = 0.015625
rope_theta = 10000000.0
beta_one = 0.5
beta_two = 0.55
adam_eps = 1e-08
weight_decay = 0.1
masked_value = -1e30


def param_count():
    return D * KVH * (GROUP + 2) * HD + KVH * GROUP * HD * D + 3 * D * FF + 2 * D


def clip_bound():
    return math.sqrt(param_count())


def step_rates():
    return (
        max(D // 12, 1) ** (-0.5),
        max(D // 16, 1) ** (-0.5),
        D ** (-0.5),
        max(FF // 64, 1) ** (-0.5),
        0.3,
    )


def tree_tables(segments, parents):
    seg_count = 1 + NBRANCH + NLEAF
    seg_ids = jnp.arange(seg_count, dtype=jnp.int32)
    member = (segments[:, None] == seg_ids[None, :]).astype(jnp.int32)
    seg_lengths = jnp.sum(member, axis=0)
    seg_starts = jnp.cumsum(seg_lengths) - seg_lengths
    branch_ids = jnp.arange(NBRANCH, dtype=jnp.int32)
    parent_pick = (parents[:, None] == branch_ids[None, :]).astype(jnp.int32)
    parent_len = jnp.sum(parent_pick * seg_lengths[1 : 1 + NBRANCH][None, :], axis=1)
    trunk_len = seg_lengths[0]
    base_depth = jnp.concatenate(
        [
            jnp.zeros((1,), jnp.int32),
            trunk_len * jnp.ones((NBRANCH,), jnp.int32),
            trunk_len + parent_len,
        ]
    )
    places = jnp.arange(segments.shape[0], dtype=jnp.int32)
    depth = places + jnp.sum(member * (base_depth - seg_starts)[None, :], axis=1)
    identity = (seg_ids[:, None] == seg_ids[None, :]).astype(jnp.int32)
    rooted = jnp.broadcast_to((seg_ids[None, :] == 0).astype(jnp.int32), (seg_count, seg_count))
    leaf_links = jnp.concatenate(
        [jnp.zeros((NLEAF, 1), jnp.int32), parent_pick, jnp.zeros((NLEAF, NLEAF), jnp.int32)],
        axis=1,
    )
    leaf_links = jnp.concatenate(
        [jnp.zeros((1 + NBRANCH, seg_count), jnp.int32), leaf_links], axis=0
    )
    ancestry = jnp.minimum(identity + rooted + leaf_links, 1)
    token_path = jnp.dot(member, ancestry)
    allowed = (jnp.dot(token_path, member.T) > 0) & (depth[None, :] <= depth[:, None])
    freqs = jnp.exp(jnp.arange(HD // 2, dtype=jnp.float32) * (-2.0 * math.log(rope_theta) / HD))
    angles = depth.astype(jnp.float32)[:, None] * freqs[None, :]
    return (allowed, jnp.cos(angles), jnp.sin(angles))


def rotate(vectors, cosines, sines):
    half_width = vectors.shape[-1] // 2
    first_half = vectors[..., :half_width]
    second_half = vectors[..., half_width:]
    return jnp.concatenate(
        [first_half * cosines - second_half * sines, second_half * cosines + first_half * sines],
        axis=-1,
    )


def normalize(values, gain):
    scaling = lax.rsqrt(jnp.mean(values * values, axis=-1, keepdims=True) + norm_eps)
    return (values * scaling * gain, scaling)


def norm_back(values, scaling, gain, upstream):
    scaled = upstream * gain
    gain_grad = jnp.sum(upstream * values * scaling, axis=0)
    inner = jnp.mean(scaled * values, axis=-1, keepdims=True)
    return (scaling * scaled - values * scaling * scaling * scaling * inner, gain_grad)


def gather_forward(values):
    return lax.all_gather(values, "col", axis=0, tiled=True)


def gather_backward(values):
    return lax.all_gather(values, "col", axis=0, tiled=True)


def sum_forward(term_fn, row_count):
    return lax.psum_scatter(
        term_fn(jnp.int32(0), lax.axis_size("col") * row_count).astype(jnp.bfloat16),
        "col",
        scatter_dimension=0,
        tiled=True,
    ).astype(jnp.float32)


def sum_backward(term_fn, row_count):
    return lax.psum_scatter(
        term_fn(jnp.int32(0), lax.axis_size("col") * row_count).astype(jnp.bfloat16),
        "col",
        scatter_dimension=0,
        tiled=True,
    ).astype(jnp.float32)


def adamw(master, moments, raw_grad, factor, step_rate):
    clipped = factor * raw_grad
    first_moment = beta_one * moments[0] + (1.0 - beta_one) * clipped
    second_moment = beta_two * moments[1] + (1.0 - beta_two) * clipped * clipped
    first_hat = first_moment / (1.0 - beta_one**STEP)
    second_hat = second_moment / (1.0 - beta_two**STEP)
    updated = master - step_rate * (
        first_hat / (jnp.sqrt(second_hat) + adam_eps) + weight_decay * master
    )
    return (updated, jnp.stack([first_moment, second_moment]))


def local(
    tokens,
    cotangent,
    segment_of,
    leaf_parent,
    w_qkv,
    mom_qkv,
    w_out,
    mom_out,
    w_gu,
    mom_gu,
    w_down,
    mom_down,
    gains,
    mom_gains,
):
    low_shards = (
        w_qkv.astype(jnp.bfloat16),
        w_out.astype(jnp.bfloat16),
        w_gu.astype(jnp.bfloat16),
        w_down.astype(jnp.bfloat16),
    )

    def fetch():
        return (
            lax.all_gather(low_shards[0], "row", axis=0, tiled=True),
            lax.all_gather(low_shards[1], "row", axis=1, tiled=True),
            lax.all_gather(low_shards[2], "row", axis=1, tiled=True),
            lax.all_gather(low_shards[3], "row", axis=1, tiled=True),
        )

    outputs = []
    input_grads = []
    owned = None
    unsummed = None
    gain_partial = None
    for batch_index in range(tokens.shape[0]):
        x_local = tokens[batch_index].astype(jnp.float32)
        row_count = x_local.shape[0]
        allowed, cosines, sines = tree_tables(segment_of[batch_index], leaf_parent[batch_index])
        w_a, w_b, w_c, w_d = fetch()
        normed_a, scale_a = normalize(x_local, gains[0])
        attn_in = gather_forward(normed_a.astype(jnp.bfloat16))
        projected = jnp.einsum("td,dkf->tkf", attn_in, w_a, preferred_element_type=jnp.float32)
        tree_len = projected.shape[0]
        groups = projected.shape[1]
        queries = rotate(
            projected[:, :, : GROUP * HD].reshape(tree_len, groups, GROUP, HD),
            cosines[:, None, None, :],
            sines[:, None, None, :],
        ).astype(jnp.bfloat16)
        key_heads = rotate(
            projected[:, :, GROUP * HD : (GROUP + 1) * HD], cosines[:, None, :], sines[:, None, :]
        ).astype(jnp.bfloat16)
        values = projected[:, :, (GROUP + 1) * HD :].astype(jnp.bfloat16)
        scores = jnp.einsum(
            "tkgh,skh->kgts", queries, key_heads, preferred_element_type=jnp.float32
        )
        logits = jnp.where(allowed, score_mult * scores, masked_value)
        row_peak = jnp.max(logits, axis=-1, keepdims=True)
        exp_terms = jnp.exp(logits - row_peak)
        exp_total = jnp.sum(exp_terms, axis=-1, keepdims=True)
        log_total = row_peak + jnp.log(exp_total)
        attn_probs = exp_terms / exp_total
        mixed_heads = (
            jnp.einsum(
                "kgts,skh->tkgh",
                attn_probs.astype(jnp.bfloat16),
                values,
                preferred_element_type=jnp.float32,
            )
            .astype(jnp.bfloat16)
            .reshape(tree_len, -1)
        )

        def out_terms(first_row, row_total):
            return jnp.dot(mixed_heads, w_b, preferred_element_type=jnp.float32)

        attn_sum = sum_forward(out_terms, row_count)
        residual_mid = x_local + residual_mult * attn_sum
        normed_b, scale_b = normalize(residual_mid, gains[1])
        ffn_in = gather_forward(normed_b.astype(jnp.bfloat16))
        gate_up = jnp.einsum("td,edf->tef", ffn_in, w_c, preferred_element_type=jnp.float32)
        gate_act = jax.nn.sigmoid(gate_up[:, 0])
        silu_gate = gate_up[:, 0] * gate_act
        hidden = (silu_gate * gate_up[:, 1]).astype(jnp.bfloat16)

        def down_terms(first_row, row_total):
            return jnp.dot(hidden, w_d, preferred_element_type=jnp.float32)

        mlp_sum = sum_forward(down_terms, row_count)
        outputs.append((residual_mid + residual_mult * mlp_sum).astype(jnp.bfloat16))
        w_a, w_b, w_c, w_d = fetch()
        cot_full = gather_backward(cotangent[batch_index])
        hidden_grad = residual_mult * jnp.einsum(
            "td,fd->tf", cot_full, w_d, preferred_element_type=jnp.float32
        )
        down_grad = residual_mult * jnp.einsum(
            "tf,td->fd", hidden, cot_full, preferred_element_type=jnp.float32
        )
        gate_grad = (
            hidden_grad * gate_up[:, 1] * gate_act * (1.0 + gate_up[:, 0] * (1.0 - gate_act))
        )
        up_grad = hidden_grad * silu_gate
        gate_up_grad = jnp.stack([gate_grad, up_grad], axis=1).astype(jnp.bfloat16)
        gu_grad = jnp.einsum(
            "td,tef->edf", ffn_in, gate_up_grad, preferred_element_type=jnp.float32
        )

        def ffn_back_terms(first_row, row_total):
            return jnp.einsum("tef,edf->td", gate_up_grad, w_c, preferred_element_type=jnp.float32)

        ffn_in_grad = sum_backward(ffn_back_terms, row_count)
        mid_norm_grad, gain_b_grad = norm_back(residual_mid, scale_b, gains[1], ffn_in_grad)
        mid_grad = cotangent[batch_index].astype(jnp.float32) + mid_norm_grad
        attn_out_grad = gather_backward((residual_mult * mid_grad).astype(jnp.bfloat16))
        out_grad = jnp.einsum(
            "tf,td->fd", mixed_heads, attn_out_grad, preferred_element_type=jnp.float32
        )
        heads_grad = (
            jnp.einsum("td,fd->tf", attn_out_grad, w_b, preferred_element_type=jnp.float32)
            .astype(jnp.bfloat16)
            .reshape(tree_len, groups, GROUP, HD)
        )
        attn_probs = jnp.exp(logits - log_total)
        prob_grad = jnp.einsum(
            "tkgh,skh->kgts", heads_grad, values, preferred_element_type=jnp.float32
        )
        row_inner = jnp.sum(prob_grad * attn_probs, axis=-1, keepdims=True)
        score_grad = (score_mult * attn_probs * (prob_grad - row_inner)).astype(jnp.bfloat16)
        query_grad = jnp.einsum(
            "kgts,skh->tkgh", score_grad, key_heads, preferred_element_type=jnp.float32
        )
        key_grad = jnp.einsum(
            "kgts,tkgh->skh", score_grad, queries, preferred_element_type=jnp.float32
        )
        value_grad = jnp.einsum(
            "kgts,tkgh->skh",
            attn_probs.astype(jnp.bfloat16),
            heads_grad,
            preferred_element_type=jnp.float32,
        )
        query_grad = rotate(query_grad, cosines[:, None, None, :], -sines[:, None, None, :])
        key_grad = rotate(key_grad, cosines[:, None, :], -sines[:, None, :])
        proj_grad = jnp.concatenate(
            [query_grad.reshape(tree_len, groups, GROUP * HD), key_grad, value_grad], axis=-1
        ).astype(jnp.bfloat16)
        qkv_grad = jnp.einsum("td,tkf->dkf", attn_in, proj_grad, preferred_element_type=jnp.float32)

        def attn_back_terms(first_row, row_total):
            return jnp.einsum("tkf,dkf->td", proj_grad, w_a, preferred_element_type=jnp.float32)

        attn_in_grad = sum_backward(attn_back_terms, row_count)
        input_norm_grad, gain_a_grad = norm_back(x_local, scale_a, gains[0], attn_in_grad)
        input_grads.append(mid_grad + input_norm_grad)
        gain_step = jnp.stack([gain_a_grad, gain_b_grad])
        gain_partial = gain_step if gain_partial is None else gain_partial + gain_step
        partials = (qkv_grad, out_grad, gu_grad, down_grad)
        unsummed = (
            partials
            if unsummed is None
            else tuple((running + addend for running, addend in zip(unsummed, partials)))
        )
    owned = (
        lax.psum_scatter(
            unsummed[0].astype(jnp.bfloat16), "row", scatter_dimension=0, tiled=True
        ).astype(jnp.float32),
        lax.psum_scatter(
            unsummed[1].astype(jnp.bfloat16), "row", scatter_dimension=1, tiled=True
        ).astype(jnp.float32),
        lax.psum_scatter(
            unsummed[2].astype(jnp.bfloat16), "row", scatter_dimension=1, tiled=True
        ).astype(jnp.float32),
        lax.psum_scatter(
            unsummed[3].astype(jnp.bfloat16), "row", scatter_dimension=1, tiled=True
        ).astype(jnp.float32),
    )
    local_squares = jnp.float32(0.0)
    for grad_piece in owned:
        local_squares = local_squares + jnp.sum(grad_piece * grad_piece)
    total_squares, gain_total = lax.psum((local_squares, gain_partial), ("row", "col"))
    grad_norm = jnp.sqrt(total_squares + jnp.sum(gain_total * gain_total))
    factor = jnp.minimum(1.0, clip_bound() / (grad_norm + 1e-06))
    rates = step_rates()
    masters = (w_qkv, w_out, w_gu, w_down)
    states = (mom_qkv, mom_out, mom_gu, mom_down)
    results = []
    for index_w in range(4):
        updated, moments = adamw(
            masters[index_w], states[index_w], owned[index_w], factor, rates[index_w]
        )
        results.append((updated, moments, updated.astype(jnp.bfloat16)))
    new_gains, moments_gains = adamw(gains, mom_gains, gain_total, factor, rates[4])
    mixed = jnp.stack(outputs, axis=0)
    d_tokens = jnp.stack(input_grads, axis=0)
    return (
        mixed,
        d_tokens,
        grad_norm,
        results[0][0],
        results[0][1],
        results[0][2],
        results[1][0],
        results[1][1],
        results[1][2],
        results[2][0],
        results[2][1],
        results[2][2],
        results[3][0],
        results[3][1],
        results[3][2],
        new_gains,
        moments_gains,
    )


def position_tables(segments, parents):
    seg_ids = jnp.arange(1 + NBRANCH + NLEAF, dtype=jnp.int32)
    member = (segments[:, None] == seg_ids[None, :]).astype(jnp.int32)
    seg_lengths = jnp.sum(member, axis=0)
    seg_starts = jnp.cumsum(seg_lengths) - seg_lengths
    parent_of = jnp.concatenate([jnp.full((1 + NBRANCH,), -1, jnp.int32), 1 + parents])
    branch_ids = jnp.arange(NBRANCH, dtype=jnp.int32)
    parent_pick = (parents[:, None] == branch_ids[None, :]).astype(jnp.int32)
    parent_len = jnp.sum(parent_pick * seg_lengths[1 : 1 + NBRANCH][None, :], axis=1)
    base_depth = jnp.concatenate(
        [
            jnp.zeros((1,), jnp.int32),
            seg_lengths[0] * jnp.ones((NBRANCH,), jnp.int32),
            seg_lengths[0] + parent_len,
        ]
    )
    places = jnp.arange(segments.shape[0], dtype=jnp.int32)
    depth = places + jnp.sum(member * (base_depth - seg_starts)[None, :], axis=1)
    parent = jnp.sum(member * parent_of[None, :], axis=1)
    freqs = jnp.exp(jnp.arange(HD // 2, dtype=jnp.float32) * (-2.0 * math.log(rope_theta) / HD))
    angles = depth.astype(jnp.float32)[:, None] * freqs[None, :]
    cosines, sines = jnp.cos(angles), jnp.sin(angles)
    return (
        jnp.concatenate([cosines] * 4, axis=1),
        jnp.concatenate([-sines, sines] * 2, axis=1),
        jnp.broadcast_to(segments[:, None].astype(jnp.float32), (segments.shape[0], 128)),
        jnp.broadcast_to(parent[:, None].astype(jnp.float32), (segments.shape[0], 128)),
        jnp.broadcast_to(segments[None, :].astype(jnp.float32), (8, segments.shape[0])),
    )

def dot_nn(a, b):
    return lax.dot_general(a, b, (((1,), (0,)), ((), ())), preferred_element_type=jnp.float32)


def dot_nt(a, b):
    return lax.dot_general(a, b, (((1,), (1,)), ((), ())), preferred_element_type=jnp.float32)


def dot_tn(a, b):
    return lax.dot_general(a, b, (((0,), (0,)), ((), ())), preferred_element_type=jnp.float32)


MICRO = 2
TREE = 1024
OWN = 256
WIDE = 2048
NX, NC, NZ, NY = 2, 2, 4, 2
SEG = 128
MESH = pl.DeviceIdType.MESH
HBM = pl.BlockSpec(memory_space=pl.ANY)


class Place:
    def __init__(self):
        row, col = lax.axis_index("row"), lax.axis_index("col")
        self.row, self.col = row, col
        self.z, self.y = row // NY, row % NY
        self.x, self.c = col // NC, col % NC
        self.own = col
        self.row_z = [lax.rem(row + NY * off, NZ * NY) for off in range(NZ)]
        self.row_y = self.z * NY + (1 - self.y)
        self.row_yz = [lax.rem(self.z + off, NZ) * NY + (1 - self.y) for off in range(NZ)]
        self.col_x = (1 - self.x) * NC + self.c
        self.col_c = self.x * NC + (1 - self.c)
        self.col_xc = (1 - self.x) * NC + (1 - self.c)
        self.at_z = [None] + [(self.row_z[off], col) for off in range(1, NZ)]
        self.at_y = (self.row_y, col)
        self.at_x = (row, self.col_x)
        self.at_c = (row, self.col_c)

    def greet(self):
        barrier = pltpu.get_barrier_semaphore()
        partners = self.at_z[1:] + [self.at_y, self.at_x, self.at_c]
        for partner in partners:
            pl.semaphore_signal(barrier, inc=1, device_id=partner, device_id_type=MESH)
        pl.semaphore_wait(barrier, len(partners))


class Copies:
    def __init__(self):
        self.open_sends = []

    def send(self, src, dst, send_sem, recv_sem, device):
        copy = pltpu.make_async_remote_copy(
            src_ref=src, dst_ref=dst, send_sem=send_sem, recv_sem=recv_sem,
            device_id=device, device_id_type=MESH,
        )
        copy.start()
        self.open_sends.append(copy)
        return copy

    def arrive(self, dst, send_sem, recv_sem, device):
        pltpu.make_async_remote_copy(
            src_ref=dst, dst_ref=dst, send_sem=send_sem, recv_sem=recv_sem,
            device_id=device, device_id_type=MESH,
        ).wait_recv()

    def local(self, src, dst, sem):
        copy = pltpu.make_async_copy(src, dst, sem)
        copy.start()
        return copy

    def close(self):
        for copy in self.open_sends:
            copy.wait_send()
        self.open_sends = []


def rows_of(index, size):
    return pl.ds(pl.multiple_of(index * size, size), size)


class WeightGather:
    def __init__(self, place, copies, own, full, view, send, recv, keep):
        self.place, self.copies, self.own, self.full, self.view = place, copies, own, full, view
        self.send, self.recv, self.keep = send, recv, keep

    def start(self):
        p = self.place
        here = self.view(self.full, p.row)
        self.kept = self.copies.local(self.own, here, self.keep)
        for off in (1, 3, 2):
            self.copies.send(self.own, here, self.send.at[off - 1], self.recv.at[p.row], p.at_z[off])
        self.copies.send(self.own, here, self.send.at[3], self.recv.at[p.row], p.at_y)

    def relay(self):
        p = self.place
        for off in (1, 3, 2):
            block = self.view(self.full, p.row_z[off])
            self.copies.arrive(block, self.send.at[3 + off], self.recv.at[p.row_z[off]], p.at_y)
            self.copies.send(block, block, self.send.at[3 + off], self.recv.at[p.row_z[off]], p.at_y)

    def finish(self):
        p = self.place
        for off in range(NZ):
            block = self.view(self.full, p.row_yz[off])
            self.copies.arrive(block, self.send.at[3], self.recv.at[p.row_yz[off]], p.at_y)
        self.kept.wait()


class TokenGather:
    def __init__(self, place, copies, full, base, send, recv):
        self.place, self.copies, self.full, self.base = place, copies, full, base
        self.send, self.recv = send, recv

    def block(self, index):
        return self.full.at[pl.ds(pl.multiple_of(self.base + index * OWN, OWN), OWN), :]

    def start(self, own, keep):
        p = self.place
        here = self.block(p.own)
        self.kept = self.copies.local(own, here, keep)
        self.copies.send(own, here, self.send.at[0], self.recv.at[p.own], p.at_x)
        self.copies.send(own, here, self.send.at[1], self.recv.at[p.own], p.at_c)

    def relay(self):
        p = self.place
        block = self.block(p.col_x)
        self.copies.arrive(block, self.send.at[2], self.recv.at[p.col_x], p.at_c)
        self.copies.send(block, block, self.send.at[2], self.recv.at[p.col_x], p.at_c)

    def finish(self):
        p = self.place
        for index in (p.col_c, p.col_xc):
            self.copies.arrive(self.block(index), self.send.at[2], self.recv.at[index], p.at_c)
        self.kept.wait()


class TokenSum:
    def __init__(self, place, copies, partial, from_core, from_x, send, recv):
        self.place, self.copies, self.partial = place, copies, partial
        self.from_core, self.from_x, self.send, self.recv = from_core, from_x, send, recv

    def start(self):
        p = self.place
        self.sent = []
        for there in range(NX):
            self.sent.append(
                self.copies.send(
                    self.partial.at[there * NC + (1 - p.c)], self.from_core.at[there],
                    self.send.at[there], self.recv.at[there], p.at_c,
                )
            )

    def middle(self):
        p = self.place
        for there in range(NX):
            self.copies.arrive(self.from_core.at[there], self.send.at[there], self.recv.at[there], p.at_c)
        away = 1 - p.x

        @pl.loop(0, OWN // 32)
        def _(i):
            rows = rows_of(i, 32)
            self.partial[p.col_x, rows, :] = (
                self.partial[p.col_x, rows, :].astype(jnp.float32)
                + self.from_core[away, rows, :].astype(jnp.float32)
            ).astype(jnp.bfloat16)

        self.copies.send(self.partial.at[p.col_x], self.from_x, self.send.at[2], self.recv.at[2], p.at_x)

    def arrive(self):
        p = self.place
        self.copies.arrive(self.from_x, self.send.at[2], self.recv.at[2], p.at_x)

    def rows(self, rows):
        p = self.place
        return (
            self.partial[p.own, rows, :].astype(jnp.float32)
            + self.from_core[p.x, rows, :].astype(jnp.float32)
            + self.from_x[rows, :].astype(jnp.float32)
        )


def swap_halves(tile):
    lane = lax.broadcasted_iota(jnp.int32, tile.shape, 1)
    return jnp.where(lane % HD < HD // 2, pltpu.roll(tile, 128 - HD // 2, 1), pltpu.roll(tile, HD // 2, 1))


def key_value_tiles(kv):
    wide = kv.astype(jnp.float32)
    lane = lax.broadcasted_iota(jnp.int32, wide.shape, 1)
    key_low = jnp.where(lane < HD, wide, 0.0)
    value_high = jnp.where(lane < HD, 0.0, wide)
    key_high = pltpu.roll(key_low, HD, 1)
    value_low = pltpu.roll(value_high, HD, 1)
    low = jnp.bfloat16
    return (key_low.astype(low), key_high.astype(low)), (value_low.astype(low), value_high.astype(low))


def masked_parts(run, seg_col, parent_col, seg_row):
    rows = slice(run * SEG, (run + 1) * SEG)

    def causal():
        shape = (SEG, 2 * SEG)
        return lax.broadcasted_iota(jnp.int32, shape, 1) <= lax.broadcasted_iota(jnp.int32, shape, 0) + run * SEG

    def of_parent():
        return seg_row[0:1, 2 * SEG : 4 * SEG] == parent_col[rows, 0:1]

    def of_run():
        shape = (SEG, SEG)
        order = lax.broadcasted_iota(jnp.int32, shape, 1) <= lax.broadcasted_iota(jnp.int32, shape, 0)
        return order & (seg_row[0:1, rows] == seg_col[rows, 0:1])

    if run < 2:
        return [(slice(0, 2 * SEG), causal())]
    parts = [(slice(0, 2 * SEG), None)]
    if run >= 4:
        parts.append((slice(2 * SEG, 4 * SEG), of_parent()))
    parts.append((rows, of_run()))
    return parts


def score_parts(pairs, keys, parts):
    scores = []
    for span, mask in parts:
        score = dot_nt(pairs, keys[span])
        if mask is not None:
            both = jnp.concatenate([mask, mask], axis=0)
            score = jnp.where(both, score, masked_value)
        scores.append(score)
    return scores


def softmax_parts(scores):
    peak = None
    for score in scores:
        top = jnp.max(score, axis=-1, keepdims=True)
        peak = top if peak is None else jnp.maximum(peak, top)
    exps = [jnp.exp((score - peak) * score_mult) for score in scores]
    total = None
    for term in exps:
        part = jnp.sum(term, axis=-1, keepdims=True)
        total = part if total is None else total + part
    return exps, 1.0 / total


def attend(qkv_ref, seg_col_ref, parent_col_ref, seg_row_ref, heads_ref):
    seg_row = seg_row_ref[...]
    keys, values = key_value_tiles(qkv_ref[:, 2 * SEG : 3 * SEG])
    for run in range(TREE // SEG):
        rows = slice(run * SEG, (run + 1) * SEG)
        pairs = jnp.concatenate([qkv_ref[rows, 0:128], qkv_ref[rows, 128:256]], axis=0)
        parts = masked_parts(run, seg_col_ref, parent_col_ref, seg_row)
        mixed = None
        for half in range(2):
            exps, inverse = softmax_parts(score_parts(pairs, keys[half], parts))
            for (span, _), term in zip(parts, exps):
                got = dot_nn((term * inverse).astype(jnp.bfloat16), values[half][span])
                mixed = got if mixed is None else mixed + got
        low = mixed.astype(jnp.bfloat16)
        heads_ref[rows, 0:128] = low[0:SEG]
        heads_ref[rows, 128:256] = low[SEG:]


def forward_kernel(
    near, tokens, cot, own_qkv, own_out, own_gu, own_down, gain, cosines, sines,
    seg_col, parent_col, seg_row,
    w_qkv, w_out, w_gu, w_down, attn_in, cot_full, ffn_in, qkv, heads, resid, gate, up, hidden, down_grad,
    partial, from_core, from_x, resid_buf, normed_buf, tokens_buf, gain_buf,
    w_send, w_recv, w_keep, t_send, t_recv, t_keep, s_send, s_recv, l_sem,
):
    place = Place()
    copies = Copies()
    place.greet()

    def row_block(full, r):
        return full.at[rows_of(r, OWN), :]

    def col_block(full, r):
        return full.at[:, rows_of(r, OWN)]

    def weight(index, own, full, view):
        return WeightGather(
            place, copies, own, full, view, w_send.at[index], w_recv.at[index], w_keep.at[index]
        )

    g_qkv = weight(0, own_qkv, w_qkv, row_block)
    g_out = weight(1, own_out, w_out, col_block)
    g_gate = weight(2, own_gu.at[0], w_gu.at[0], row_block)
    g_up = weight(3, own_gu.at[1], w_gu.at[1], row_block)
    g_down = weight(4, own_down, w_down, col_block)

    def token_gather(index, full, m):
        return TokenGather(place, copies, full, m * TREE, t_send.at[index], t_recv.at[index])

    a_in = [token_gather(m, attn_in, m) for m in range(MICRO)]
    a_cot = [token_gather(2 + m, cot_full, m) for m in range(MICRO)]
    a_ffn = [token_gather(4 + m, ffn_in, m) for m in range(MICRO)]
    sums = [
        TokenSum(place, copies, partial.at[m], from_core.at[m], from_x.at[m], s_send.at[m], s_recv.at[m])
        for m in range(MICRO)
    ]

    def project(m):
        def body(a_ref, w_ref, cos_ref, sin_ref, out_ref):
            got = dot_nn(a_ref[...], w_ref[...])
            cos, sin = cos_ref[...], sin_ref[...]
            lane = lax.broadcasted_iota(jnp.int32, cos.shape, 1)
            cos_key = jnp.where(lane < HD, cos, 1.0)
            sin_key = jnp.where(lane < HD, sin, 0.0)
            for tile in range(got.shape[1] // 128):
                part = got[:, tile * 128 : (tile + 1) * 128]
                is_key = tile % 3 == 2
                turned = part * (cos_key if is_key else cos) + swap_halves(part) * (sin_key if is_key else sin)
                out_ref[:, tile * 128 : (tile + 1) * 128] = turned.astype(jnp.bfloat16)

        steps = TREE // OWN
        rows = pl.BlockSpec((OWN, D), lambda i: (m * steps + i, 0))
        table = pl.BlockSpec((OWN, 128), lambda i: (m * steps + i, 0))
        out = pl.BlockSpec((OWN, 768), lambda i: (m * steps + i, 0))
        whole = pl.BlockSpec((D, 768), lambda i: (0, 0))
        pltpu.emit_pipeline(body, grid=(steps,), in_specs=[rows, whole, table, table], out_specs=[out])(
            attn_in, w_qkv, cosines, sines, qkv
        )

    def attention(m):
        tree = pl.BlockSpec((TREE, 128), lambda g: (m, 0))
        pltpu.emit_pipeline(
            attend,
            grid=(2,),
            in_specs=[
                pl.BlockSpec((TREE, 384), lambda g: (m, g)),
                tree,
                tree,
                pl.BlockSpec((8, TREE), lambda g: (m, 0)),
            ],
            out_specs=[pl.BlockSpec((TREE, 256), lambda g: (m, g))],
        )(qkv, seg_col, parent_col, seg_row, heads)

    def out_project(m):
        def body_at(step, a_ref, w_ref):
            partial[m, step.index[0]] = dot_nn(a_ref[...], w_ref[...]).astype(jnp.bfloat16)

        steps = TREE // OWN
        pltpu.emit_pipeline(
            body_at,
            grid=(steps,),
            in_specs=[
                pl.BlockSpec((OWN, 512), lambda i: (m * steps + i, 0)),
                pl.BlockSpec((512, D), lambda i: (0, 0)),
            ],
            out_specs=[],
            _explicit_indices=True,
        )(heads, w_out)

    def middle_norm(m):
        sums[m].arrive()
        load = copies.local(tokens.at[m], tokens_buf, l_sem.at[0])
        load_gain = copies.local(gain, gain_buf, l_sem.at[1])
        load.wait()
        load_gain.wait()

        @pl.loop(0, OWN // 32)
        def _(i):
            rows = rows_of(i, 32)
            value = tokens_buf[rows, :].astype(jnp.float32) + residual_mult * sums[m].rows(rows)
            resid_buf[m, rows, :] = value
            scale = lax.rsqrt(jnp.mean(value * value, axis=-1, keepdims=True) + norm_eps)
            normed_buf[m, rows, :] = (value * scale * gain_buf[1:2, :]).astype(jnp.bfloat16)

        a_ffn[m].start(normed_buf.at[m], t_keep.at[4 + m])
        return copies.local(resid_buf.at[m], resid.at[m], l_sem.at[2 + m])

    def gate_up(m):
        def body(a_ref, g_ref, u_ref, gate_ref, up_ref, hidden_ref):
            for part in range(TREE // OWN):
                rows = slice(part * OWN, (part + 1) * OWN)
                value = a_ref[rows, :]
                g = dot_nn(value, g_ref[0])
                u = dot_nn(value, u_ref[0])
                gate_ref[rows, :] = g.astype(jnp.bfloat16)
                up_ref[rows, :] = u.astype(jnp.bfloat16)
                hidden_ref[rows, :] = (g * jax.nn.sigmoid(g) * u).astype(jnp.bfloat16)

        cols = pl.BlockSpec((TREE, 256), lambda j: (m, j))
        pltpu.emit_pipeline(
            body,
            grid=(WIDE // 256,),
            in_specs=[
                pl.BlockSpec((TREE, D), lambda j: (m, 0)),
                pl.BlockSpec((1, D, 256), lambda j: (0, 0, j)),
                pl.BlockSpec((1, D, 256), lambda j: (1, 0, j)),
            ],
            out_specs=[cols, cols, cols],
        )(ffn_in, w_gu, w_gu, gate, up, hidden)

    def grad_down():
        def body(h_ref, c_ref, out_ref):
            out_ref[...] = (residual_mult * dot_tn(h_ref[...], c_ref[...])).astype(jnp.bfloat16)

        pltpu.emit_pipeline(
            body,
            grid=(WIDE // 256,),
            in_specs=[
                pl.BlockSpec((MICRO * TREE, 256), lambda i: (0, i)),
                pl.BlockSpec((MICRO * TREE, D), lambda i: (0, 0)),
            ],
            out_specs=[pl.BlockSpec((256, D), lambda i: (i, 0))],
        )(hidden, cot_full, down_grad)

    g_qkv.start()
    for m in range(MICRO):
        a_in[m].start(near.at[m], t_keep.at[m])
    g_out.start()
    g_gate.start()
    for m in range(MICRO):
        a_cot[m].start(cot.at[m], t_keep.at[2 + m])
    a_in[0].relay()
    a_in[1].relay()
    g_qkv.relay()
    g_out.relay()
    g_up.start()
    a_in[0].finish()
    g_qkv.finish()
    project(0)
    a_in[1].finish()
    project(1)
    a_cot[0].relay()
    a_cot[1].relay()
    attention(0)
    g_out.finish()
    out_project(0)
    sums[0].start()
    attention(1)
    sums[0].middle()
    out_project(1)
    sums[1].start()
    g_gate.relay()
    g_down.start()
    stored = [middle_norm(0)]
    sums[1].middle()
    a_ffn[0].relay()
    stored.append(middle_norm(1))
    a_ffn[1].relay()
    g_up.relay()
    a_cot[0].finish()
    a_cot[1].finish()
    a_ffn[0].finish()
    g_gate.finish()
    g_up.finish()
    gate_up(0)
    a_ffn[1].finish()
    gate_up(1)
    g_down.relay()
    grad_down()
    g_down.finish()
    for copy in stored:
        copy.wait()
    copies.close()


def forward(near, tokens, cot, low_qkv, low_out, low_gu, low_down, gains, cosines, sines, seg_col, parent_col, seg_row):
    low = jnp.bfloat16
    shape = jax.ShapeDtypeStruct
    all_tokens = MICRO * TREE
    outs = [
        shape((D, 768), low), shape((512, D), low), shape((2, D, WIDE), low), shape((WIDE, D), low),
        shape((all_tokens, D), low), shape((all_tokens, D), low), shape((all_tokens, D), low),
        shape((all_tokens, 768), low), shape((all_tokens, 512), low), shape((MICRO, OWN, D), jnp.float32),
        shape((all_tokens, WIDE), low), shape((all_tokens, WIDE), low), shape((all_tokens, WIDE), low),
        shape((WIDE, D), low),
    ]
    dma = pltpu.SemaphoreType.DMA
    return pl.pallas_call(
        forward_kernel,
        out_shape=outs,
        in_specs=[HBM] * 13,
        out_specs=[HBM] * len(outs),
        scratch_shapes=[
            pltpu.VMEM((MICRO, NX * NC, OWN, D), low),
            pltpu.VMEM((MICRO, NX, OWN, D), low),
            pltpu.VMEM((MICRO, OWN, D), low),
            pltpu.VMEM((MICRO, OWN, D), jnp.float32),
            pltpu.VMEM((MICRO, OWN, D), low),
            pltpu.VMEM((OWN, D), low),
            pltpu.VMEM((2, D), jnp.float32),
            dma((5, 7)), dma((5, NZ * NY)), dma((5,)),
            dma((6, 3)), dma((6, NX * NC)), dma((6,)),
            dma((MICRO, 3)), dma((MICRO, 3)), dma((4,)),
        ],
        compiler_params=pltpu.CompilerParams(
            collective_id=0, has_side_effects=True, vmem_limit_bytes=60 * 1024 * 1024
        ),
        cost_estimate=pl.CostEstimate(flops=90 * 10**9, bytes_accessed=2 * 10**8, transcendentals=10**7),
        name="forward",
    )(near, tokens, cot, low_qkv, low_out, low_gu, low_down, gains, cosines, sines, seg_col, parent_col, seg_row)


def fast_local(
    tokens,
    cotangent,
    segment_of,
    leaf_parent,
    w_qkv,
    mom_qkv,
    w_out,
    mom_out,
    w_gu,
    mom_gu,
    w_down,
    mom_down,
    gains,
    mom_gains,
):
    low = jnp.bfloat16
    tables = [position_tables(segment_of[m], leaf_parent[m]) for m in range(MICRO)]
    cos_all, sin_all, seg_col, parent_col, seg_row = (
        jnp.concatenate([table[i] for table in tables], axis=0) for i in range(5)
    )
    wide = tokens.astype(jnp.float32)
    near, scales = normalize(wide, gains[0])
    (w_a, w_b, w_c, w_d, attn_all, cot_all, ffn_all, qkv_all, heads_all, resid_all, gate_all, up_all, hidden_all, down_all) = forward(
        near.astype(low), tokens, cotangent,
        w_qkv.astype(low).reshape(OWN, 768), w_out.astype(low), w_gu.astype(low), w_down.astype(low),
        gains, cos_all, sin_all, seg_col, parent_col, seg_row,
    )
    w_a = w_a.reshape(D, 2, 384)
    groups = 2
    tree_len = TREE
    row_count = OWN
    outputs = []
    input_grads = []
    unsummed = None
    gain_partial = None
    for batch_index in range(MICRO):
        span = slice(batch_index * TREE, (batch_index + 1) * TREE)
        allowed, cosines, sines = tree_tables(segment_of[batch_index], leaf_parent[batch_index])
        x_local = wide[batch_index]
        scale_a = scales[batch_index]
        attn_in, cot_full, ffn_in, hidden, mixed_heads = attn_all[span], cot_all[span], ffn_all[span], hidden_all[span], heads_all[span]
        gate_up = jnp.stack([gate_all[span], up_all[span]], axis=1).astype(jnp.float32)
        gate_act = jax.nn.sigmoid(gate_up[:, 0])
        silu_gate = gate_up[:, 0] * gate_act
        residual_mid = resid_all[batch_index]
        normed_b, scale_b = normalize(residual_mid, gains[1])
        packed = qkv_all[span].reshape(tree_len, groups, 384)
        queries = packed[:, :, :256].reshape(tree_len, groups, GROUP, HD)
        key_heads, values = packed[:, :, 256:320], packed[:, :, 320:]
        scores = jnp.einsum("tkgh,skh->kgts", queries, key_heads, preferred_element_type=jnp.float32)
        logits = jnp.where(allowed, score_mult * scores, masked_value)
        row_peak = jnp.max(logits, axis=-1, keepdims=True)
        log_total = row_peak + jnp.log(jnp.sum(jnp.exp(logits - row_peak), axis=-1, keepdims=True))

        def down_terms(first_row, row_total):
            return jnp.dot(hidden, w_d, preferred_element_type=jnp.float32)

        mlp_sum = sum_forward(down_terms, row_count)
        outputs.append((residual_mid + residual_mult * mlp_sum).astype(jnp.bfloat16))
        hidden_grad = residual_mult * jnp.einsum(
            "td,fd->tf", cot_full, w_d, preferred_element_type=jnp.float32
        )
        gate_grad = (
            hidden_grad * gate_up[:, 1] * gate_act * (1.0 + gate_up[:, 0] * (1.0 - gate_act))
        )
        up_grad = hidden_grad * silu_gate
        gate_up_grad = jnp.stack([gate_grad, up_grad], axis=1).astype(jnp.bfloat16)
        gu_grad = jnp.einsum(
            "td,tef->edf", ffn_in, gate_up_grad, preferred_element_type=jnp.float32
        )

        def ffn_back_terms(first_row, row_total):
            return jnp.einsum("tef,edf->td", gate_up_grad, w_c, preferred_element_type=jnp.float32)

        ffn_in_grad = sum_backward(ffn_back_terms, row_count)
        mid_norm_grad, gain_b_grad = norm_back(residual_mid, scale_b, gains[1], ffn_in_grad)
        mid_grad = cotangent[batch_index].astype(jnp.float32) + mid_norm_grad
        attn_out_grad = gather_backward((residual_mult * mid_grad).astype(jnp.bfloat16))
        out_grad = jnp.einsum(
            "tf,td->fd", mixed_heads, attn_out_grad, preferred_element_type=jnp.float32
        )
        heads_grad = (
            jnp.einsum("td,fd->tf", attn_out_grad, w_b, preferred_element_type=jnp.float32)
            .astype(jnp.bfloat16)
            .reshape(tree_len, groups, GROUP, HD)
        )
        attn_probs = jnp.exp(logits - log_total)
        prob_grad = jnp.einsum(
            "tkgh,skh->kgts", heads_grad, values, preferred_element_type=jnp.float32
        )
        row_inner = jnp.sum(prob_grad * attn_probs, axis=-1, keepdims=True)
        score_grad = (score_mult * attn_probs * (prob_grad - row_inner)).astype(jnp.bfloat16)
        query_grad = jnp.einsum(
            "kgts,skh->tkgh", score_grad, key_heads, preferred_element_type=jnp.float32
        )
        key_grad = jnp.einsum(
            "kgts,tkgh->skh", score_grad, queries, preferred_element_type=jnp.float32
        )
        value_grad = jnp.einsum(
            "kgts,tkgh->skh",
            attn_probs.astype(jnp.bfloat16),
            heads_grad,
            preferred_element_type=jnp.float32,
        )
        query_grad = rotate(query_grad, cosines[:, None, None, :], -sines[:, None, None, :])
        key_grad = rotate(key_grad, cosines[:, None, :], -sines[:, None, :])
        proj_grad = jnp.concatenate(
            [query_grad.reshape(tree_len, groups, GROUP * HD), key_grad, value_grad], axis=-1
        ).astype(jnp.bfloat16)
        qkv_grad = jnp.einsum("td,tkf->dkf", attn_in, proj_grad, preferred_element_type=jnp.float32)

        def attn_back_terms(first_row, row_total):
            return jnp.einsum("tkf,dkf->td", proj_grad, w_a, preferred_element_type=jnp.float32)

        attn_in_grad = sum_backward(attn_back_terms, row_count)
        input_norm_grad, gain_a_grad = norm_back(x_local, scale_a, gains[0], attn_in_grad)
        input_grads.append(mid_grad + input_norm_grad)
        gain_step = jnp.stack([gain_a_grad, gain_b_grad])
        gain_partial = gain_step if gain_partial is None else gain_partial + gain_step
        partials = (qkv_grad, out_grad, gu_grad)
        unsummed = (
            partials
            if unsummed is None
            else tuple((running + addend for running, addend in zip(unsummed, partials)))
        )
    owned = (
        lax.psum_scatter(
            unsummed[0].astype(jnp.bfloat16), "row", scatter_dimension=0, tiled=True
        ).astype(jnp.float32),
        lax.psum_scatter(
            unsummed[1].astype(jnp.bfloat16), "row", scatter_dimension=1, tiled=True
        ).astype(jnp.float32),
        lax.psum_scatter(
            unsummed[2].astype(jnp.bfloat16), "row", scatter_dimension=1, tiled=True
        ).astype(jnp.float32),
        lax.psum_scatter(
            down_all, "row", scatter_dimension=1, tiled=True
        ).astype(jnp.float32),
    )
    local_squares = jnp.float32(0.0)
    for grad_piece in owned:
        local_squares = local_squares + jnp.sum(grad_piece * grad_piece)
    total_squares, gain_total = lax.psum((local_squares, gain_partial), ("row", "col"))
    grad_norm = jnp.sqrt(total_squares + jnp.sum(gain_total * gain_total))
    factor = jnp.minimum(1.0, clip_bound() / (grad_norm + 1e-06))
    rates = step_rates()
    masters = (w_qkv, w_out, w_gu, w_down)
    states = (mom_qkv, mom_out, mom_gu, mom_down)
    results = []
    for index_w in range(4):
        updated, moments = adamw(
            masters[index_w], states[index_w], owned[index_w], factor, rates[index_w]
        )
        results.append((updated, moments, updated.astype(jnp.bfloat16)))
    new_gains, moments_gains = adamw(gains, mom_gains, gain_total, factor, rates[4])
    mixed = jnp.stack(outputs, axis=0)
    d_tokens = jnp.stack(input_grads, axis=0)
    return (
        mixed,
        d_tokens,
        grad_norm,
        results[0][0],
        results[0][1],
        results[0][2],
        results[1][0],
        results[1][1],
        results[1][2],
        results[2][0],
        results[2][1],
        results[2][2],
        results[3][0],
        results[3][1],
        results[3][2],
        new_gains,
        moments_gains,
    )


def solution(mesh):
    placed = (
        P(None, ("row", "col"), None),
        P(None, ("row", "col"), None),
        P(None, "row"),
        P(None, "row"),
        P("row", "col", None),
        P(None, "row", "col", None),
        P("col", "row"),
        P(None, "col", "row"),
        P(None, "row", "col"),
        P(None, None, "row", "col"),
        P("col", "row"),
        P(None, "col", "row"),
        P(),
        P(),
    )
    sizes = dict(mesh.shape)
    fits = sizes == {"row": NZ * NY, "col": NX * NC}
    return jax.shard_map(
        fast_local if fits else local,
        mesh=mesh,
        in_specs=placed,
        out_specs=(
            P(None, ("row", "col"), None),
            P(None, ("row", "col"), None),
            P(),
            P("row", "col", None),
            P(None, "row", "col", None),
            P("row", "col", None),
            P("col", "row"),
            P(None, "col", "row"),
            P("col", "row"),
            P(None, "row", "col"),
            P(None, None, "row", "col"),
            P(None, "row", "col"),
            P("col", "row"),
            P(None, "col", "row"),
            P("col", "row"),
            P(),
            P(),
        ),
        check_vma=False,
    )
```

```python
import functools
import math

import jax
import jax.numpy as jnp
from jax import lax
from jax.experimental import pallas as pl
from jax.experimental.pallas import tpu as pltpu
from jax.sharding import PartitionSpec as P

D = 2048
FF = 8192
HD = 64
KVH = 8
GROUP = 4
NBRANCH = 4
NLEAF = 8
STEP = 7


norm_eps = 1e-05
residual_mult = 0.22
score_mult = 0.015625
rope_theta = 10000000.0
beta_one = 0.5
beta_two = 0.55
adam_eps = 1e-08
weight_decay = 0.1
masked_value = -1e30


def param_count():
    return D * KVH * (GROUP + 2) * HD + KVH * GROUP * HD * D + 3 * D * FF + 2 * D


def clip_bound():
    return math.sqrt(param_count())


def step_rates():
    return (
        max(D // 12, 1) ** (-0.5),
        max(D // 16, 1) ** (-0.5),
        D ** (-0.5),
        max(FF // 64, 1) ** (-0.5),
        0.3,
    )


def tree_tables(segments, parents):
    seg_count = 1 + NBRANCH + NLEAF
    seg_ids = jnp.arange(seg_count, dtype=jnp.int32)
    member = (segments[:, None] == seg_ids[None, :]).astype(jnp.int32)
    seg_lengths = jnp.sum(member, axis=0)
    seg_starts = jnp.cumsum(seg_lengths) - seg_lengths
    branch_ids = jnp.arange(NBRANCH, dtype=jnp.int32)
    parent_pick = (parents[:, None] == branch_ids[None, :]).astype(jnp.int32)
    parent_len = jnp.sum(parent_pick * seg_lengths[1 : 1 + NBRANCH][None, :], axis=1)
    trunk_len = seg_lengths[0]
    base_depth = jnp.concatenate(
        [
            jnp.zeros((1,), jnp.int32),
            trunk_len * jnp.ones((NBRANCH,), jnp.int32),
            trunk_len + parent_len,
        ]
    )
    places = jnp.arange(segments.shape[0], dtype=jnp.int32)
    depth = places + jnp.sum(member * (base_depth - seg_starts)[None, :], axis=1)
    identity = (seg_ids[:, None] == seg_ids[None, :]).astype(jnp.int32)
    rooted = jnp.broadcast_to((seg_ids[None, :] == 0).astype(jnp.int32), (seg_count, seg_count))
    leaf_links = jnp.concatenate(
        [jnp.zeros((NLEAF, 1), jnp.int32), parent_pick, jnp.zeros((NLEAF, NLEAF), jnp.int32)],
        axis=1,
    )
    leaf_links = jnp.concatenate(
        [jnp.zeros((1 + NBRANCH, seg_count), jnp.int32), leaf_links], axis=0
    )
    ancestry = jnp.minimum(identity + rooted + leaf_links, 1)
    token_path = jnp.dot(member, ancestry)
    allowed = (jnp.dot(token_path, member.T) > 0) & (depth[None, :] <= depth[:, None])
    freqs = jnp.exp(jnp.arange(HD // 2, dtype=jnp.float32) * (-2.0 * math.log(rope_theta) / HD))
    angles = depth.astype(jnp.float32)[:, None] * freqs[None, :]
    return (allowed, jnp.cos(angles), jnp.sin(angles))


def rotate(vectors, cosines, sines):
    half_width = vectors.shape[-1] // 2
    first_half = vectors[..., :half_width]
    second_half = vectors[..., half_width:]
    return jnp.concatenate(
        [first_half * cosines - second_half * sines, second_half * cosines + first_half * sines],
        axis=-1,
    )


def normalize(values, gain):
    scaling = lax.rsqrt(jnp.mean(values * values, axis=-1, keepdims=True) + norm_eps)
    return (values * scaling * gain, scaling)


def norm_back(values, scaling, gain, upstream):
    scaled = upstream * gain
    gain_grad = jnp.sum(upstream * values * scaling, axis=0)
    inner = jnp.mean(scaled * values, axis=-1, keepdims=True)
    return (scaling * scaled - values * scaling * scaling * scaling * inner, gain_grad)


def gather_forward(values):
    return lax.all_gather(values, "col", axis=0, tiled=True)


def gather_backward(values):
    return lax.all_gather(values, "col", axis=0, tiled=True)


def sum_forward(term_fn, row_count):
    return lax.psum_scatter(
        term_fn(jnp.int32(0), lax.axis_size("col") * row_count).astype(jnp.bfloat16),
        "col",
        scatter_dimension=0,
        tiled=True,
    ).astype(jnp.float32)


def sum_backward(term_fn, row_count):
    return lax.psum_scatter(
        term_fn(jnp.int32(0), lax.axis_size("col") * row_count).astype(jnp.bfloat16),
        "col",
        scatter_dimension=0,
        tiled=True,
    ).astype(jnp.float32)


def adamw(master, moments, raw_grad, factor, step_rate):
    clipped = factor * raw_grad
    first_moment = beta_one * moments[0] + (1.0 - beta_one) * clipped
    second_moment = beta_two * moments[1] + (1.0 - beta_two) * clipped * clipped
    first_hat = first_moment / (1.0 - beta_one**STEP)
    second_hat = second_moment / (1.0 - beta_two**STEP)
    updated = master - step_rate * (
        first_hat / (jnp.sqrt(second_hat) + adam_eps) + weight_decay * master
    )
    return (updated, jnp.stack([first_moment, second_moment]))


def local(
    tokens,
    cotangent,
    segment_of,
    leaf_parent,
    w_qkv,
    mom_qkv,
    w_out,
    mom_out,
    w_gu,
    mom_gu,
    w_down,
    mom_down,
    gains,
    mom_gains,
):
    low_shards = (
        w_qkv.astype(jnp.bfloat16),
        w_out.astype(jnp.bfloat16),
        w_gu.astype(jnp.bfloat16),
        w_down.astype(jnp.bfloat16),
    )

    def fetch():
        return (
            lax.all_gather(low_shards[0], "row", axis=0, tiled=True),
            lax.all_gather(low_shards[1], "row", axis=1, tiled=True),
            lax.all_gather(low_shards[2], "row", axis=1, tiled=True),
            lax.all_gather(low_shards[3], "row", axis=1, tiled=True),
        )

    outputs = []
    input_grads = []
    owned = None
    unsummed = None
    gain_partial = None
    for batch_index in range(tokens.shape[0]):
        x_local = tokens[batch_index].astype(jnp.float32)
        row_count = x_local.shape[0]
        allowed, cosines, sines = tree_tables(segment_of[batch_index], leaf_parent[batch_index])
        w_a, w_b, w_c, w_d = fetch()
        normed_a, scale_a = normalize(x_local, gains[0])
        attn_in = gather_forward(normed_a.astype(jnp.bfloat16))
        projected = jnp.einsum("td,dkf->tkf", attn_in, w_a, preferred_element_type=jnp.float32)
        tree_len = projected.shape[0]
        groups = projected.shape[1]
        queries = rotate(
            projected[:, :, : GROUP * HD].reshape(tree_len, groups, GROUP, HD),
            cosines[:, None, None, :],
            sines[:, None, None, :],
        ).astype(jnp.bfloat16)
        key_heads = rotate(
            projected[:, :, GROUP * HD : (GROUP + 1) * HD], cosines[:, None, :], sines[:, None, :]
        ).astype(jnp.bfloat16)
        values = projected[:, :, (GROUP + 1) * HD :].astype(jnp.bfloat16)
        scores = jnp.einsum(
            "tkgh,skh->kgts", queries, key_heads, preferred_element_type=jnp.float32
        )
        logits = jnp.where(allowed, score_mult * scores, masked_value)
        row_peak = jnp.max(logits, axis=-1, keepdims=True)
        exp_terms = jnp.exp(logits - row_peak)
        exp_total = jnp.sum(exp_terms, axis=-1, keepdims=True)
        log_total = row_peak + jnp.log(exp_total)
        attn_probs = exp_terms / exp_total
        mixed_heads = (
            jnp.einsum(
                "kgts,skh->tkgh",
                attn_probs.astype(jnp.bfloat16),
                values,
                preferred_element_type=jnp.float32,
            )
            .astype(jnp.bfloat16)
            .reshape(tree_len, -1)
        )

        def out_terms(first_row, row_total):
            return jnp.dot(mixed_heads, w_b, preferred_element_type=jnp.float32)

        attn_sum = sum_forward(out_terms, row_count)
        residual_mid = x_local + residual_mult * attn_sum
        normed_b, scale_b = normalize(residual_mid, gains[1])
        ffn_in = gather_forward(normed_b.astype(jnp.bfloat16))
        gate_up = jnp.einsum("td,edf->tef", ffn_in, w_c, preferred_element_type=jnp.float32)
        gate_act = jax.nn.sigmoid(gate_up[:, 0])
        silu_gate = gate_up[:, 0] * gate_act
        hidden = (silu_gate * gate_up[:, 1]).astype(jnp.bfloat16)

        def down_terms(first_row, row_total):
            return jnp.dot(hidden, w_d, preferred_element_type=jnp.float32)

        mlp_sum = sum_forward(down_terms, row_count)
        outputs.append((residual_mid + residual_mult * mlp_sum).astype(jnp.bfloat16))
        w_a, w_b, w_c, w_d = fetch()
        cot_full = gather_backward(cotangent[batch_index])
        hidden_grad = residual_mult * jnp.einsum(
            "td,fd->tf", cot_full, w_d, preferred_element_type=jnp.float32
        )
        down_grad = residual_mult * jnp.einsum(
            "tf,td->fd", hidden, cot_full, preferred_element_type=jnp.float32
        )
        gate_grad = (
            hidden_grad * gate_up[:, 1] * gate_act * (1.0 + gate_up[:, 0] * (1.0 - gate_act))
        )
        up_grad = hidden_grad * silu_gate
        gate_up_grad = jnp.stack([gate_grad, up_grad], axis=1).astype(jnp.bfloat16)
        gu_grad = jnp.einsum(
            "td,tef->edf", ffn_in, gate_up_grad, preferred_element_type=jnp.float32
        )

        def ffn_back_terms(first_row, row_total):
            return jnp.einsum("tef,edf->td", gate_up_grad, w_c, preferred_element_type=jnp.float32)

        ffn_in_grad = sum_backward(ffn_back_terms, row_count)
        mid_norm_grad, gain_b_grad = norm_back(residual_mid, scale_b, gains[1], ffn_in_grad)
        mid_grad = cotangent[batch_index].astype(jnp.float32) + mid_norm_grad
        attn_out_grad = gather_backward((residual_mult * mid_grad).astype(jnp.bfloat16))
        out_grad = jnp.einsum(
            "tf,td->fd", mixed_heads, attn_out_grad, preferred_element_type=jnp.float32
        )
        heads_grad = (
            jnp.einsum("td,fd->tf", attn_out_grad, w_b, preferred_element_type=jnp.float32)
            .astype(jnp.bfloat16)
            .reshape(tree_len, groups, GROUP, HD)
        )
        attn_probs = jnp.exp(logits - log_total)
        prob_grad = jnp.einsum(
            "tkgh,skh->kgts", heads_grad, values, preferred_element_type=jnp.float32
        )
        row_inner = jnp.sum(prob_grad * attn_probs, axis=-1, keepdims=True)
        score_grad = (score_mult * attn_probs * (prob_grad - row_inner)).astype(jnp.bfloat16)
        query_grad = jnp.einsum(
            "kgts,skh->tkgh", score_grad, key_heads, preferred_element_type=jnp.float32
        )
        key_grad = jnp.einsum(
            "kgts,tkgh->skh", score_grad, queries, preferred_element_type=jnp.float32
        )
        value_grad = jnp.einsum(
            "kgts,tkgh->skh",
            attn_probs.astype(jnp.bfloat16),
            heads_grad,
            preferred_element_type=jnp.float32,
        )
        query_grad = rotate(query_grad, cosines[:, None, None, :], -sines[:, None, None, :])
        key_grad = rotate(key_grad, cosines[:, None, :], -sines[:, None, :])
        proj_grad = jnp.concatenate(
            [query_grad.reshape(tree_len, groups, GROUP * HD), key_grad, value_grad], axis=-1
        ).astype(jnp.bfloat16)
        qkv_grad = jnp.einsum("td,tkf->dkf", attn_in, proj_grad, preferred_element_type=jnp.float32)

        def attn_back_terms(first_row, row_total):
            return jnp.einsum("tkf,dkf->td", proj_grad, w_a, preferred_element_type=jnp.float32)

        attn_in_grad = sum_backward(attn_back_terms, row_count)
        input_norm_grad, gain_a_grad = norm_back(x_local, scale_a, gains[0], attn_in_grad)
        input_grads.append(mid_grad + input_norm_grad)
        gain_step = jnp.stack([gain_a_grad, gain_b_grad])
        gain_partial = gain_step if gain_partial is None else gain_partial + gain_step
        partials = (qkv_grad, out_grad, gu_grad, down_grad)
        unsummed = (
            partials
            if unsummed is None
            else tuple((running + addend for running, addend in zip(unsummed, partials)))
        )
    owned = (
        lax.psum_scatter(
            unsummed[0].astype(jnp.bfloat16), "row", scatter_dimension=0, tiled=True
        ).astype(jnp.float32),
        lax.psum_scatter(
            unsummed[1].astype(jnp.bfloat16), "row", scatter_dimension=1, tiled=True
        ).astype(jnp.float32),
        lax.psum_scatter(
            unsummed[2].astype(jnp.bfloat16), "row", scatter_dimension=1, tiled=True
        ).astype(jnp.float32),
        lax.psum_scatter(
            unsummed[3].astype(jnp.bfloat16), "row", scatter_dimension=1, tiled=True
        ).astype(jnp.float32),
    )
    local_squares = jnp.float32(0.0)
    for grad_piece in owned:
        local_squares = local_squares + jnp.sum(grad_piece * grad_piece)
    total_squares, gain_total = lax.psum((local_squares, gain_partial), ("row", "col"))
    grad_norm = jnp.sqrt(total_squares + jnp.sum(gain_total * gain_total))
    factor = jnp.minimum(1.0, clip_bound() / (grad_norm + 1e-06))
    rates = step_rates()
    masters = (w_qkv, w_out, w_gu, w_down)
    states = (mom_qkv, mom_out, mom_gu, mom_down)
    results = []
    for index_w in range(4):
        updated, moments = adamw(
            masters[index_w], states[index_w], owned[index_w], factor, rates[index_w]
        )
        results.append((updated, moments, updated.astype(jnp.bfloat16)))
    new_gains, moments_gains = adamw(gains, mom_gains, gain_total, factor, rates[4])
    mixed = jnp.stack(outputs, axis=0)
    d_tokens = jnp.stack(input_grads, axis=0)
    return (
        mixed,
        d_tokens,
        grad_norm,
        results[0][0],
        results[0][1],
        results[0][2],
        results[1][0],
        results[1][1],
        results[1][2],
        results[2][0],
        results[2][1],
        results[2][2],
        results[3][0],
        results[3][1],
        results[3][2],
        new_gains,
        moments_gains,
    )


def position_tables(segments, parents):
    seg_ids = jnp.arange(1 + NBRANCH + NLEAF, dtype=jnp.int32)
    member = (segments[:, None] == seg_ids[None, :]).astype(jnp.int32)
    seg_lengths = jnp.sum(member, axis=0)
    seg_starts = jnp.cumsum(seg_lengths) - seg_lengths
    parent_of = jnp.concatenate([jnp.full((1 + NBRANCH,), -1, jnp.int32), 1 + parents])
    branch_ids = jnp.arange(NBRANCH, dtype=jnp.int32)
    parent_pick = (parents[:, None] == branch_ids[None, :]).astype(jnp.int32)
    parent_len = jnp.sum(parent_pick * seg_lengths[1 : 1 + NBRANCH][None, :], axis=1)
    base_depth = jnp.concatenate(
        [
            jnp.zeros((1,), jnp.int32),
            seg_lengths[0] * jnp.ones((NBRANCH,), jnp.int32),
            seg_lengths[0] + parent_len,
        ]
    )
    places = jnp.arange(segments.shape[0], dtype=jnp.int32)
    depth = places + jnp.sum(member * (base_depth - seg_starts)[None, :], axis=1)
    parent = jnp.sum(member * parent_of[None, :], axis=1)
    freqs = jnp.exp(jnp.arange(HD // 2, dtype=jnp.float32) * (-2.0 * math.log(rope_theta) / HD))
    angles = depth.astype(jnp.float32)[:, None] * freqs[None, :]
    cosines, sines = jnp.cos(angles), jnp.sin(angles)
    return (
        jnp.concatenate([cosines] * 4, axis=1),
        jnp.concatenate([-sines, sines] * 2, axis=1),
        jnp.broadcast_to(segments[:, None].astype(jnp.float32), (segments.shape[0], 128)),
        jnp.broadcast_to(parent[:, None].astype(jnp.float32), (segments.shape[0], 128)),
        jnp.broadcast_to(segments[None, :].astype(jnp.float32), (8, segments.shape[0])),
    )

def dot_nn(a, b):
    return lax.dot_general(a, b, (((1,), (0,)), ((), ())), preferred_element_type=jnp.float32)


def dot_nt(a, b):
    return lax.dot_general(a, b, (((1,), (1,)), ((), ())), preferred_element_type=jnp.float32)


def dot_tn(a, b):
    return lax.dot_general(a, b, (((0,), (0,)), ((), ())), preferred_element_type=jnp.float32)


MICRO = 2
TREE = 1024
OWN = 256
WIDE = 2048
NX, NC, NZ, NY = 2, 2, 4, 2
SEG = 128
MESH = pl.DeviceIdType.MESH
HBM = pl.BlockSpec(memory_space=pl.ANY)


class Place:
    def __init__(self):
        row, col = lax.axis_index("row"), lax.axis_index("col")
        self.row, self.col = row, col
        self.z, self.y = row // NY, row % NY
        self.x, self.c = col // NC, col % NC
        self.own = col
        self.row_z = [lax.rem(row + NY * off, NZ * NY) for off in range(NZ)]
        self.row_y = self.z * NY + (1 - self.y)
        self.row_yz = [lax.rem(self.z + off, NZ) * NY + (1 - self.y) for off in range(NZ)]
        self.col_x = (1 - self.x) * NC + self.c
        self.col_c = self.x * NC + (1 - self.c)
        self.col_xc = (1 - self.x) * NC + (1 - self.c)
        self.at_z = [None] + [(self.row_z[off], col) for off in range(1, NZ)]
        self.at_y = (self.row_y, col)
        self.at_x = (row, self.col_x)
        self.at_c = (row, self.col_c)

    def greet(self):
        barrier = pltpu.get_barrier_semaphore()
        partners = self.at_z[1:] + [self.at_y, self.at_x, self.at_c]
        for partner in partners:
            pl.semaphore_signal(barrier, inc=1, device_id=partner, device_id_type=MESH)
        pl.semaphore_wait(barrier, len(partners))


class Copies:
    def __init__(self):
        self.open_sends = []

    def send(self, src, dst, send_sem, recv_sem, device):
        copy = pltpu.make_async_remote_copy(
            src_ref=src, dst_ref=dst, send_sem=send_sem, recv_sem=recv_sem,
            device_id=device, device_id_type=MESH,
        )
        copy.start()
        self.open_sends.append(copy)
        return copy

    def arrive(self, dst, send_sem, recv_sem, device):
        pltpu.make_async_remote_copy(
            src_ref=dst, dst_ref=dst, send_sem=send_sem, recv_sem=recv_sem,
            device_id=device, device_id_type=MESH,
        ).wait_recv()

    def local(self, src, dst, sem):
        copy = pltpu.make_async_copy(src, dst, sem)
        copy.start()
        return copy

    def close(self):
        for copy in self.open_sends:
            copy.wait_send()
        self.open_sends = []


def rows_of(index, size):
    return pl.ds(pl.multiple_of(index * size, size), size)


class WeightGather:
    def __init__(self, place, copies, own, full, view, send, recv, keep):
        self.place, self.copies, self.own, self.full, self.view = place, copies, own, full, view
        self.send, self.recv, self.keep = send, recv, keep

    def start(self):
        p = self.place
        here = self.view(self.full, p.row)
        self.kept = self.copies.local(self.own, here, self.keep)
        for off in (1, 3, 2):
            self.copies.send(self.own, here, self.send.at[off - 1], self.recv.at[p.row], p.at_z[off])
        self.copies.send(self.own, here, self.send.at[3], self.recv.at[p.row], p.at_y)

    def relay(self):
        p = self.place
        for off in (1, 3, 2):
            block = self.view(self.full, p.row_z[off])
            self.copies.arrive(block, self.send.at[3 + off], self.recv.at[p.row_z[off]], p.at_y)
            self.copies.send(block, block, self.send.at[3 + off], self.recv.at[p.row_z[off]], p.at_y)

    def finish(self):
        p = self.place
        for off in range(NZ):
            block = self.view(self.full, p.row_yz[off])
            self.copies.arrive(block, self.send.at[3], self.recv.at[p.row_yz[off]], p.at_y)
        self.kept.wait()


class TokenGather:
    def __init__(self, place, copies, full, base, send, recv):
        self.place, self.copies, self.full, self.base = place, copies, full, base
        self.send, self.recv = send, recv

    def block(self, index):
        return self.full.at[pl.ds(pl.multiple_of(self.base + index * OWN, OWN), OWN), :]

    def start(self, own, keep):
        p = self.place
        here = self.block(p.own)
        self.kept = self.copies.local(own, here, keep)
        self.copies.send(own, here, self.send.at[0], self.recv.at[p.own], p.at_x)
        self.copies.send(own, here, self.send.at[1], self.recv.at[p.own], p.at_c)

    def relay(self):
        p = self.place
        block = self.block(p.col_x)
        self.copies.arrive(block, self.send.at[2], self.recv.at[p.col_x], p.at_c)
        self.copies.send(block, block, self.send.at[2], self.recv.at[p.col_x], p.at_c)

    def finish(self):
        p = self.place
        for index in (p.col_c, p.col_xc):
            self.copies.arrive(self.block(index), self.send.at[2], self.recv.at[index], p.at_c)
        self.kept.wait()


class TokenSum:
    def __init__(self, place, copies, partial, from_core, from_x, send, recv):
        self.place, self.copies, self.partial = place, copies, partial
        self.from_core, self.from_x, self.send, self.recv = from_core, from_x, send, recv

    def start(self):
        p = self.place
        self.sent = []
        for there in range(NX):
            self.sent.append(
                self.copies.send(
                    self.partial.at[there * NC + (1 - p.c)], self.from_core.at[there],
                    self.send.at[there], self.recv.at[there], p.at_c,
                )
            )

    def middle(self):
        p = self.place
        for there in range(NX):
            self.copies.arrive(self.from_core.at[there], self.send.at[there], self.recv.at[there], p.at_c)
        away = 1 - p.x

        @pl.loop(0, OWN // 32)
        def _(i):
            rows = rows_of(i, 32)
            self.partial[p.col_x, rows, :] = (
                self.partial[p.col_x, rows, :].astype(jnp.float32)
                + self.from_core[away, rows, :].astype(jnp.float32)
            ).astype(jnp.bfloat16)

        self.passed = self.copies.send(
            self.partial.at[p.col_x], self.from_x, self.send.at[2], self.recv.at[2], p.at_x
        )

    def arrive(self):
        p = self.place
        self.copies.arrive(self.from_x, self.send.at[2], self.recv.at[2], p.at_x)

    def rows(self, rows):
        p = self.place
        return (
            self.partial[p.own, rows, :].astype(jnp.float32)
            + self.from_core[p.x, rows, :].astype(jnp.float32)
            + self.from_x[rows, :].astype(jnp.float32)
        )


def swap_halves(tile):
    lane = lax.broadcasted_iota(jnp.int32, tile.shape, 1)
    return jnp.where(lane % HD < HD // 2, pltpu.roll(tile, 128 - HD // 2, 1), pltpu.roll(tile, HD // 2, 1))


def masked_parts(run, seg_col, parent_col, seg_row):
    rows = slice(run * SEG, (run + 1) * SEG)

    def causal():
        shape = (SEG, 2 * SEG)
        return lax.broadcasted_iota(jnp.int32, shape, 1) <= lax.broadcasted_iota(jnp.int32, shape, 0) + run * SEG

    def of_parent():
        return seg_row[0:1, 2 * SEG : 4 * SEG] == parent_col[rows, 0:1]

    def of_run():
        shape = (SEG, SEG)
        order = lax.broadcasted_iota(jnp.int32, shape, 1) <= lax.broadcasted_iota(jnp.int32, shape, 0)
        return order & (seg_row[0:1, rows] == seg_col[rows, 0:1])

    if run < 2:
        return [(slice(0, 2 * SEG), causal())]
    parts = [(slice(0, 2 * SEG), None)]
    if run >= 4:
        parts.append((slice(2 * SEG, 4 * SEG), of_parent()))
    parts.append((rows, of_run()))
    return parts


def softmax_parts(scores):
    peak = None
    for score in scores:
        top = jnp.max(score, axis=-1, keepdims=True)
        peak = top if peak is None else jnp.maximum(peak, top)
    exps = [jnp.exp((score - peak) * score_mult) for score in scores]
    total = None
    for term in exps:
        part = jnp.sum(term, axis=-1, keepdims=True)
        total = part if total is None else total + part
    return exps, 1.0 / total


def stacked_pairs(tile_ref, rows):
    both = jnp.concatenate([tile_ref[rows, 0:128], tile_ref[rows, 128:256]], axis=0)
    lane = lax.broadcasted_iota(jnp.int32, both.shape, 1)
    zero = jnp.zeros_like(both)
    return jnp.concatenate([jnp.where(lane < HD, both, zero), jnp.where(lane < HD, zero, both)], axis=0)


def unstack_pairs(wide):
    half = wide.shape[0] // 2
    lane = lax.broadcasted_iota(jnp.int32, (half, 128), 1)
    return jnp.where(lane < HD, wide[:half], wide[half:])


def twice(kv):
    wide = kv.astype(jnp.float32)
    lane = lax.broadcasted_iota(jnp.int32, wide.shape, 1)
    other = pltpu.roll(wide, HD, 1)
    key = jnp.where(lane < HD, wide, other)
    value = jnp.where(lane < HD, other, wide)
    return key.astype(jnp.bfloat16), value.astype(jnp.bfloat16)


def score_parts(queries, keys, parts):
    scores = []
    for span, mask in parts:
        score = dot_nt(queries, keys[span])
        if mask is not None:
            score = jnp.where(jnp.concatenate([mask] * 4, axis=0), score, masked_value)
        scores.append(score)
    return scores


def attend(qkv_ref, seg_col_ref, parent_col_ref, seg_row_ref, heads_ref):
    seg_row = seg_row_ref[...]
    keys, values = twice(qkv_ref[:, 256:384])
    for run in range(TREE // SEG):
        rows = slice(run * SEG, (run + 1) * SEG)
        parts = masked_parts(run, seg_col_ref, parent_col_ref, seg_row)
        exps, inverse = softmax_parts(score_parts(stacked_pairs(qkv_ref, rows), keys, parts))
        mixed = None
        for (span, _), term in zip(parts, exps):
            got = dot_nn((term * inverse).astype(jnp.bfloat16), values[span])
            mixed = got if mixed is None else mixed + got
        low = unstack_pairs(mixed).astype(jnp.bfloat16)
        heads_ref[rows, 0:128] = low[0:SEG]
        heads_ref[rows, 128:256] = low[SEG:]


def attend_back(
    key_sum, value_sum, qkv_ref, grad_ref, cos_ref, sin_ref, seg_col_ref, parent_col_ref, seg_row_ref, out_ref
):
    seg_row = seg_row_ref[...]
    keys, values = twice(qkv_ref[:, 256:384])
    key_sum[...] = jnp.zeros_like(key_sum)
    value_sum[...] = jnp.zeros_like(value_sum)
    for run in range(TREE // SEG):
        rows = slice(run * SEG, (run + 1) * SEG)
        parts = masked_parts(run, seg_col_ref, parent_col_ref, seg_row)
        queries = stacked_pairs(qkv_ref, rows)
        upstream = stacked_pairs(grad_ref, rows)
        exps, inverse = softmax_parts(score_parts(queries, keys, parts))
        probs = [term * inverse for term in exps]
        prob_grads = [dot_nt(upstream, values[span]) for span, _ in parts]
        inner = None
        for prob, prob_grad in zip(probs, prob_grads):
            term = jnp.sum(prob * prob_grad, axis=-1, keepdims=True)
            inner = term if inner is None else inner + term
        query_grad = None
        for (span, _), prob, prob_grad in zip(parts, probs, prob_grads):
            score_grad = (score_mult * prob * (prob_grad - inner)).astype(jnp.bfloat16)
            term = dot_nn(score_grad, keys[span])
            query_grad = term if query_grad is None else query_grad + term
            key_sum[span, :] += dot_tn(score_grad, queries)
            value_sum[span, :] += dot_tn(prob.astype(jnp.bfloat16), upstream)
        pair_grad = unstack_pairs(query_grad)
        cos, sin = cos_ref[rows, :], sin_ref[rows, :]
        for tile in range(2):
            part = pair_grad[tile * SEG : (tile + 1) * SEG]
            out_ref[rows, tile * 128 : (tile + 1) * 128] = (part * cos - swap_halves(part) * sin).astype(jnp.bfloat16)
    key_grad = key_sum[...]
    key_grad = key_grad + pltpu.roll(key_grad, HD, 1)
    value_grad = value_sum[...]
    value_grad = value_grad + pltpu.roll(value_grad, HD, 1)
    turned = key_grad * cos_ref[...] - swap_halves(key_grad) * sin_ref[...]
    lane = lax.broadcasted_iota(jnp.int32, turned.shape, 1)
    out_ref[:, 256:384] = jnp.where(lane < HD, turned, value_grad).astype(jnp.bfloat16)


def forward_kernel(
    near, tokens, cot, own_qkv, own_out, own_gu, own_down, gain, cosines, sines,
    seg_col, parent_col, seg_row,
    w_qkv, w_out, w_gu, w_down, attn_in, cot_full, ffn_in, qkv, heads, resid, gate, up, hidden, down_grad,
    partial, from_core, from_x, resid_buf, normed_buf, tokens_buf, gain_buf,
    w_send, w_recv, w_keep, t_send, t_recv, t_keep, s_send, s_recv, l_sem,
):
    place = Place()
    copies = Copies()
    place.greet()

    def row_block(full, r):
        return full.at[rows_of(r, OWN), :]

    def col_block(full, r):
        return full.at[:, rows_of(r, OWN)]

    def weight(index, own, full, view):
        return WeightGather(
            place, copies, own, full, view, w_send.at[index], w_recv.at[index], w_keep.at[index]
        )

    g_qkv = weight(0, own_qkv, w_qkv, row_block)
    g_out = weight(1, own_out, w_out, col_block)
    g_gate = weight(2, own_gu.at[0], w_gu.at[0], row_block)
    g_up = weight(3, own_gu.at[1], w_gu.at[1], row_block)
    g_down = weight(4, own_down, w_down, col_block)

    def token_gather(index, full, m):
        return TokenGather(place, copies, full, m * TREE, t_send.at[index], t_recv.at[index])

    a_in = [token_gather(m, attn_in, m) for m in range(MICRO)]
    a_cot = [token_gather(2 + m, cot_full, m) for m in range(MICRO)]
    a_ffn = [token_gather(4 + m, ffn_in, m) for m in range(MICRO)]
    sums = [
        TokenSum(place, copies, partial.at[m], from_core.at[m], from_x.at[m], s_send.at[m], s_recv.at[m])
        for m in range(MICRO)
    ]

    def project(m):
        def body(a_ref, w_ref, cos_ref, sin_ref, out_ref):
            got = dot_nn(a_ref[...], w_ref[...])
            cos, sin = cos_ref[...], sin_ref[...]
            lane = lax.broadcasted_iota(jnp.int32, cos.shape, 1)
            cos_key = jnp.where(lane < HD, cos, 1.0)
            sin_key = jnp.where(lane < HD, sin, 0.0)
            for tile in range(got.shape[1] // 128):
                part = got[:, tile * 128 : (tile + 1) * 128]
                is_key = tile % 3 == 2
                turned = part * (cos_key if is_key else cos) + swap_halves(part) * (sin_key if is_key else sin)
                out_ref[:, tile * 128 : (tile + 1) * 128] = turned.astype(jnp.bfloat16)

        steps = TREE // OWN
        rows = pl.BlockSpec((OWN, D), lambda i: (m * steps + i, 0))
        table = pl.BlockSpec((OWN, 128), lambda i: (m * steps + i, 0))
        out = pl.BlockSpec((OWN, 768), lambda i: (m * steps + i, 0))
        whole = pl.BlockSpec((D, 768), lambda i: (0, 0))
        pltpu.emit_pipeline(body, grid=(steps,), in_specs=[rows, whole, table, table], out_specs=[out])(
            attn_in, w_qkv, cosines, sines, qkv
        )

    def attention(m):
        tree = pl.BlockSpec((TREE, 128), lambda g: (m, 0))
        pltpu.emit_pipeline(
            attend,
            grid=(2,),
            in_specs=[
                pl.BlockSpec((TREE, 384), lambda g: (m, g)),
                tree,
                tree,
                pl.BlockSpec((8, TREE), lambda g: (m, 0)),
            ],
            out_specs=[pl.BlockSpec((TREE, 256), lambda g: (m, g))],
        )(qkv, seg_col, parent_col, seg_row, heads)

    def out_project(m):
        def body_at(step, a_ref, w_ref):
            partial[m, step.index[0]] = dot_nn(a_ref[...], w_ref[...]).astype(jnp.bfloat16)

        steps = TREE // OWN
        pltpu.emit_pipeline(
            body_at,
            grid=(steps,),
            in_specs=[
                pl.BlockSpec((OWN, 512), lambda i: (m * steps + i, 0)),
                pl.BlockSpec((512, D), lambda i: (0, 0)),
            ],
            out_specs=[],
            _explicit_indices=True,
        )(heads, w_out)

    def middle_norm(m):
        sums[m].arrive()
        load = copies.local(tokens.at[m], tokens_buf, l_sem.at[0])
        load_gain = copies.local(gain, gain_buf, l_sem.at[1])
        load.wait()
        load_gain.wait()

        @pl.loop(0, OWN // 32)
        def _(i):
            rows = rows_of(i, 32)
            value = tokens_buf[rows, :].astype(jnp.float32) + residual_mult * sums[m].rows(rows)
            resid_buf[m, rows, :] = value
            scale = lax.rsqrt(jnp.mean(value * value, axis=-1, keepdims=True) + norm_eps)
            normed_buf[m, rows, :] = (value * scale * gain_buf[1:2, :]).astype(jnp.bfloat16)

        a_ffn[m].start(normed_buf.at[m], t_keep.at[4 + m])
        return copies.local(resid_buf.at[m], resid.at[m], l_sem.at[2 + m])

    def gate_up(m):
        def body(a_ref, g_ref, u_ref, gate_ref, up_ref, hidden_ref):
            for part in range(TREE // OWN):
                rows = slice(part * OWN, (part + 1) * OWN)
                value = a_ref[rows, :]
                g = dot_nn(value, g_ref[0])
                u = dot_nn(value, u_ref[0])
                gate_ref[rows, :] = g.astype(jnp.bfloat16)
                up_ref[rows, :] = u.astype(jnp.bfloat16)
                hidden_ref[rows, :] = (g * jax.nn.sigmoid(g) * u).astype(jnp.bfloat16)

        cols = pl.BlockSpec((TREE, 256), lambda j: (m, j))
        pltpu.emit_pipeline(
            body,
            grid=(WIDE // 256,),
            in_specs=[
                pl.BlockSpec((TREE, D), lambda j: (m, 0)),
                pl.BlockSpec((1, D, 256), lambda j: (0, 0, j)),
                pl.BlockSpec((1, D, 256), lambda j: (1, 0, j)),
            ],
            out_specs=[cols, cols, cols],
        )(ffn_in, w_gu, w_gu, gate, up, hidden)

    def grad_down():
        def body(h_ref, c_ref, out_ref):
            out_ref[...] = (residual_mult * dot_tn(h_ref[...], c_ref[...])).astype(jnp.bfloat16)

        pltpu.emit_pipeline(
            body,
            grid=(WIDE // 256,),
            in_specs=[
                pl.BlockSpec((MICRO * TREE, 256), lambda i: (0, i)),
                pl.BlockSpec((MICRO * TREE, D), lambda i: (0, 0)),
            ],
            out_specs=[pl.BlockSpec((256, D), lambda i: (i, 0))],
        )(hidden, cot_full, down_grad)

    g_qkv.start()
    for m in range(MICRO):
        a_in[m].start(near.at[m], t_keep.at[m])
    g_out.start()
    g_gate.start()
    for m in range(MICRO):
        a_cot[m].start(cot.at[m], t_keep.at[2 + m])
    a_in[0].relay()
    a_in[1].relay()
    g_qkv.relay()
    g_out.relay()
    g_up.start()
    a_in[0].finish()
    g_qkv.finish()
    project(0)
    a_in[1].finish()
    project(1)
    a_cot[0].relay()
    a_cot[1].relay()
    attention(0)
    g_out.finish()
    out_project(0)
    sums[0].start()
    attention(1)
    sums[0].middle()
    out_project(1)
    sums[1].start()
    g_gate.relay()
    g_down.start()
    stored = [middle_norm(0)]
    sums[1].middle()
    a_ffn[0].relay()
    stored.append(middle_norm(1))
    a_ffn[1].relay()
    g_up.relay()
    a_cot[0].finish()
    a_cot[1].finish()
    a_ffn[0].finish()
    g_gate.finish()
    g_up.finish()
    gate_up(0)
    a_ffn[1].finish()
    gate_up(1)
    g_down.relay()
    grad_down()
    g_down.finish()
    for copy in stored:
        copy.wait()
    copies.close()


def forward(near, tokens, cot, low_qkv, low_out, low_gu, low_down, gains, cosines, sines, seg_col, parent_col, seg_row):
    low = jnp.bfloat16
    shape = jax.ShapeDtypeStruct
    all_tokens = MICRO * TREE
    outs = [
        shape((D, 768), low), shape((512, D), low), shape((2, D, WIDE), low), shape((WIDE, D), low),
        shape((all_tokens, D), low), shape((all_tokens, D), low), shape((all_tokens, D), low),
        shape((all_tokens, 768), low), shape((all_tokens, 512), low), shape((MICRO, OWN, D), jnp.float32),
        shape((all_tokens, WIDE), low), shape((all_tokens, WIDE), low), shape((all_tokens, WIDE), low),
        shape((WIDE, D), low),
    ]
    dma = pltpu.SemaphoreType.DMA
    return pl.pallas_call(
        forward_kernel,
        out_shape=outs,
        in_specs=[HBM] * 13,
        out_specs=[HBM] * len(outs),
        scratch_shapes=[
            pltpu.VMEM((MICRO, NX * NC, OWN, D), low),
            pltpu.VMEM((MICRO, NX, OWN, D), low),
            pltpu.VMEM((MICRO, OWN, D), low),
            pltpu.VMEM((MICRO, OWN, D), jnp.float32),
            pltpu.VMEM((MICRO, OWN, D), low),
            pltpu.VMEM((OWN, D), low),
            pltpu.VMEM((2, D), jnp.float32),
            dma((5, 7)), dma((5, NZ * NY)), dma((5,)),
            dma((6, 3)), dma((6, NX * NC)), dma((6,)),
            dma((MICRO, 3)), dma((MICRO, 3)), dma((4,)),
        ],
        compiler_params=pltpu.CompilerParams(
            collective_id=0, has_side_effects=True, vmem_limit_bytes=60 * 1024 * 1024
        ),
        cost_estimate=pl.CostEstimate(flops=90 * 10**9, bytes_accessed=2 * 10**8, transcendentals=10**7),
        name="forward",
    )(near, tokens, cot, low_qkv, low_out, low_gu, low_down, gains, cosines, sines, seg_col, parent_col, seg_row)


class GradSum:
    ORDER = (2, 1, 3)

    def __init__(self, place, copies, full, view, from_y, summed, from_z, owned, squares, sems):
        self.place, self.copies, self.full, self.view = place, copies, full, view
        self.from_y, self.summed, self.from_z, self.owned = from_y, summed, from_z, owned
        self.squares = squares
        self.y_send, self.y_recv, self.z_send, self.z_recv = sems
        rows, cols = owned.shape
        step = max(16, min(rows, (256 * 1024) // cols))
        self.grid = rows // step
        self.spec = pl.BlockSpec((step, cols), lambda i: (i, 0))

    def start(self):
        p = self.place
        for off in self.ORDER + (0,):
            self.copies.send(
                self.view(self.full, p.row_yz[off]), self.from_y.at[off], self.y_send.at[off], self.y_recv.at[off], p.at_y
            )

    def got_y(self, off):
        self.copies.arrive(self.from_y.at[off], self.y_send.at[off], self.y_recv.at[off], self.place.at_y)

    def middle(self, off):
        p = self.place
        self.got_y(off)

        def body(a_ref, b_ref, out_ref):
            out_ref[...] = (a_ref[...].astype(jnp.float32) + b_ref[...].astype(jnp.float32)).astype(jnp.bfloat16)

        mine = self.view(self.full, p.row_z[off])
        pltpu.emit_pipeline(body, grid=(self.grid,), in_specs=[self.spec] * 2, out_specs=[self.spec])(
            mine, self.from_y.at[off], self.summed.at[off - 1]
        )
        self.copies.send(
            self.summed.at[off - 1], self.from_z.at[off - 1], self.z_send.at[off - 1], self.z_recv.at[off - 1], p.at_z[off]
        )

    def end(self):
        p = self.place
        self.got_y(0)
        for off in (1, 3, 2):
            self.copies.arrive(self.from_z.at[off - 1], self.z_send.at[off - 1], self.z_recv.at[off - 1], p.at_z[off])

        def body(a_ref, b_ref, c_ref, d_ref, e_ref, out_ref):
            total = a_ref[...].astype(jnp.float32)
            for ref in (b_ref, c_ref, d_ref, e_ref):
                total = total + ref[...].astype(jnp.float32)
            out_ref[...] = total
            cols = total.shape[1]
            self.squares[0:1, 0:cols] += jnp.sum(total * total, axis=0, keepdims=True)

        mine = self.view(self.full, p.row)
        pltpu.emit_pipeline(body, grid=(self.grid,), in_specs=[self.spec] * 5, out_specs=[self.spec])(
            mine, self.from_y.at[0], self.from_z.at[0], self.from_z.at[1], self.from_z.at[2], self.owned
        )


def backward_kernel(
    w_qkv, w_out, w_gu, w_down, attn_in, cot_full, ffn_in, qkv, heads, resid, gate, up, hidden, down_grad,
    tokens, cot, gain, cosines, sines, seg_col, parent_col, seg_row,
    mixed, d_tokens, own_qkv, own_out, own_gate, own_up, own_down, gain_out, square_out,
    gate_grad, up_grad, out_back, heads_grad, proj_grad, gu_grad, out_grad, qkv_grad,
    y_qkv, y_out, y_gate, y_up, y_down, s_qkv, s_out, s_gate, s_up, s_down, z_qkv, z_out, z_gate, z_up, z_down,
    partial, from_core, from_x, mid, wide_buf, low_buf, near_buf, gain_buf, gain_sum, squares, key_sum, value_sum,
    r_ysend, r_yrecv, r_zsend, r_zrecv, t_send, t_recv, t_keep, u_send, u_recv, l_sem,
):
    place = Place()
    copies = Copies()
    place.greet()

    def row_block(full, r):
        return full.at[rows_of(r, OWN), :]

    def col_block(full, r):
        return full.at[:, rows_of(r, OWN)]

    def grad_sum(index, full, view, *refs):
        sems = (r_ysend.at[index], r_yrecv.at[index], r_zsend.at[index], r_zrecv.at[index])
        return GradSum(place, copies, full, view, *refs, squares, sems)

    r_qkv = grad_sum(0, qkv_grad, row_block, y_qkv, s_qkv, z_qkv, own_qkv)
    r_out = grad_sum(1, out_grad, col_block, y_out, s_out, z_out, own_out)
    r_gate = grad_sum(2, gu_grad.at[0], row_block, y_gate, s_gate, z_gate, own_gate)
    r_up = grad_sum(3, gu_grad.at[1], row_block, y_up, s_up, z_up, own_up)
    r_down = grad_sum(4, down_grad, col_block, y_down, s_down, z_down, own_down)
    a_back = [
        TokenGather(place, copies, out_back, m * TREE, t_send.at[m], t_recv.at[m]) for m in range(MICRO)
    ]

    def token_sum(turn, m):
        lands = 1 if turn == 1 else 0
        return TokenSum(
            place, copies, partial.at[m], from_core.at[lands, m], from_x.at[lands, m], u_send.at[turn, m], u_recv.at[turn, m]
        )

    ffn_sum = [token_sum(0, m) for m in range(MICRO)]
    mlp_sum = [token_sum(1, m) for m in range(MICRO)]
    attn_sum = [token_sum(2, m) for m in range(MICRO)]

    def grad_hidden(m):
        def body(c_ref, w_ref, gate_ref, up_ref, gate_out, up_out):
            for part in range(TREE // OWN):
                rows = slice(part * OWN, (part + 1) * OWN)
                back = residual_mult * dot_nt(c_ref[rows, :], w_ref[...])
                g = gate_ref[rows, :].astype(jnp.float32)
                u = up_ref[rows, :].astype(jnp.float32)
                act = jax.nn.sigmoid(g)
                gate_out[rows, :] = (back * u * act * (1.0 + g * (1.0 - act))).astype(jnp.bfloat16)
                up_out[rows, :] = (back * g * act).astype(jnp.bfloat16)

        cols = pl.BlockSpec((TREE, 256), lambda j: (m, j))
        pltpu.emit_pipeline(
            body,
            grid=(WIDE // 256,),
            in_specs=[
                pl.BlockSpec((TREE, D), lambda j: (m, 0)),
                pl.BlockSpec((256, D), lambda j: (j, 0)),
                cols,
                cols,
            ],
            out_specs=[cols, cols],
        )(cot_full, w_down, gate, up, gate_grad, up_grad)

    def grad_weight(near_all, far_all, out, near_cols, far_cols):
        def body(a_ref, b_ref, out_ref):
            out_ref[...] = dot_tn(a_ref[...], b_ref[...]).astype(jnp.bfloat16)

        step = min(256, near_cols)
        pltpu.emit_pipeline(
            body,
            grid=(near_cols // step,),
            in_specs=[
                pl.BlockSpec((MICRO * TREE, step), lambda i: (0, i)),
                pl.BlockSpec((MICRO * TREE, far_cols), lambda i: (0, 0)),
            ],
            out_specs=[pl.BlockSpec((step, far_cols), lambda i: (i, 0))],
        )(near_all, far_all, out)

    def back_ffn(m):
        def body(step, g_ref, u_ref, wg_ref, wu_ref):
            for part in range(TREE // OWN):
                rows = slice(part * OWN, (part + 1) * OWN)
                value = dot_nt(g_ref[rows, :], wg_ref[0]) + dot_nt(u_ref[rows, :], wu_ref[0])
                partial[m, part, :, pl.ds(pl.multiple_of(step.index[0] * 256, 256), 256)] = value.astype(jnp.bfloat16)

        tree = pl.BlockSpec((TREE, WIDE), lambda j: (m, 0))
        pltpu.emit_pipeline(
            body,
            grid=(D // 256,),
            in_specs=[
                tree,
                tree,
                pl.BlockSpec((1, 256, WIDE), lambda j: (0, j, 0)),
                pl.BlockSpec((1, 256, WIDE), lambda j: (1, j, 0)),
            ],
            out_specs=[],
            _explicit_indices=True,
        )(gate_grad, up_grad, w_gu, w_gu)

    def down(m):
        def body(step, h_ref, w_ref):
            for part in range(TREE // OWN):
                rows = slice(part * OWN, (part + 1) * OWN)
                value = dot_nn(h_ref[rows, :], w_ref[...])
                partial[m, part, :, pl.ds(pl.multiple_of(step.index[0] * 256, 256), 256)] = value.astype(jnp.bfloat16)

        pltpu.emit_pipeline(
            body,
            grid=(D // 256,),
            in_specs=[
                pl.BlockSpec((TREE, WIDE), lambda j: (m, 0)),
                pl.BlockSpec((WIDE, 256), lambda j: (0, j)),
            ],
            out_specs=[],
            _explicit_indices=True,
        )(hidden, w_down)

    def back_heads(m):
        def body(a_ref, w_ref, out_ref):
            out_ref[...] = dot_nt(a_ref[...], w_ref[...]).astype(jnp.bfloat16)

        steps = TREE // OWN
        pltpu.emit_pipeline(
            body,
            grid=(steps,),
            in_specs=[
                pl.BlockSpec((OWN, D), lambda i: (m * steps + i, 0)),
                pl.BlockSpec((512, D), lambda i: (0, 0)),
            ],
            out_specs=[pl.BlockSpec((OWN, 512), lambda i: (m * steps + i, 0))],
        )(out_back, w_out, heads_grad)

    def back_attention(m):
        tree = pl.BlockSpec((TREE, 128), lambda g: (m, 0))
        group = pl.BlockSpec((TREE, 384), lambda g: (m, g))
        pltpu.emit_pipeline(
            functools.partial(attend_back, key_sum, value_sum),
            grid=(2,),
            in_specs=[
                group,
                pl.BlockSpec((TREE, 256), lambda g: (m, g)),
                tree,
                tree,
                tree,
                tree,
                pl.BlockSpec((8, TREE), lambda g: (m, 0)),
            ],
            out_specs=[group],
        )(qkv, heads_grad, cosines, sines, seg_col, parent_col, seg_row, proj_grad)

    def back_project(m):
        def body(step, a_ref, w_ref):
            partial[m, step.index[0]] = dot_nt(a_ref[...], w_ref[...]).astype(jnp.bfloat16)

        steps = TREE // OWN
        pltpu.emit_pipeline(
            body,
            grid=(steps,),
            in_specs=[
                pl.BlockSpec((OWN, 768), lambda i: (m * steps + i, 0)),
                pl.BlockSpec((D, 768), lambda i: (0, 0)),
            ],
            out_specs=[],
            _explicit_indices=True,
        )(proj_grad, w_qkv)

    def norm_back_rows(value, upstream, which):
        row_gain = gain_buf[which : which + 1, :]
        scale = lax.rsqrt(jnp.mean(value * value, axis=-1, keepdims=True) + norm_eps)
        scaled = upstream * row_gain
        inner = jnp.mean(scaled * value, axis=-1, keepdims=True)
        gain_sum[which : which + 1, :] += jnp.sum(upstream * value * scale, axis=0, keepdims=True)
        return scale * scaled - value * (scale * scale * scale * inner)

    def middle_back(m):
        ffn_sum[m].arrive()
        load = copies.local(resid.at[m], wide_buf, l_sem.at[0])
        load_low = copies.local(cot.at[m], low_buf, l_sem.at[1])
        load.wait()
        load_low.wait()

        @pl.loop(0, OWN // 16)
        def _(i):
            rows = rows_of(i, 16)
            back = norm_back_rows(wide_buf[rows, :], ffn_sum[m].rows(rows), 1)
            value = low_buf[rows, :].astype(jnp.float32) + back
            mid[m, rows, :] = value
            near_buf[m, rows, :] = (residual_mult * value).astype(jnp.bfloat16)

        a_back[m].start(near_buf.at[m], t_keep.at[m])

    def finish_mixed(m):
        mlp_sum[m].arrive()
        load = copies.local(resid.at[m], wide_buf, l_sem.at[0])
        load.wait()

        @pl.loop(0, OWN // 16)
        def _(i):
            rows = rows_of(i, 16)
            low_buf[rows, :] = (wide_buf[rows, :] + residual_mult * mlp_sum[m].rows(rows)).astype(jnp.bfloat16)

        copies.local(low_buf, mixed.at[m], l_sem.at[1]).wait()

    def finish_tokens(m):
        attn_sum[m].arrive()
        copies.local(tokens.at[m], low_buf, l_sem.at[1]).wait()

        @pl.loop(0, OWN // 16)
        def _(i):
            rows = rows_of(i, 16)
            back = norm_back_rows(low_buf[rows, :].astype(jnp.float32), attn_sum[m].rows(rows), 0)
            mid[m, rows, :] = mid[m, rows, :] + back

        return copies.local(mid.at[m], d_tokens.at[m], l_sem.at[2 + m])

    def sent(part):
        done = part.sent + [part.passed]
        for copy in done:
            copy.wait_send()
        copies.open_sends = [copy for copy in copies.open_sends if not any(copy is gone for gone in done)]

    r_down.start()
    load_gain = copies.local(gain, gain_buf, l_sem.at[0])
    gain_sum[...] = jnp.zeros_like(gain_sum)
    squares[...] = jnp.zeros_like(squares)
    load_gain.wait()
    grad_hidden(0)
    grad_hidden(1)
    back_ffn(0)
    ffn_sum[0].start()
    r_down.middle(2)
    back_ffn(1)
    ffn_sum[1].start()
    ffn_sum[0].middle()
    r_down.middle(1)
    grad_weight(ffn_in, gate_grad, gu_grad.at[0], D, WIDE)
    r_gate.start()
    ffn_sum[1].middle()
    r_down.middle(3)
    middle_back(0)
    middle_back(1)
    sent(ffn_sum[0])
    down(0)
    mlp_sum[0].start()
    r_gate.middle(2)
    a_back[0].relay()
    a_back[1].relay()
    sent(ffn_sum[1])
    down(1)
    mlp_sum[1].start()
    mlp_sum[0].middle()
    r_gate.middle(1)
    grad_weight(ffn_in, up_grad, gu_grad.at[1], D, WIDE)
    r_up.start()
    mlp_sum[1].middle()
    r_gate.middle(3)
    a_back[0].finish()
    back_heads(0)
    back_attention(0)
    finish_mixed(0)
    sent(mlp_sum[0])
    back_project(0)
    attn_sum[0].start()
    r_up.middle(2)
    a_back[1].finish()
    back_heads(1)
    back_attention(1)
    finish_mixed(1)
    sent(mlp_sum[1])
    back_project(1)
    attn_sum[1].start()
    attn_sum[0].middle()
    grad_weight(attn_in, proj_grad, qkv_grad, D, 768)
    r_qkv.start()
    grad_weight(heads, out_back, out_grad, 512, D)
    r_out.start()
    r_up.middle(1)
    attn_sum[1].middle()
    r_up.middle(3)
    r_down.end()
    stores = [finish_tokens(0)]
    for off in GradSum.ORDER:
        r_qkv.middle(off)
    stores.append(finish_tokens(1))
    for off in GradSum.ORDER:
        r_out.middle(off)
    stores.append(copies.local(gain_sum, gain_out, l_sem.at[0]))
    r_gate.end()
    r_up.end()
    r_qkv.end()
    r_out.end()
    stores.append(copies.local(squares, square_out, l_sem.at[1]))
    for copy in stores:
        copy.wait()
    copies.close()


def backward(saved, tokens, cot, gains, tables):
    low = jnp.bfloat16
    wide = jnp.float32
    shape = jax.ShapeDtypeStruct
    all_tokens = MICRO * TREE
    blocks = [(OWN, 768), (512, OWN), (OWN, WIDE), (OWN, WIDE), (WIDE, OWN)]
    outs = [shape((MICRO, OWN, D), low), shape((MICRO, OWN, D), wide)]
    outs += [shape(block, wide) for block in blocks]
    outs += [shape((8, D), wide), shape((8, D), wide)]
    outs += [
        shape((all_tokens, WIDE), low), shape((all_tokens, WIDE), low), shape((all_tokens, D), low),
        shape((all_tokens, 512), low), shape((all_tokens, 768), low),
        shape((2, D, WIDE), low), shape((512, D), low), shape((D, 768), low),
    ]
    outs += [shape((NZ,) + block, low) for block in blocks]
    outs += [shape((NZ - 1,) + block, low) for block in blocks]
    outs += [shape((NZ - 1,) + block, low) for block in blocks]
    dma = pltpu.SemaphoreType.DMA
    return pl.pallas_call(
        backward_kernel,
        out_shape=outs,
        in_specs=[HBM] * 22,
        out_specs=[HBM] * len(outs),
        scratch_shapes=[
            pltpu.VMEM((MICRO, NX * NC, OWN, D), low),
            pltpu.VMEM((2, MICRO, NX, OWN, D), low),
            pltpu.VMEM((2, MICRO, OWN, D), low),
            pltpu.VMEM((MICRO, OWN, D), wide),
            pltpu.VMEM((OWN, D), wide),
            pltpu.VMEM((OWN, D), low),
            pltpu.VMEM((MICRO, OWN, D), low),
            pltpu.VMEM((2, D), wide),
            pltpu.VMEM((8, D), wide),
            pltpu.VMEM((8, D), wide),
            pltpu.VMEM((TREE, 128), wide),
            pltpu.VMEM((TREE, 128), wide),
            dma((5, NZ)), dma((5, NZ)), dma((5, NZ)), dma((5, NZ)),
            dma((MICRO, 3)), dma((MICRO, NX * NC)), dma((MICRO,)),
            dma((3, MICRO, 3)), dma((3, MICRO, 3)), dma((4,)),
        ],
        compiler_params=pltpu.CompilerParams(
            collective_id=1, has_side_effects=True, vmem_limit_bytes=63 * 1024 * 1024
        ),
        cost_estimate=pl.CostEstimate(flops=140 * 10**9, bytes_accessed=5 * 10**8, transcendentals=10**7),
        name="backward",
    )(*saved, tokens, cot, gains, *tables)


def fast_local(
    tokens,
    cotangent,
    segment_of,
    leaf_parent,
    w_qkv,
    mom_qkv,
    w_out,
    mom_out,
    w_gu,
    mom_gu,
    w_down,
    mom_down,
    gains,
    mom_gains,
):
    low = jnp.bfloat16
    tables = [position_tables(segment_of[m], leaf_parent[m]) for m in range(MICRO)]
    tables = [jnp.concatenate([table[i] for table in tables], axis=0) for i in range(5)]
    near, _ = normalize(tokens.astype(jnp.float32), gains[0])
    saved = forward(
        near.astype(low), tokens, cotangent,
        w_qkv.astype(low).reshape(OWN, 768), w_out.astype(low), w_gu.astype(low), w_down.astype(low),
        gains, *tables,
    )
    mixed, d_tokens, g_qkv, g_out, g_gate, g_up, g_down, gain_rows, squares = backward(
        saved, tokens, cotangent, gains, tables
    )[:9]
    owned = (g_qkv.reshape(w_qkv.shape), g_out, jnp.stack([g_gate, g_up]), g_down)
    local_squares = jnp.sum(squares[0])
    gain_partial = gain_rows[:2]
    total_squares, gain_total = lax.psum((local_squares, gain_partial), ("row", "col"))
    grad_norm = jnp.sqrt(total_squares + jnp.sum(gain_total * gain_total))
    factor = jnp.minimum(1.0, clip_bound() / (grad_norm + 1e-06))
    rates = step_rates()
    masters = (w_qkv, w_out, w_gu, w_down)
    states = (mom_qkv, mom_out, mom_gu, mom_down)
    results = []
    for index_w in range(4):
        updated, moments = adamw(
            masters[index_w], states[index_w], owned[index_w], factor, rates[index_w]
        )
        results.append((updated, moments, updated.astype(jnp.bfloat16)))
    new_gains, moments_gains = adamw(gains, mom_gains, gain_total, factor, rates[4])
    return (
        mixed,
        d_tokens,
        grad_norm,
        results[0][0],
        results[0][1],
        results[0][2],
        results[1][0],
        results[1][1],
        results[1][2],
        results[2][0],
        results[2][1],
        results[2][2],
        results[3][0],
        results[3][1],
        results[3][2],
        new_gains,
        moments_gains,
    )


def solution(mesh):
    placed = (
        P(None, ("row", "col"), None),
        P(None, ("row", "col"), None),
        P(None, "row"),
        P(None, "row"),
        P("row", "col", None),
        P(None, "row", "col", None),
        P("col", "row"),
        P(None, "col", "row"),
        P(None, "row", "col"),
        P(None, None, "row", "col"),
        P("col", "row"),
        P(None, "col", "row"),
        P(),
        P(),
    )
    sizes = dict(mesh.shape)
    fits = sizes == {"row": NZ * NY, "col": NX * NC}
    return jax.shard_map(
        fast_local if fits else local,
        mesh=mesh,
        in_specs=placed,
        out_specs=(
            P(None, ("row", "col"), None),
            P(None, ("row", "col"), None),
            P(),
            P("row", "col", None),
            P(None, "row", "col", None),
            P("row", "col", None),
            P("col", "row"),
            P(None, "col", "row"),
            P("col", "row"),
            P(None, "row", "col"),
            P(None, None, "row", "col"),
            P(None, "row", "col"),
            P("col", "row"),
            P(None, "col", "row"),
            P("col", "row"),
            P(),
            P(),
        ),
        check_vma=False,
    )
```

```python
import functools
import math

import jax
import jax.numpy as jnp
from jax import lax
from jax.experimental import pallas as pl
from jax.experimental.pallas import tpu as pltpu
from jax.sharding import PartitionSpec as P

D = 2048
FF = 8192
HD = 64
KVH = 8
GROUP = 4
NBRANCH = 4
NLEAF = 8
STEP = 7


norm_eps = 1e-05
residual_mult = 0.22
score_mult = 0.015625
rope_theta = 10000000.0
beta_one = 0.5
beta_two = 0.55
adam_eps = 1e-08
weight_decay = 0.1
masked_value = -1e30


def param_count():
    return D * KVH * (GROUP + 2) * HD + KVH * GROUP * HD * D + 3 * D * FF + 2 * D


def clip_bound():
    return math.sqrt(param_count())


def step_rates():
    return (
        max(D // 12, 1) ** (-0.5),
        max(D // 16, 1) ** (-0.5),
        D ** (-0.5),
        max(FF // 64, 1) ** (-0.5),
        0.3,
    )


def tree_tables(segments, parents):
    seg_count = 1 + NBRANCH + NLEAF
    seg_ids = jnp.arange(seg_count, dtype=jnp.int32)
    member = (segments[:, None] == seg_ids[None, :]).astype(jnp.int32)
    seg_lengths = jnp.sum(member, axis=0)
    seg_starts = jnp.cumsum(seg_lengths) - seg_lengths
    branch_ids = jnp.arange(NBRANCH, dtype=jnp.int32)
    parent_pick = (parents[:, None] == branch_ids[None, :]).astype(jnp.int32)
    parent_len = jnp.sum(parent_pick * seg_lengths[1 : 1 + NBRANCH][None, :], axis=1)
    trunk_len = seg_lengths[0]
    base_depth = jnp.concatenate(
        [
            jnp.zeros((1,), jnp.int32),
            trunk_len * jnp.ones((NBRANCH,), jnp.int32),
            trunk_len + parent_len,
        ]
    )
    places = jnp.arange(segments.shape[0], dtype=jnp.int32)
    depth = places + jnp.sum(member * (base_depth - seg_starts)[None, :], axis=1)
    identity = (seg_ids[:, None] == seg_ids[None, :]).astype(jnp.int32)
    rooted = jnp.broadcast_to((seg_ids[None, :] == 0).astype(jnp.int32), (seg_count, seg_count))
    leaf_links = jnp.concatenate(
        [jnp.zeros((NLEAF, 1), jnp.int32), parent_pick, jnp.zeros((NLEAF, NLEAF), jnp.int32)],
        axis=1,
    )
    leaf_links = jnp.concatenate(
        [jnp.zeros((1 + NBRANCH, seg_count), jnp.int32), leaf_links], axis=0
    )
    ancestry = jnp.minimum(identity + rooted + leaf_links, 1)
    token_path = jnp.dot(member, ancestry)
    allowed = (jnp.dot(token_path, member.T) > 0) & (depth[None, :] <= depth[:, None])
    freqs = jnp.exp(jnp.arange(HD // 2, dtype=jnp.float32) * (-2.0 * math.log(rope_theta) / HD))
    angles = depth.astype(jnp.float32)[:, None] * freqs[None, :]
    return (allowed, jnp.cos(angles), jnp.sin(angles))


def rotate(vectors, cosines, sines):
    half_width = vectors.shape[-1] // 2
    first_half = vectors[..., :half_width]
    second_half = vectors[..., half_width:]
    return jnp.concatenate(
        [first_half * cosines - second_half * sines, second_half * cosines + first_half * sines],
        axis=-1,
    )


def normalize(values, gain):
    scaling = lax.rsqrt(jnp.mean(values * values, axis=-1, keepdims=True) + norm_eps)
    return (values * scaling * gain, scaling)


def norm_back(values, scaling, gain, upstream):
    scaled = upstream * gain
    gain_grad = jnp.sum(upstream * values * scaling, axis=0)
    inner = jnp.mean(scaled * values, axis=-1, keepdims=True)
    return (scaling * scaled - values * scaling * scaling * scaling * inner, gain_grad)


def gather_forward(values):
    return lax.all_gather(values, "col", axis=0, tiled=True)


def gather_backward(values):
    return lax.all_gather(values, "col", axis=0, tiled=True)


def sum_forward(term_fn, row_count):
    return lax.psum_scatter(
        term_fn(jnp.int32(0), lax.axis_size("col") * row_count).astype(jnp.bfloat16),
        "col",
        scatter_dimension=0,
        tiled=True,
    ).astype(jnp.float32)


def sum_backward(term_fn, row_count):
    return lax.psum_scatter(
        term_fn(jnp.int32(0), lax.axis_size("col") * row_count).astype(jnp.bfloat16),
        "col",
        scatter_dimension=0,
        tiled=True,
    ).astype(jnp.float32)


def adamw(master, moments, raw_grad, factor, step_rate):
    clipped = factor * raw_grad
    first_moment = beta_one * moments[0] + (1.0 - beta_one) * clipped
    second_moment = beta_two * moments[1] + (1.0 - beta_two) * clipped * clipped
    first_hat = first_moment / (1.0 - beta_one**STEP)
    second_hat = second_moment / (1.0 - beta_two**STEP)
    updated = master - step_rate * (
        first_hat / (jnp.sqrt(second_hat) + adam_eps) + weight_decay * master
    )
    return (updated, jnp.stack([first_moment, second_moment]))


def local(
    tokens,
    cotangent,
    segment_of,
    leaf_parent,
    w_qkv,
    mom_qkv,
    w_out,
    mom_out,
    w_gu,
    mom_gu,
    w_down,
    mom_down,
    gains,
    mom_gains,
):
    low_shards = (
        w_qkv.astype(jnp.bfloat16),
        w_out.astype(jnp.bfloat16),
        w_gu.astype(jnp.bfloat16),
        w_down.astype(jnp.bfloat16),
    )

    def fetch():
        return (
            lax.all_gather(low_shards[0], "row", axis=0, tiled=True),
            lax.all_gather(low_shards[1], "row", axis=1, tiled=True),
            lax.all_gather(low_shards[2], "row", axis=1, tiled=True),
            lax.all_gather(low_shards[3], "row", axis=1, tiled=True),
        )

    outputs = []
    input_grads = []
    owned = None
    unsummed = None
    gain_partial = None
    for batch_index in range(tokens.shape[0]):
        x_local = tokens[batch_index].astype(jnp.float32)
        row_count = x_local.shape[0]
        allowed, cosines, sines = tree_tables(segment_of[batch_index], leaf_parent[batch_index])
        w_a, w_b, w_c, w_d = fetch()
        normed_a, scale_a = normalize(x_local, gains[0])
        attn_in = gather_forward(normed_a.astype(jnp.bfloat16))
        projected = jnp.einsum("td,dkf->tkf", attn_in, w_a, preferred_element_type=jnp.float32)
        tree_len = projected.shape[0]
        groups = projected.shape[1]
        queries = rotate(
            projected[:, :, : GROUP * HD].reshape(tree_len, groups, GROUP, HD),
            cosines[:, None, None, :],
            sines[:, None, None, :],
        ).astype(jnp.bfloat16)
        key_heads = rotate(
            projected[:, :, GROUP * HD : (GROUP + 1) * HD], cosines[:, None, :], sines[:, None, :]
        ).astype(jnp.bfloat16)
        values = projected[:, :, (GROUP + 1) * HD :].astype(jnp.bfloat16)
        scores = jnp.einsum(
            "tkgh,skh->kgts", queries, key_heads, preferred_element_type=jnp.float32
        )
        logits = jnp.where(allowed, score_mult * scores, masked_value)
        row_peak = jnp.max(logits, axis=-1, keepdims=True)
        exp_terms = jnp.exp(logits - row_peak)
        exp_total = jnp.sum(exp_terms, axis=-1, keepdims=True)
        log_total = row_peak + jnp.log(exp_total)
        attn_probs = exp_terms / exp_total
        mixed_heads = (
            jnp.einsum(
                "kgts,skh->tkgh",
                attn_probs.astype(jnp.bfloat16),
                values,
                preferred_element_type=jnp.float32,
            )
            .astype(jnp.bfloat16)
            .reshape(tree_len, -1)
        )

        def out_terms(first_row, row_total):
            return jnp.dot(mixed_heads, w_b, preferred_element_type=jnp.float32)

        attn_sum = sum_forward(out_terms, row_count)
        residual_mid = x_local + residual_mult * attn_sum
        normed_b, scale_b = normalize(residual_mid, gains[1])
        ffn_in = gather_forward(normed_b.astype(jnp.bfloat16))
        gate_up = jnp.einsum("td,edf->tef", ffn_in, w_c, preferred_element_type=jnp.float32)
        gate_act = jax.nn.sigmoid(gate_up[:, 0])
        silu_gate = gate_up[:, 0] * gate_act
        hidden = (silu_gate * gate_up[:, 1]).astype(jnp.bfloat16)

        def down_terms(first_row, row_total):
            return jnp.dot(hidden, w_d, preferred_element_type=jnp.float32)

        mlp_sum = sum_forward(down_terms, row_count)
        outputs.append((residual_mid + residual_mult * mlp_sum).astype(jnp.bfloat16))
        w_a, w_b, w_c, w_d = fetch()
        cot_full = gather_backward(cotangent[batch_index])
        hidden_grad = residual_mult * jnp.einsum(
            "td,fd->tf", cot_full, w_d, preferred_element_type=jnp.float32
        )
        down_grad = residual_mult * jnp.einsum(
            "tf,td->fd", hidden, cot_full, preferred_element_type=jnp.float32
        )
        gate_grad = (
            hidden_grad * gate_up[:, 1] * gate_act * (1.0 + gate_up[:, 0] * (1.0 - gate_act))
        )
        up_grad = hidden_grad * silu_gate
        gate_up_grad = jnp.stack([gate_grad, up_grad], axis=1).astype(jnp.bfloat16)
        gu_grad = jnp.einsum(
            "td,tef->edf", ffn_in, gate_up_grad, preferred_element_type=jnp.float32
        )

        def ffn_back_terms(first_row, row_total):
            return jnp.einsum("tef,edf->td", gate_up_grad, w_c, preferred_element_type=jnp.float32)

        ffn_in_grad = sum_backward(ffn_back_terms, row_count)
        mid_norm_grad, gain_b_grad = norm_back(residual_mid, scale_b, gains[1], ffn_in_grad)
        mid_grad = cotangent[batch_index].astype(jnp.float32) + mid_norm_grad
        attn_out_grad = gather_backward((residual_mult * mid_grad).astype(jnp.bfloat16))
        out_grad = jnp.einsum(
            "tf,td->fd", mixed_heads, attn_out_grad, preferred_element_type=jnp.float32
        )
        heads_grad = (
            jnp.einsum("td,fd->tf", attn_out_grad, w_b, preferred_element_type=jnp.float32)
            .astype(jnp.bfloat16)
            .reshape(tree_len, groups, GROUP, HD)
        )
        attn_probs = jnp.exp(logits - log_total)
        prob_grad = jnp.einsum(
            "tkgh,skh->kgts", heads_grad, values, preferred_element_type=jnp.float32
        )
        row_inner = jnp.sum(prob_grad * attn_probs, axis=-1, keepdims=True)
        score_grad = (score_mult * attn_probs * (prob_grad - row_inner)).astype(jnp.bfloat16)
        query_grad = jnp.einsum(
            "kgts,skh->tkgh", score_grad, key_heads, preferred_element_type=jnp.float32
        )
        key_grad = jnp.einsum(
            "kgts,tkgh->skh", score_grad, queries, preferred_element_type=jnp.float32
        )
        value_grad = jnp.einsum(
            "kgts,tkgh->skh",
            attn_probs.astype(jnp.bfloat16),
            heads_grad,
            preferred_element_type=jnp.float32,
        )
        query_grad = rotate(query_grad, cosines[:, None, None, :], -sines[:, None, None, :])
        key_grad = rotate(key_grad, cosines[:, None, :], -sines[:, None, :])
        proj_grad = jnp.concatenate(
            [query_grad.reshape(tree_len, groups, GROUP * HD), key_grad, value_grad], axis=-1
        ).astype(jnp.bfloat16)
        qkv_grad = jnp.einsum("td,tkf->dkf", attn_in, proj_grad, preferred_element_type=jnp.float32)

        def attn_back_terms(first_row, row_total):
            return jnp.einsum("tkf,dkf->td", proj_grad, w_a, preferred_element_type=jnp.float32)

        attn_in_grad = sum_backward(attn_back_terms, row_count)
        input_norm_grad, gain_a_grad = norm_back(x_local, scale_a, gains[0], attn_in_grad)
        input_grads.append(mid_grad + input_norm_grad)
        gain_step = jnp.stack([gain_a_grad, gain_b_grad])
        gain_partial = gain_step if gain_partial is None else gain_partial + gain_step
        partials = (qkv_grad, out_grad, gu_grad, down_grad)
        unsummed = (
            partials
            if unsummed is None
            else tuple((running + addend for running, addend in zip(unsummed, partials)))
        )
    owned = (
        lax.psum_scatter(
            unsummed[0].astype(jnp.bfloat16), "row", scatter_dimension=0, tiled=True
        ).astype(jnp.float32),
        lax.psum_scatter(
            unsummed[1].astype(jnp.bfloat16), "row", scatter_dimension=1, tiled=True
        ).astype(jnp.float32),
        lax.psum_scatter(
            unsummed[2].astype(jnp.bfloat16), "row", scatter_dimension=1, tiled=True
        ).astype(jnp.float32),
        lax.psum_scatter(
            unsummed[3].astype(jnp.bfloat16), "row", scatter_dimension=1, tiled=True
        ).astype(jnp.float32),
    )
    local_squares = jnp.float32(0.0)
    for grad_piece in owned:
        local_squares = local_squares + jnp.sum(grad_piece * grad_piece)
    total_squares, gain_total = lax.psum((local_squares, gain_partial), ("row", "col"))
    grad_norm = jnp.sqrt(total_squares + jnp.sum(gain_total * gain_total))
    factor = jnp.minimum(1.0, clip_bound() / (grad_norm + 1e-06))
    rates = step_rates()
    masters = (w_qkv, w_out, w_gu, w_down)
    states = (mom_qkv, mom_out, mom_gu, mom_down)
    results = []
    for index_w in range(4):
        updated, moments = adamw(
            masters[index_w], states[index_w], owned[index_w], factor, rates[index_w]
        )
        results.append((updated, moments, updated.astype(jnp.bfloat16)))
    new_gains, moments_gains = adamw(gains, mom_gains, gain_total, factor, rates[4])
    mixed = jnp.stack(outputs, axis=0)
    d_tokens = jnp.stack(input_grads, axis=0)
    return (
        mixed,
        d_tokens,
        grad_norm,
        results[0][0],
        results[0][1],
        results[0][2],
        results[1][0],
        results[1][1],
        results[1][2],
        results[2][0],
        results[2][1],
        results[2][2],
        results[3][0],
        results[3][1],
        results[3][2],
        new_gains,
        moments_gains,
    )


def position_tables(segments, parents):
    seg_ids = jnp.arange(1 + NBRANCH + NLEAF, dtype=jnp.int32)
    member = (segments[:, None] == seg_ids[None, :]).astype(jnp.int32)
    seg_lengths = jnp.sum(member, axis=0)
    seg_starts = jnp.cumsum(seg_lengths) - seg_lengths
    parent_of = jnp.concatenate([jnp.full((1 + NBRANCH,), -1, jnp.int32), 1 + parents])
    branch_ids = jnp.arange(NBRANCH, dtype=jnp.int32)
    parent_pick = (parents[:, None] == branch_ids[None, :]).astype(jnp.int32)
    parent_len = jnp.sum(parent_pick * seg_lengths[1 : 1 + NBRANCH][None, :], axis=1)
    base_depth = jnp.concatenate(
        [
            jnp.zeros((1,), jnp.int32),
            seg_lengths[0] * jnp.ones((NBRANCH,), jnp.int32),
            seg_lengths[0] + parent_len,
        ]
    )
    places = jnp.arange(segments.shape[0], dtype=jnp.int32)
    depth = places + jnp.sum(member * (base_depth - seg_starts)[None, :], axis=1)
    parent = jnp.sum(member * parent_of[None, :], axis=1)
    freqs = jnp.exp(jnp.arange(HD // 2, dtype=jnp.float32) * (-2.0 * math.log(rope_theta) / HD))
    angles = depth.astype(jnp.float32)[:, None] * freqs[None, :]
    cosines, sines = jnp.cos(angles), jnp.sin(angles)
    return (
        jnp.concatenate([cosines] * 4, axis=1),
        jnp.concatenate([-sines, sines] * 2, axis=1),
        jnp.broadcast_to(segments[:, None].astype(jnp.float32), (segments.shape[0], 128)),
        jnp.broadcast_to(parent[:, None].astype(jnp.float32), (segments.shape[0], 128)),
        jnp.broadcast_to(segments[None, :].astype(jnp.float32), (8, segments.shape[0])),
    )

def dot_nn(a, b):
    return lax.dot_general(a, b, (((1,), (0,)), ((), ())), preferred_element_type=jnp.float32)


def dot_nt(a, b):
    return lax.dot_general(a, b, (((1,), (1,)), ((), ())), preferred_element_type=jnp.float32)


def dot_tn(a, b):
    return lax.dot_general(a, b, (((0,), (0,)), ((), ())), preferred_element_type=jnp.float32)


MICRO = 2
TREE = 1024
OWN = 256
WIDE = 2048
NX, NC, NZ, NY = 2, 2, 4, 2
SEG = 128
MESH = pl.DeviceIdType.MESH
HBM = pl.BlockSpec(memory_space=pl.ANY)


class Place:
    def __init__(self):
        row, col = lax.axis_index("row"), lax.axis_index("col")
        self.row, self.col = row, col
        self.z, self.y = row // NY, row % NY
        self.x, self.c = col // NC, col % NC
        self.own = col
        self.row_z = [lax.rem(row + NY * off, NZ * NY) for off in range(NZ)]
        self.row_y = self.z * NY + (1 - self.y)
        self.row_yz = [lax.rem(self.z + off, NZ) * NY + (1 - self.y) for off in range(NZ)]
        self.col_x = (1 - self.x) * NC + self.c
        self.col_c = self.x * NC + (1 - self.c)
        self.col_xc = (1 - self.x) * NC + (1 - self.c)
        self.at_z = [None] + [(self.row_z[off], col) for off in range(1, NZ)]
        self.at_up = (lax.rem(row + NY, NZ * NY), col)
        self.at_down = (lax.rem(row + (NZ - 1) * NY, NZ * NY), col)
        self.at_y = (self.row_y, col)
        self.at_x = (row, self.col_x)
        self.at_c = (row, self.col_c)

    def greet(self):
        barrier = pltpu.get_barrier_semaphore()
        partners = self.at_z[1:] + [self.at_y, self.at_x, self.at_c]
        for partner in partners:
            pl.semaphore_signal(barrier, inc=1, device_id=partner, device_id_type=MESH)
        pl.semaphore_wait(barrier, len(partners))


class Copies:
    def __init__(self):
        self.open_sends = []

    def send(self, src, dst, send_sem, recv_sem, device, when=True):
        copy = pltpu.make_async_remote_copy(
            src_ref=src, dst_ref=dst, send_sem=send_sem, recv_sem=recv_sem,
            device_id=device, device_id_type=MESH,
        )
        if when is True:
            copy.start()
        else:
            pl.when(when)(copy.start)
        self.open_sends.append((copy, when))
        return copy

    def arrive(self, dst, send_sem, recv_sem, device, when=True):
        copy = pltpu.make_async_remote_copy(
            src_ref=dst, dst_ref=dst, send_sem=send_sem, recv_sem=recv_sem,
            device_id=device, device_id_type=MESH,
        )
        if when is True:
            copy.wait_recv()
        else:
            pl.when(when)(copy.wait_recv)

    def local(self, src, dst, sem):
        copy = pltpu.make_async_copy(src, dst, sem)
        copy.start()
        return copy

    def close(self, some=None):
        left = []
        for copy, when in self.open_sends:
            if some is not None and not any(copy is one for one in some):
                left.append((copy, when))
            elif when is True:
                copy.wait_send()
            else:
                pl.when(when)(copy.wait_send)
        self.open_sends = left


def rows_of(index, size):
    return pl.ds(pl.multiple_of(index * size, size), size)


class WeightGather:
    def __init__(self, place, copies, own, full, view, send, recv, keep, over_y_first):
        self.place, self.copies, self.own, self.full, self.view = place, copies, own, full, view
        self.send, self.recv, self.keep = send, recv, keep
        self.sides = (place.y, 1 - place.y) if over_y_first else (place.y,)
        self.over_y_first = over_y_first

    def block(self, r):
        return self.view(self.full, r)

    def pass_on(self, src, r, up, down, over_y):
        p = self.place
        here = self.block(r)
        if up is not None:
            self.copies.send(src, here, self.send.at[0, r], self.recv.at[r], p.at_up, up)
        if down is not None:
            self.copies.send(src, here, self.send.at[1, r], self.recv.at[r], p.at_down, down)
        if over_y is not None:
            self.copies.send(src, here, self.send.at[2, r], self.recv.at[r], p.at_y, over_y)

    def start_y(self):
        p = self.place
        self.kept = self.copies.local(self.own, self.block(p.row), self.keep)
        self.pass_on(self.own, p.row, None, None, True)

    def start_z(self):
        p = self.place
        self.pass_on(self.own, p.row, p.z < NZ - 1, p.z > 0, None)

    def arrive(self, r, when=True):
        self.copies.arrive(self.block(r), self.send.at[2, r], self.recv.at[r], self.place.at_y, when)

    def relay_y(self):
        p = self.place
        self.arrive(p.row_y)
        self.pass_on(self.block(p.row_y), p.row_y, p.z < NZ - 1, p.z > 0, None)

    def relay(self, k):
        p = self.place
        for there, upward in ((p.z - k, True), (p.z + k, False)):
            came = there >= 0 if upward else there < NZ
            safe = lax.rem(there + NZ, NZ)
            for side in self.sides:
                r = safe * NY + side
                self.arrive(r, came)
                on = jnp.logical_and(came, p.z < NZ - 1) if upward else jnp.logical_and(came, p.z > 0)
                self.pass_on(
                    self.block(r), r, on if upward else None, None if upward else on, None if self.over_y_first else came
                )

    def finish(self):
        if not self.over_y_first:
            for off in range(NZ):
                self.arrive(self.place.row_yz[off])
        if self.kept is not None:
            self.keep_own()

    def keep_own(self):
        self.kept.wait()
        self.kept = None


class TokenGather:
    def __init__(self, place, copies, full, base, send, recv):
        self.place, self.copies, self.full, self.base = place, copies, full, base
        self.send, self.recv = send, recv

    def block(self, index):
        return self.full.at[pl.ds(pl.multiple_of(self.base + index * OWN, OWN), OWN), :]

    def start(self, own, keep):
        p = self.place
        here = self.block(p.own)
        self.kept = self.copies.local(own, here, keep)
        self.copies.send(own, here, self.send.at[0], self.recv.at[p.own], p.at_x)
        self.copies.send(own, here, self.send.at[1], self.recv.at[p.own], p.at_c)

    def relay(self):
        p = self.place
        block = self.block(p.col_x)
        self.copies.arrive(block, self.send.at[2], self.recv.at[p.col_x], p.at_c)
        self.copies.send(block, block, self.send.at[2], self.recv.at[p.col_x], p.at_c)

    def finish(self):
        p = self.place
        for index in (p.col_c, p.col_xc):
            self.copies.arrive(self.block(index), self.send.at[2], self.recv.at[index], p.at_c)
        self.kept.wait()


class TokenSum:
    def __init__(self, place, copies, blocks, away, mine, from_core, from_x, send, recv):
        self.place, self.copies, self.blocks, self.away, self.mine = place, copies, blocks, away, mine
        self.from_core, self.from_x, self.send, self.recv = from_core, from_x, send, recv

    def start(self):
        p = self.place
        self.sent = []
        for there in range(NX):
            self.sent.append(
                self.copies.send(
                    self.blocks(there * NC + (1 - p.c)), self.from_core.at[there],
                    self.send.at[there], self.recv.at[there], p.at_c,
                )
            )

    def middle(self):
        p = self.place
        for there in range(NX):
            self.copies.arrive(self.from_core.at[there], self.send.at[there], self.recv.at[there], p.at_c)
        other = 1 - p.x

        @pl.loop(0, OWN // 32)
        def _(i):
            rows = rows_of(i, 32)
            self.away[rows, :] = (
                self.away[rows, :].astype(jnp.float32) + self.from_core[other, rows, :].astype(jnp.float32)
            ).astype(jnp.bfloat16)

        self.sent.append(self.copies.send(self.away, self.from_x, self.send.at[2], self.recv.at[2], p.at_x))

    def arrive(self):
        p = self.place
        self.copies.arrive(self.from_x, self.send.at[2], self.recv.at[2], p.at_x)

    def rows(self, rows):
        p = self.place
        return (
            self.mine[rows, :].astype(jnp.float32)
            + self.from_core[p.x, rows, :].astype(jnp.float32)
            + self.from_x[rows, :].astype(jnp.float32)
        )


def swap_halves(tile):
    lane = lax.broadcasted_iota(jnp.int32, tile.shape, 1)
    return jnp.where(lane % HD < HD // 2, pltpu.roll(tile, 128 - HD // 2, 1), pltpu.roll(tile, HD // 2, 1))


def masked_parts(run, seg_col, parent_col, seg_row):
    rows = slice(run * SEG, (run + 1) * SEG)

    def causal():
        shape = (SEG, 2 * SEG)
        return lax.broadcasted_iota(jnp.int32, shape, 1) <= lax.broadcasted_iota(jnp.int32, shape, 0) + run * SEG

    def of_parent():
        return seg_row[0:1, 2 * SEG : 4 * SEG] == parent_col[rows, 0:1]

    def of_run():
        shape = (SEG, SEG)
        order = lax.broadcasted_iota(jnp.int32, shape, 1) <= lax.broadcasted_iota(jnp.int32, shape, 0)
        return order & (seg_row[0:1, rows] == seg_col[rows, 0:1])

    if run < 2:
        return [(slice(0, 2 * SEG), causal())]
    parts = [(slice(0, 2 * SEG), None)]
    if run >= 4:
        parts.append((slice(2 * SEG, 4 * SEG), of_parent()))
    parts.append((rows, of_run()))
    return parts


def softmax_parts(scores):
    peak = None
    for score in scores:
        top = jnp.max(score, axis=-1, keepdims=True)
        peak = top if peak is None else jnp.maximum(peak, top)
    peak = peak * score_mult
    exps = [jnp.exp(score * score_mult - peak) for score in scores]
    total = None
    for term in exps:
        part = jnp.sum(term, axis=-1, keepdims=True)
        total = part if total is None else total + part
    return exps, total, peak + jnp.log(total)


def stacked_pairs(tile_ref, rows):
    both = jnp.concatenate([tile_ref[rows, 0:128], tile_ref[rows, 128:256]], axis=0)
    lane = lax.broadcasted_iota(jnp.int32, both.shape, 1)
    zero = jnp.zeros_like(both)
    return jnp.concatenate([jnp.where(lane < HD, both, zero), jnp.where(lane < HD, zero, both)], axis=0)


def unstack_pairs(wide):
    half = wide.shape[0] // 2
    lane = lax.broadcasted_iota(jnp.int32, (half, 128), 1)
    return jnp.where(lane < HD, wide[:half], wide[half:])


def twice(kv):
    wide = kv.astype(jnp.float32)
    lane = lax.broadcasted_iota(jnp.int32, wide.shape, 1)
    other = pltpu.roll(wide, HD, 1)
    key = jnp.where(lane < HD, wide, other)
    value = jnp.where(lane < HD, other, wide)
    return key.astype(jnp.bfloat16), value.astype(jnp.bfloat16)


def score_parts(queries, keys, parts):
    scores = []
    for span, mask in parts:
        score = dot_nt(queries, keys[span])
        if mask is not None:
            score = jnp.where(jnp.concatenate([mask] * 4, axis=0), score, masked_value)
        scores.append(score)
    return scores


def attend(qkv_ref, seg_col_ref, parent_col_ref, seg_row_ref, heads_ref, log_ref):
    seg_row = seg_row_ref[...]
    keys, values = twice(qkv_ref[:, 256:384])
    for run in range(TREE // SEG):
        rows = slice(run * SEG, (run + 1) * SEG)
        parts = masked_parts(run, seg_col_ref, parent_col_ref, seg_row)
        exps, total, log_total = softmax_parts(score_parts(stacked_pairs(qkv_ref, rows), keys, parts))
        mixed = None
        for (span, _), term in zip(parts, exps):
            got = dot_nn(term.astype(jnp.bfloat16), values[span])
            mixed = got if mixed is None else mixed + got
        low = unstack_pairs(mixed * (1.0 / total)).astype(jnp.bfloat16)
        heads_ref[rows, 0:128] = low[0:SEG]
        heads_ref[rows, 128:256] = low[SEG:]
        log_ref[run * 4 * SEG : (run + 1) * 4 * SEG, :] = jnp.broadcast_to(log_total, (4 * SEG, 128))


def attend_back(
    key_sum, value_sum, grad_buf, back_ref, w_ref, heads_ref, log_ref, qkv_ref, cos_ref, sin_ref, seg_col_ref,
    parent_col_ref, seg_row_ref, out_ref,
):
    for part in range(TREE // OWN):
        rows = slice(part * OWN, (part + 1) * OWN)
        grad_buf[rows, :] = dot_nt(back_ref[rows, :], w_ref[...]).astype(jnp.bfloat16)
    seg_row = seg_row_ref[...]
    keys, values = twice(qkv_ref[:, 256:384])
    key_sum[...] = jnp.zeros_like(key_sum)
    value_sum[...] = jnp.zeros_like(value_sum)
    for run in range(TREE // SEG):
        rows = slice(run * SEG, (run + 1) * SEG)
        parts = masked_parts(run, seg_col_ref, parent_col_ref, seg_row)
        queries = stacked_pairs(qkv_ref, rows)
        upstream = stacked_pairs(grad_buf, rows)
        mixed = stacked_pairs(heads_ref, rows)
        inner = jnp.sum(upstream.astype(jnp.float32) * mixed.astype(jnp.float32), axis=-1, keepdims=True)
        log_total = log_ref[run * 4 * SEG : (run + 1) * 4 * SEG, 0:1]
        query_grad = None
        for (span, _), score in zip(parts, score_parts(queries, keys, parts)):
            prob = jnp.exp(score * score_mult - log_total)
            prob_grad = dot_nt(upstream, values[span])
            score_grad = (prob * (prob_grad - inner)).astype(jnp.bfloat16)
            term = dot_nn(score_grad, keys[span])
            query_grad = term if query_grad is None else query_grad + term
            key_sum[span, :] += dot_tn(score_grad, queries)
            value_sum[span, :] += dot_tn(prob.astype(jnp.bfloat16), upstream)
        pair_grad = unstack_pairs(query_grad) * score_mult
        cos, sin = cos_ref[rows, :], sin_ref[rows, :]
        for tile in range(2):
            part = pair_grad[tile * SEG : (tile + 1) * SEG]
            out_ref[rows, tile * 128 : (tile + 1) * 128] = (part * cos - swap_halves(part) * sin).astype(jnp.bfloat16)
    key_grad = key_sum[...] * score_mult
    key_grad = key_grad + pltpu.roll(key_grad, HD, 1)
    value_grad = value_sum[...]
    value_grad = value_grad + pltpu.roll(value_grad, HD, 1)
    turned = key_grad * cos_ref[...] - swap_halves(key_grad) * sin_ref[...]
    lane = lax.broadcasted_iota(jnp.int32, turned.shape, 1)
    out_ref[:, 256:384] = jnp.where(lane < HD, turned, value_grad).astype(jnp.bfloat16)


def forward_kernel(
    tokens, cot, own_qkv, own_out, own_gu, own_down, gain, cosines, sines, seg_col, parent_col, seg_row,
    w_qkv, w_out, w_gu, w_down, attn_in, cot_full, ffn_in, qkv, heads, log_sums, resid, gate, up, hidden, down_grad,
    down_out,
    partial, from_core, from_x, normed_buf, tokens_buf, cot_buf, near_buf, gain_buf,
    wide_qkv, wide_out, wide_gu, wide_down, low_qkv, low_out, low_gu, low_down,
    w_send, w_recv, w_keep, t_send, t_recv, t_keep, s_send, s_recv, l_sem,
):
    resid_buf = wide_gu
    place = Place()
    copies = Copies()
    pairs = (
        (own_qkv, wide_qkv), (tokens, tokens_buf), (gain, gain_buf), (own_out, wide_out),
        (own_gu, wide_gu), (cot, cot_buf), (own_down, wide_down),
    )
    loads = [copies.local(src, dst, l_sem.at[i]) for i, (src, dst) in enumerate(pairs)]
    place.greet()

    def row_block(full, r):
        return full.at[rows_of(r, OWN), :]

    def col_block(full, r):
        return full.at[:, rows_of(r, OWN)]

    def weight(index, own, full, view, over_y_first):
        return WeightGather(
            place, copies, own, full, view, w_send.at[index], w_recv.at[index], w_keep.at[index], over_y_first
        )

    g_qkv = weight(0, low_qkv, w_qkv, row_block, True)
    g_out = weight(1, low_out, w_out, col_block, True)
    g_gate = weight(2, low_gu.at[0], w_gu.at[0], row_block, False)
    g_up = weight(3, low_gu.at[1], w_gu.at[1], row_block, False)
    g_down = weight(4, low_down, w_down, col_block, False)

    def token_gather(index, full, m):
        return TokenGather(place, copies, full, m * TREE, t_send.at[index], t_recv.at[index])

    a_in = [token_gather(m, attn_in, m) for m in range(MICRO)]
    a_cot = [token_gather(2 + m, cot_full, m) for m in range(MICRO)]
    a_ffn = [token_gather(4 + m, ffn_in, m) for m in range(MICRO)]
    sums = [
        TokenSum(
            place, copies, functools.partial(lambda m, i: partial.at[m, i], m), partial.at[m, place.col_x],
            partial.at[m, place.own], from_core.at[m], from_x.at[m], s_send.at[m], s_recv.at[m],
        )
        for m in range(MICRO)
    ]

    def project(m):
        def body(a_ref, w_ref, cos_ref, sin_ref, out_ref):
            got = dot_nn(a_ref[...], w_ref[...])
            cos, sin = cos_ref[...], sin_ref[...]
            lane = lax.broadcasted_iota(jnp.int32, cos.shape, 1)
            cos_key = jnp.where(lane < HD, cos, 1.0)
            sin_key = jnp.where(lane < HD, sin, 0.0)
            for tile in range(got.shape[1] // 128):
                part = got[:, tile * 128 : (tile + 1) * 128]
                is_key = tile % 3 == 2
                turned = part * (cos_key if is_key else cos) + swap_halves(part) * (sin_key if is_key else sin)
                out_ref[:, tile * 128 : (tile + 1) * 128] = turned.astype(jnp.bfloat16)

        steps = TREE // OWN
        rows = pl.BlockSpec((OWN, D), lambda i: (m * steps + i, 0))
        table = pl.BlockSpec((OWN, 128), lambda i: (m * steps + i, 0))
        out = pl.BlockSpec((OWN, 768), lambda i: (m * steps + i, 0))
        whole = pl.BlockSpec((D, 768), lambda i: (0, 0))
        pltpu.emit_pipeline(body, grid=(steps,), in_specs=[rows, whole, table, table], out_specs=[out])(
            attn_in, w_qkv, cosines, sines, qkv
        )

    def attention(m):
        tree = pl.BlockSpec((TREE, 128), lambda g: (m, 0))
        pltpu.emit_pipeline(
            attend,
            grid=(2,),
            in_specs=[
                pl.BlockSpec((TREE, 384), lambda g: (m, g)),
                tree,
                tree,
                pl.BlockSpec((8, TREE), lambda g: (m, 0)),
            ],
            out_specs=[
                pl.BlockSpec((TREE, 256), lambda g: (m, g)),
                pl.BlockSpec((4 * TREE, 128), lambda g: (m * 2 + g, 0)),
            ],
        )(qkv, seg_col, parent_col, seg_row, heads, log_sums)

    def out_project(m):
        def body_at(step, a_ref, w_ref):
            partial[m, step.index[0]] = dot_nn(a_ref[...], w_ref[...]).astype(jnp.bfloat16)

        steps = TREE // OWN
        pltpu.emit_pipeline(
            body_at,
            grid=(steps,),
            in_specs=[
                pl.BlockSpec((OWN, 512), lambda i: (m * steps + i, 0)),
                pl.BlockSpec((512, D), lambda i: (0, 0)),
            ],
            out_specs=[],
            _explicit_indices=True,
        )(heads, w_out)

    def lower(wide, low):
        step = 64

        @pl.loop(0, wide.shape[0] // step)
        def _(i):
            rows = rows_of(i, step)
            low[rows, :] = wide[rows, :].astype(jnp.bfloat16)

    def first_norm(m):
        @pl.loop(0, OWN // 32)
        def _(i):
            rows = rows_of(i, 32)
            value = tokens_buf[m, rows, :].astype(jnp.float32)
            scale = lax.rsqrt(jnp.mean(value * value, axis=-1, keepdims=True) + norm_eps)
            near_buf[m, rows, :] = (value * scale * gain_buf[0:1, :]).astype(jnp.bfloat16)

        a_in[m].start(near_buf.at[m], t_keep.at[m])

    def middle_norm(m):
        sums[m].arrive()

        @pl.loop(0, OWN // 32)
        def _(i):
            rows = rows_of(i, 32)
            value = tokens_buf[m, rows, :].astype(jnp.float32) + residual_mult * sums[m].rows(rows)
            resid_buf[m, rows, :] = value
            scale = lax.rsqrt(jnp.mean(value * value, axis=-1, keepdims=True) + norm_eps)
            normed_buf[m, rows, :] = (value * scale * gain_buf[1:2, :]).astype(jnp.bfloat16)

        a_ffn[m].start(normed_buf.at[m], t_keep.at[4 + m])
        return copies.local(resid_buf.at[m], resid.at[m], l_sem.at[m])

    def gate_up(m):
        def body(a_ref, g_ref, u_ref, gate_ref, up_ref, hidden_ref):
            for part in range(TREE // OWN):
                rows = slice(part * OWN, (part + 1) * OWN)
                value = a_ref[rows, :]
                g = dot_nn(value, g_ref[0])
                u = dot_nn(value, u_ref[0])
                act = jax.nn.sigmoid(g)
                silu = g * act
                gate_ref[rows, :] = (u * act * (1.0 + g * (1.0 - act))).astype(jnp.bfloat16)
                up_ref[rows, :] = silu.astype(jnp.bfloat16)
                hidden_ref[rows, :] = (silu * u).astype(jnp.bfloat16)

        cols = pl.BlockSpec((TREE, 256), lambda j: (m, j))
        pltpu.emit_pipeline(
            body,
            grid=(WIDE // 256,),
            in_specs=[
                pl.BlockSpec((TREE, D), lambda j: (m, 0)),
                pl.BlockSpec((1, D, 256), lambda j: (0, 0, j)),
                pl.BlockSpec((1, D, 256), lambda j: (1, 0, j)),
            ],
            out_specs=[cols, cols, cols],
        )(ffn_in, w_gu, w_gu, gate, up, hidden)

    def grad_down():
        def body(h_ref, c_ref, out_ref):
            out_ref[...] = (residual_mult * dot_tn(h_ref[...], c_ref[...])).astype(jnp.bfloat16)

        pltpu.emit_pipeline(
            body,
            grid=(WIDE // 256,),
            in_specs=[
                pl.BlockSpec((MICRO * TREE, 256), lambda i: (0, i)),
                pl.BlockSpec((MICRO * TREE, D), lambda i: (0, 0)),
            ],
            out_specs=[pl.BlockSpec((256, D), lambda i: (i, 0))],
        )(hidden, cot_full, down_grad)

    def down(m, near):
        def body(h_ref, w_ref, out_ref):
            for part in range(TREE // OWN):
                rows = slice(part * OWN, (part + 1) * OWN)
                out_ref[rows, :] = dot_nn(h_ref[rows, :], w_ref[...]).astype(jnp.bfloat16)

        side = place.y if near else 1 - place.y
        pltpu.emit_pipeline(
            body,
            grid=(NZ,),
            in_specs=[
                pl.BlockSpec((TREE, WIDE), lambda j: (m, 0)),
                pl.BlockSpec((WIDE, OWN), lambda j: (0, j * NY + side)),
            ],
            out_specs=[pl.BlockSpec((TREE, OWN), lambda j: (m, j * NY + side))],
        )(hidden, w_down, down_out)

    g_qkv_load, tokens_load, gain_load, out_load, gu_load, cot_load, down_load = loads
    g_qkv_load.wait()
    lower(wide_qkv, low_qkv)
    g_qkv.start_y()
    g_qkv.start_z()
    out_load.wait()
    lower(wide_out, low_out)
    g_out.start_y()
    g_out.start_z()
    tokens_load.wait()
    gain_load.wait()
    for m in range(MICRO):
        first_norm(m)
    gu_load.wait()
    lower(wide_gu.at[0], low_gu.at[0])
    g_gate.start_y()
    g_qkv.relay_y()
    g_out.relay_y()
    lower(wide_gu.at[1], low_gu.at[1])
    g_up.start_y()
    cot_load.wait()
    for m in range(MICRO):
        a_cot[m].start(cot_buf.at[m], t_keep.at[2 + m])
    down_load.wait()
    lower(wide_down, low_down)
    g_down.start_y()
    a_in[0].relay()
    g_qkv.relay(1)
    g_out.relay(1)
    a_in[1].relay()
    g_qkv.relay(2)
    g_out.relay(2)
    g_gate.start_z()
    a_in[0].finish()
    a_in[1].finish()
    a_cot[0].relay()
    g_qkv.relay(3)
    g_qkv.finish()
    project(0)
    g_out.relay(3)
    g_out.finish()
    g_gate.relay(1)
    project(1)
    a_cot[1].relay()
    attention(0)
    g_gate.relay(2)
    g_up.start_z()
    out_project(0)
    sums[0].start()
    attention(1)
    sums[0].middle()
    out_project(1)
    sums[1].start()
    g_gate.relay(3)
    sums[1].middle()
    stored = [middle_norm(0)]
    g_up.relay(1)
    stored.append(middle_norm(1))
    a_ffn[0].relay()
    g_up.relay(2)
    g_down.start_z()
    a_ffn[1].relay()
    g_up.relay(3)
    g_down.relay(1)
    a_cot[0].finish()
    a_cot[1].finish()
    a_ffn[0].finish()
    g_gate.finish()
    g_up.finish()
    gate_up(0)
    g_down.relay(2)
    a_ffn[1].finish()
    gate_up(1)
    g_down.relay(3)
    g_down.keep_own()
    down(0, True)
    down(1, True)
    grad_down()
    g_down.finish()
    down(0, False)
    down(1, False)
    for copy in stored:
        copy.wait()
    copies.close()


def forward(tokens, cot, w_qkv, w_out, w_gu, w_down, gains, tables):
    low = jnp.bfloat16
    wide = jnp.float32
    shape = jax.ShapeDtypeStruct
    all_tokens = MICRO * TREE
    outs = [
        shape((D, 768), low), shape((512, D), low), shape((2, D, WIDE), low), shape((WIDE, D), low),
        shape((all_tokens, D), low), shape((all_tokens, D), low), shape((all_tokens, D), low),
        shape((all_tokens, 768), low), shape((all_tokens, 512), low), shape((2 * MICRO * 4 * TREE, 128), wide),
        shape((MICRO, OWN, D), wide),
        shape((all_tokens, WIDE), low), shape((all_tokens, WIDE), low), shape((all_tokens, WIDE), low),
        shape((WIDE, D), low), shape((all_tokens, D), low),
    ]
    dma = pltpu.SemaphoreType.DMA
    blocks = [(OWN, 768), (512, OWN), (2, OWN, WIDE), (WIDE, OWN)]
    scratch = [
        pltpu.VMEM((MICRO, NX * NC, OWN, D), low),
        pltpu.VMEM((MICRO, NX, OWN, D), low),
        pltpu.VMEM((MICRO, OWN, D), low),
        pltpu.VMEM((MICRO, OWN, D), low),
        pltpu.VMEM((MICRO, OWN, D), low),
        pltpu.VMEM((MICRO, OWN, D), low),
        pltpu.VMEM((MICRO, OWN, D), low),
        pltpu.VMEM((2, D), wide),
    ]
    scratch += [pltpu.VMEM(block, wide) for block in blocks]
    scratch += [pltpu.VMEM(block, low) for block in blocks]
    scratch += [
        dma((5, 3, NZ * NY)), dma((5, NZ * NY)), dma((5,)),
        dma((6, 3)), dma((6, NX * NC)), dma((6,)),
        dma((MICRO, 3)), dma((MICRO, 3)), dma((7,)),
    ]
    return pl.pallas_call(
        forward_kernel,
        out_shape=outs,
        in_specs=[HBM] * 12,
        out_specs=[HBM] * len(outs),
        scratch_shapes=scratch,
        compiler_params=pltpu.CompilerParams(
            collective_id=0, has_side_effects=True, vmem_limit_bytes=63 * 1024 * 1024
        ),
        cost_estimate=pl.CostEstimate(flops=90 * 10**9, bytes_accessed=2 * 10**8, transcendentals=10**7),
        name="forward",
    )(tokens, cot, w_qkv.reshape(OWN, 768), w_out, w_gu, w_down, gains, *tables)


class GradSum:
    ORDER = (2, 1, 3)

    def __init__(self, place, copies, full, view, from_y, from_z, owned, squares, sems):
        self.place, self.copies, self.full, self.view = place, copies, full, view
        self.from_y, self.from_z, self.owned = from_y, from_z, owned
        self.squares = squares
        self.y_send, self.y_recv, self.z_send, self.z_recv = sems
        rows, cols = owned.shape
        step = max(16, min(rows, (256 * 1024) // cols))
        self.grid = rows // step
        self.spec = pl.BlockSpec((step, cols), lambda i: (i, 0))

    def start(self):
        p = self.place
        for off in self.ORDER + (0,):
            self.copies.send(
                self.view(self.full, p.row_yz[off]), self.from_y.at[off], self.y_send.at[off], self.y_recv.at[off], p.at_y
            )

    def got_y(self, off):
        self.copies.arrive(self.from_y.at[off], self.y_send.at[off], self.y_recv.at[off], self.place.at_y)

    def middle(self, off):
        p = self.place
        self.got_y(off)

        def body(a_ref, b_ref, out_ref):
            out_ref[...] = (a_ref[...].astype(jnp.float32) + b_ref[...].astype(jnp.float32)).astype(jnp.bfloat16)

        mine = self.view(self.full, p.row_z[off])
        pltpu.emit_pipeline(body, grid=(self.grid,), in_specs=[self.spec] * 2, out_specs=[self.spec])(
            mine, self.from_y.at[off], self.from_y.at[off]
        )
        self.copies.send(
            self.from_y.at[off], self.from_z.at[off - 1], self.z_send.at[off - 1], self.z_recv.at[off - 1], p.at_z[off]
        )

    def end(self):
        p = self.place
        self.got_y(0)
        for off in (1, 3, 2):
            self.copies.arrive(self.from_z.at[off - 1], self.z_send.at[off - 1], self.z_recv.at[off - 1], p.at_z[off])

        def body(a_ref, b_ref, c_ref, d_ref, e_ref, out_ref):
            total = a_ref[...].astype(jnp.float32)
            for ref in (b_ref, c_ref, d_ref, e_ref):
                total = total + ref[...].astype(jnp.float32)
            out_ref[...] = total
            cols = total.shape[1]
            self.squares[0:1, 0:cols] += jnp.sum(total * total, axis=0, keepdims=True)

        mine = self.view(self.full, p.row)
        pltpu.emit_pipeline(body, grid=(self.grid,), in_specs=[self.spec] * 5, out_specs=[self.spec])(
            mine, self.from_y.at[0], self.from_z.at[0], self.from_z.at[1], self.from_z.at[2], self.owned
        )


def backward_kernel(
    w_qkv, w_out, w_gu, w_down, attn_in, cot_full, ffn_in, qkv, heads, log_sums, resid, gate, up, hidden, down_grad,
    down_out, tokens, cot, gain, cosines, sines, seg_col, parent_col, seg_row,
    mixed, d_tokens, own_qkv, own_out, own_gu, own_down, totals_out,
    gate_grad, up_grad, out_back, proj_grad, gu_grad, out_grad, qkv_grad,
    y_qkv, y_out, y_gate, y_up, y_down, z_qkv, z_out, z_gate, z_up, z_down,
    partial, away, mine, from_core, from_x, mid, wide_buf, low_buf, near_buf, gain_buf, gain_sum, squares,
    key_sum, value_sum, grad_buf, stage, came, z_came, totals,
    r_ysend, r_yrecv, r_zsend, r_zrecv, t_send, t_recv, t_keep, u_send, u_recv, l_sem, n_send, n_recv,
):
    place = Place()
    copies = Copies()
    place.greet()

    def row_block(full, r):
        return full.at[rows_of(r, OWN), :]

    def col_block(full, r):
        return full.at[:, rows_of(r, OWN)]

    def grad_sum(index, full, view, *refs):
        sems = (r_ysend.at[index], r_yrecv.at[index], r_zsend.at[index], r_zrecv.at[index])
        return GradSum(place, copies, full, view, *refs, squares, sems)

    r_qkv = grad_sum(0, qkv_grad, row_block, y_qkv, z_qkv, own_qkv)
    r_out = grad_sum(1, out_grad, col_block, y_out, z_out, own_out)
    r_gate = grad_sum(2, gu_grad.at[0], row_block, y_gate, z_gate, own_gu.at[0])
    r_up = grad_sum(3, gu_grad.at[1], row_block, y_up, z_up, own_gu.at[1])
    r_down = grad_sum(4, down_grad, col_block, y_down, z_down, own_down)
    a_back = [
        TokenGather(place, copies, out_back, m * TREE, t_send.at[m], t_recv.at[m]) for m in range(MICRO)
    ]

    def token_sum(turn, m):
        if turn == 1:
            blocks = lambda i: down_out.at[pl.ds(pl.multiple_of(m * TREE + i * OWN, OWN), OWN), :]
            far, near = away.at[m], mine.at[m]
        else:
            blocks = lambda i: partial.at[m, i]
            far, near = partial.at[m, place.col_x], partial.at[m, place.own]
        lands = 1 if turn == 1 else 0
        return TokenSum(
            place, copies, blocks, far, near, from_core.at[lands, m], from_x.at[lands, m], u_send.at[turn, m],
            u_recv.at[turn, m],
        )

    ffn_sum = [token_sum(0, m) for m in range(MICRO)]
    mlp_sum = [token_sum(1, m) for m in range(MICRO)]
    attn_sum = [token_sum(2, m) for m in range(MICRO)]

    def grad_hidden(m):
        def body(c_ref, w_ref, gate_ref, up_ref, gate_out, up_out):
            for part in range(TREE // OWN):
                rows = slice(part * OWN, (part + 1) * OWN)
                back = residual_mult * dot_nt(c_ref[rows, :], w_ref[...])
                gate_out[rows, :] = (back * gate_ref[rows, :].astype(jnp.float32)).astype(jnp.bfloat16)
                up_out[rows, :] = (back * up_ref[rows, :].astype(jnp.float32)).astype(jnp.bfloat16)

        cols = pl.BlockSpec((TREE, 256), lambda j: (m, j))
        pltpu.emit_pipeline(
            body,
            grid=(WIDE // 256,),
            in_specs=[
                pl.BlockSpec((TREE, D), lambda j: (m, 0)),
                pl.BlockSpec((256, D), lambda j: (j, 0)),
                cols,
                cols,
            ],
            out_specs=[cols, cols],
        )(cot_full, w_down, gate, up, gate_grad, up_grad)

    def grad_weight(near_all, far_all, out, near_cols, far_cols, side=None):
        def body(a_ref, b_ref, out_ref):
            out_ref[...] = dot_tn(a_ref[...], b_ref[...]).astype(jnp.bfloat16)

        def block(j):
            return j if side is None else j * NY + side

        pltpu.emit_pipeline(
            body,
            grid=(near_cols // OWN if side is None else NZ,),
            in_specs=[
                pl.BlockSpec((MICRO * TREE, OWN), lambda j: (0, block(j))),
                pl.BlockSpec((MICRO * TREE, far_cols), lambda j: (0, 0)),
            ],
            out_specs=[pl.BlockSpec((OWN, far_cols), lambda j: (block(j), 0))],
        )(near_all, far_all, out)

    def back_ffn(m):
        def body(step, g_ref, u_ref, wg_ref, wu_ref):
            for part in range(TREE // OWN):
                rows = slice(part * OWN, (part + 1) * OWN)
                value = dot_nt(g_ref[rows, :], wg_ref[0]) + dot_nt(u_ref[rows, :], wu_ref[0])
                partial[m, part, :, pl.ds(pl.multiple_of(step.index[0] * 256, 256), 256)] = value.astype(jnp.bfloat16)

        tree = pl.BlockSpec((TREE, WIDE), lambda j: (m, 0))
        pltpu.emit_pipeline(
            body,
            grid=(D // 256,),
            in_specs=[
                tree,
                tree,
                pl.BlockSpec((1, 256, WIDE), lambda j: (0, j, 0)),
                pl.BlockSpec((1, 256, WIDE), lambda j: (1, j, 0)),
            ],
            out_specs=[],
            _explicit_indices=True,
        )(gate_grad, up_grad, w_gu, w_gu)

    def back_attention(m):
        tree = pl.BlockSpec((TREE, 128), lambda g: (m, 0))
        group = pl.BlockSpec((TREE, 384), lambda g: (m, g))
        pltpu.emit_pipeline(
            functools.partial(attend_back, key_sum, value_sum, grad_buf),
            grid=(2,),
            in_specs=[
                pl.BlockSpec((TREE, D), lambda g: (m, 0)),
                pl.BlockSpec((256, D), lambda g: (g, 0)),
                pl.BlockSpec((TREE, 256), lambda g: (m, g)),
                pl.BlockSpec((4 * TREE, 128), lambda g: (m * 2 + g, 0)),
                group,
                tree,
                tree,
                tree,
                tree,
                pl.BlockSpec((8, TREE), lambda g: (m, 0)),
            ],
            out_specs=[group],
        )(out_back, w_out, heads, log_sums, qkv, cosines, sines, seg_col, parent_col, seg_row, proj_grad)

    def back_project(m):
        def body(step, a_ref, w_ref):
            partial[m, step.index[0]] = dot_nt(a_ref[...], w_ref[...]).astype(jnp.bfloat16)

        steps = TREE // OWN
        pltpu.emit_pipeline(
            body,
            grid=(steps,),
            in_specs=[
                pl.BlockSpec((OWN, 768), lambda i: (m * steps + i, 0)),
                pl.BlockSpec((D, 768), lambda i: (0, 0)),
            ],
            out_specs=[],
            _explicit_indices=True,
        )(proj_grad, w_qkv)

    def norm_back_rows(value, upstream, which):
        row_gain = gain_buf[which : which + 1, :]
        scale = lax.rsqrt(jnp.mean(value * value, axis=-1, keepdims=True) + norm_eps)
        scaled = upstream * row_gain
        inner = jnp.mean(scaled * value, axis=-1, keepdims=True)
        gain_sum[which : which + 1, :] += jnp.sum(upstream * value * scale, axis=0, keepdims=True)
        return scale * scaled - value * (scale * scale * scale * inner)

    def middle_back(m):
        ffn_sum[m].arrive()
        load = copies.local(resid.at[m], wide_buf, l_sem.at[0])
        load_low = copies.local(cot.at[m], low_buf, l_sem.at[1])
        load.wait()
        load_low.wait()

        @pl.loop(0, OWN // 16)
        def _(i):
            rows = rows_of(i, 16)
            back = norm_back_rows(wide_buf[rows, :], ffn_sum[m].rows(rows), 1)
            value = low_buf[rows, :].astype(jnp.float32) + back
            mid[m, rows, :] = value
            near_buf[m, rows, :] = (residual_mult * value).astype(jnp.bfloat16)

        a_back[m].start(near_buf.at[m], t_keep.at[m])

    def finish_mixed(m):
        mlp_sum[m].arrive()
        load = copies.local(resid.at[m], wide_buf, l_sem.at[0])
        load.wait()

        @pl.loop(0, OWN // 16)
        def _(i):
            rows = rows_of(i, 16)
            low_buf[rows, :] = (wide_buf[rows, :] + residual_mult * mlp_sum[m].rows(rows)).astype(jnp.bfloat16)

        copies.local(low_buf, mixed.at[m], l_sem.at[1]).wait()

    def finish_tokens(m):
        attn_sum[m].arrive()
        copies.local(tokens.at[m], low_buf, l_sem.at[1]).wait()

        @pl.loop(0, OWN // 16)
        def _(i):
            rows = rows_of(i, 16)
            back = norm_back_rows(low_buf[rows, :].astype(jnp.float32), attn_sum[m].rows(rows), 0)
            mid[m, rows, :] = mid[m, rows, :] + back

        return copies.local(mid.at[m], d_tokens.at[m], l_sem.at[2 + m])

    def sent(part):
        copies.close(part.sent)

    def sum_everywhere():
        stage[0] = jnp.zeros_like(stage[0])
        stage[0, 0:2, :] = gain_sum[0:2, :]
        stage[0, 2:3, :] = squares[0:1, :]
        for k, partner in enumerate((place.at_c, place.at_x, place.at_y)):
            copies.send(stage.at[k], came.at[k], n_send.at[k], n_recv.at[k], partner)
            copies.arrive(came.at[k], n_send.at[k], n_recv.at[k], partner)
            stage[k + 1] = stage[k] + came[k]
        last = stage.at[3]
        for off in range(1, NZ):
            copies.send(last, z_came.at[place.z], n_send.at[2 + off], n_recv.at[3 + place.z], place.at_z[off])
        z_came[place.z] = stage[3]
        for off in range(1, NZ):
            there = lax.rem(place.z + off, NZ)
            copies.arrive(z_came.at[there], n_send.at[2 + off], n_recv.at[3 + there], place.at_z[off])
        total = z_came[0]
        for there in range(1, NZ):
            total = total + z_came[there]
        gains_total = total[0:2]
        norm = jnp.sqrt(
            jnp.sum(total[2:3], axis=(0, 1), keepdims=True) + jnp.sum(gains_total * gains_total, axis=(0, 1), keepdims=True)
        )
        factor = jnp.minimum(1.0, clip_bound() / (norm + 1e-06))
        totals[...] = jnp.zeros_like(totals)
        totals[0:2, :] = gains_total
        totals[2:3, :] = jnp.broadcast_to(factor, (1, D))
        totals[3:4, :] = jnp.broadcast_to(norm, (1, D))

    def load_partial(m):
        return [
            copies.local(mlp_sum[m].blocks(place.col_x), away.at[m], l_sem.at[2 + 2 * m]),
            copies.local(mlp_sum[m].blocks(place.own), mine.at[m], l_sem.at[3 + 2 * m]),
        ]

    r_down.start()
    mlp_sum[0].start()
    mlp_sum[1].start()
    load_gain = copies.local(gain, gain_buf, l_sem.at[0])
    parts = load_partial(0) + load_partial(1)
    gain_sum[...] = jnp.zeros_like(gain_sum)
    squares[...] = jnp.zeros_like(squares)
    load_gain.wait()
    for copy in parts:
        copy.wait()
    mlp_sum[0].middle()
    mlp_sum[1].middle()
    grad_hidden(0)
    grad_hidden(1)
    r_down.middle(2)
    back_ffn(0)
    ffn_sum[0].start()
    r_down.middle(1)
    back_ffn(1)
    ffn_sum[1].start()
    ffn_sum[0].middle()
    grad_weight(ffn_in, gate_grad, gu_grad.at[0], D, WIDE, 1 - place.y)
    r_gate.start()
    ffn_sum[1].middle()
    r_down.middle(3)
    grad_weight(ffn_in, gate_grad, gu_grad.at[0], D, WIDE, place.y)
    finish_mixed(0)
    middle_back(0)
    grad_weight(ffn_in, up_grad, gu_grad.at[1], D, WIDE, 1 - place.y)
    r_up.start()
    middle_back(1)
    r_gate.middle(2)
    a_back[0].relay()
    grad_weight(ffn_in, up_grad, gu_grad.at[1], D, WIDE, place.y)
    r_gate.middle(1)
    finish_mixed(1)
    a_back[1].relay()
    a_back[0].finish()
    back_attention(0)
    r_gate.middle(3)
    sent(ffn_sum[0])
    back_project(0)
    attn_sum[0].start()
    a_back[1].finish()
    grad_weight(heads, out_back, out_grad, 512, D)
    r_out.start()
    r_up.middle(2)
    back_attention(1)
    sent(ffn_sum[1])
    attn_sum[0].middle()
    grad_weight(attn_in, proj_grad, qkv_grad, D, 768)
    r_qkv.start()
    r_up.middle(1)
    back_project(1)
    attn_sum[1].start()
    r_up.middle(3)
    r_down.end()
    attn_sum[1].middle()
    for off in GradSum.ORDER:
        r_out.middle(off)
    stores = [finish_tokens(0)]
    for off in GradSum.ORDER:
        r_qkv.middle(off)
    r_gate.end()
    stores.append(finish_tokens(1))
    r_up.end()
    r_out.end()
    r_qkv.end()
    sum_everywhere()
    stores.append(copies.local(totals, totals_out, l_sem.at[1]))
    for copy in stores:
        copy.wait()
    copies.close()


def backward(saved, tokens, cot, gains, tables):
    low = jnp.bfloat16
    wide = jnp.float32
    shape = jax.ShapeDtypeStruct
    all_tokens = MICRO * TREE
    blocks = [(OWN, 768), (512, OWN), (OWN, WIDE), (OWN, WIDE), (WIDE, OWN)]
    outs = [shape((MICRO, OWN, D), low), shape((MICRO, OWN, D), wide)]
    outs += [shape(block, wide) for block in ((OWN, 768), (512, OWN), (2, OWN, WIDE), (WIDE, OWN))]
    outs += [shape((8, D), wide)]
    outs += [
        shape((all_tokens, WIDE), low), shape((all_tokens, WIDE), low), shape((all_tokens, D), low),
        shape((all_tokens, 768), low),
        shape((2, D, WIDE), low), shape((512, D), low), shape((D, 768), low),
    ]
    outs += [shape((NZ,) + block, low) for block in blocks]
    outs += [shape((NZ - 1,) + block, low) for block in blocks]
    dma = pltpu.SemaphoreType.DMA
    args = (*saved, tokens, cot, gains, *tables)
    return pl.pallas_call(
        backward_kernel,
        out_shape=outs,
        in_specs=[HBM] * len(args),
        out_specs=[HBM] * len(outs),
        scratch_shapes=[
            pltpu.VMEM((MICRO, NX * NC, OWN, D), low),
            pltpu.VMEM((MICRO, OWN, D), low),
            pltpu.VMEM((MICRO, OWN, D), low),
            pltpu.VMEM((2, MICRO, NX, OWN, D), low),
            pltpu.VMEM((2, MICRO, OWN, D), low),
            pltpu.VMEM((MICRO, OWN, D), wide),
            pltpu.VMEM((OWN, D), wide),
            pltpu.VMEM((OWN, D), low),
            pltpu.VMEM((MICRO, OWN, D), low),
            pltpu.VMEM((2, D), wide),
            pltpu.VMEM((8, D), wide),
            pltpu.VMEM((8, D), wide),
            pltpu.VMEM((TREE, 128), wide),
            pltpu.VMEM((TREE, 128), wide),
            pltpu.VMEM((TREE, 256), low),
            pltpu.VMEM((4, 8, D), wide),
            pltpu.VMEM((3, 8, D), wide),
            pltpu.VMEM((NZ, 8, D), wide),
            pltpu.VMEM((8, D), wide),
            dma((5, NZ)), dma((5, NZ)), dma((5, NZ)), dma((5, NZ)),
            dma((MICRO, 3)), dma((MICRO, NX * NC)), dma((MICRO,)),
            dma((3, MICRO, 3)), dma((3, MICRO, 3)), dma((6,)), dma((6,)), dma((3 + NZ,)),
        ],
        input_output_aliases={11: 7, 12: 8},
        compiler_params=pltpu.CompilerParams(
            collective_id=1, has_side_effects=True, vmem_limit_bytes=63 * 1024 * 1024
        ),
        cost_estimate=pl.CostEstimate(flops=140 * 10**9, bytes_accessed=5 * 10**8, transcendentals=10**7),
        name="backward",
    )(*args)


def update_kernel(
    g_qkv, g_out, g_gu, g_down, w_qkv, w_out, w_gu, w_down, mom_qkv, mom_out, mom_gu, mom_down, gains, mom_gains, totals,
    new_qkv, new_out, new_gu, new_down, moments_qkv, moments_out, moments_gu, moments_down,
    copy_qkv, copy_out, copy_gu, copy_down, new_gains, moments_gains,
):
    rates = step_rates()

    def step_of(grad, master, first, second, rate):
        clipped = totals[2:3, 0:1].reshape((1,) * grad.ndim) * grad
        first = beta_one * first + (1.0 - beta_one) * clipped
        second = beta_two * second + (1.0 - beta_two) * clipped * clipped
        first_hat = first / (1.0 - beta_one**STEP)
        second_hat = second / (1.0 - beta_two**STEP)
        updated = master - rate * (first_hat / (jnp.sqrt(second_hat) + adam_eps) + weight_decay * master)
        return updated, first, second

    def weight(rate, rows, grad, master, moments, new, new_moments, new_copy):
        def body(g_ref, w_ref, m_ref, new_ref, mom_ref, low_ref):
            updated, first, second = step_of(g_ref[...], w_ref[...], m_ref[0], m_ref[1], rate)
            new_ref[...] = updated
            mom_ref[0] = first
            mom_ref[1] = second
            low_ref[...] = updated.astype(jnp.bfloat16)

        rest = master.shape[1:]
        zeros = (0,) * len(rest)
        one = pl.BlockSpec((rows,) + rest, lambda i: (i,) + zeros)
        two = pl.BlockSpec((2, rows) + rest, lambda i: (0, i) + zeros)
        pltpu.emit_pipeline(
            body, grid=(master.shape[0] // rows,), in_specs=[one, one, two], out_specs=[one, two, one]
        )(grad, master, moments, new, new_moments, new_copy)

    weight(rates[2], 64, g_gu, w_gu, mom_gu, new_gu, moments_gu, copy_gu)
    weight(rates[3], 512, g_down, w_down, mom_down, new_down, moments_down, copy_down)
    weight(rates[1], 256, g_out, w_out, mom_out, new_out, moments_out, copy_out)
    weight(rates[0], 64, g_qkv, w_qkv, mom_qkv, new_qkv, moments_qkv, copy_qkv)
    updated, first, second = step_of(totals[0:2, :], gains[...], mom_gains[0], mom_gains[1], rates[4])
    new_gains[...] = updated
    moments_gains[0] = first
    moments_gains[1] = second


def update(grads, masters, states, gains, mom_gains, totals):
    shape = jax.ShapeDtypeStruct
    outs = [shape(master.shape, jnp.float32) for master in masters]
    outs += [shape(state.shape, jnp.float32) for state in states]
    outs += [shape(master.shape, jnp.bfloat16) for master in masters]
    outs += [shape(gains.shape, jnp.float32), shape(mom_gains.shape, jnp.float32)]
    whole = pl.BlockSpec(memory_space=pltpu.VMEM)
    return pl.pallas_call(
        update_kernel,
        out_shape=outs,
        in_specs=[HBM] * 12 + [whole] * 3,
        out_specs=[HBM] * 12 + [whole] * 2,
        compiler_params=pltpu.CompilerParams(vmem_limit_bytes=63 * 1024 * 1024),
        cost_estimate=pl.CostEstimate(flops=60 * 10**6, bytes_accessed=58 * 10**6, transcendentals=4 * 10**6),
        name="update",
    )(*grads, *masters, *states, gains, mom_gains, totals)


def fast_local(
    tokens,
    cotangent,
    segment_of,
    leaf_parent,
    w_qkv,
    mom_qkv,
    w_out,
    mom_out,
    w_gu,
    mom_gu,
    w_down,
    mom_down,
    gains,
    mom_gains,
):
    tables = [position_tables(segment_of[m], leaf_parent[m]) for m in range(MICRO)]
    tables = [jnp.concatenate([table[i] for table in tables], axis=0) for i in range(5)]
    saved = forward(tokens, cotangent, w_qkv, w_out, w_gu, w_down, gains, tables)
    mixed, d_tokens, g_qkv, g_out, g_gu, g_down, totals = backward(saved, tokens, cotangent, gains, tables)[:7]

    def flat(value, lead):
        return value.reshape(value.shape[:lead] + (-1, WIDE))

    masters = (w_qkv, w_out, flat(w_gu, 0), w_down)
    states = (mom_qkv, mom_out, flat(mom_gu, 1), mom_down)
    done = update(
        (g_qkv.reshape(w_qkv.shape), g_out, flat(g_gu, 0), g_down), masters, states, gains, mom_gains, totals
    )
    new, moments, copies = list(done[:4]), list(done[4:8]), list(done[8:12])
    new[2] = new[2].reshape(w_gu.shape)
    moments[2] = moments[2].reshape(mom_gu.shape)
    copies[2] = copies[2].reshape(w_gu.shape)
    results = []
    for i in range(4):
        results += [new[i], moments[i], copies[i]]
    return (mixed, d_tokens, totals[3, 0], *results, done[12], done[13])


def solution(mesh):
    placed = (
        P(None, ("row", "col"), None),
        P(None, ("row", "col"), None),
        P(None, "row"),
        P(None, "row"),
        P("row", "col", None),
        P(None, "row", "col", None),
        P("col", "row"),
        P(None, "col", "row"),
        P(None, "row", "col"),
        P(None, None, "row", "col"),
        P("col", "row"),
        P(None, "col", "row"),
        P(),
        P(),
    )
    sizes = dict(mesh.shape)
    fits = sizes == {"row": NZ * NY, "col": NX * NC}
    return jax.shard_map(
        fast_local if fits else local,
        mesh=mesh,
        in_specs=placed,
        out_specs=(
            P(None, ("row", "col"), None),
            P(None, ("row", "col"), None),
            P(),
            P("row", "col", None),
            P(None, "row", "col", None),
            P("row", "col", None),
            P("col", "row"),
            P(None, "col", "row"),
            P("col", "row"),
            P(None, "row", "col"),
            P(None, None, "row", "col"),
            P(None, "row", "col"),
            P("col", "row"),
            P(None, "col", "row"),
            P("col", "row"),
            P(),
            P(),
        ),
        check_vma=False,
    )
```

```python
import functools
import math

import jax
import jax.numpy as jnp
from jax import lax
from jax.experimental import pallas as pl
from jax.experimental.pallas import tpu as pltpu
from jax.sharding import PartitionSpec as P

D = 2048
FF = 8192
HD = 64
KVH = 8
GROUP = 4
NBRANCH = 4
NLEAF = 8
STEP = 7


norm_eps = 1e-05
residual_mult = 0.22
score_mult = 0.015625
rope_theta = 10000000.0
beta_one = 0.5
beta_two = 0.55
adam_eps = 1e-08
weight_decay = 0.1
masked_value = -1e30


def param_count():
    return D * KVH * (GROUP + 2) * HD + KVH * GROUP * HD * D + 3 * D * FF + 2 * D


def clip_bound():
    return math.sqrt(param_count())


def step_rates():
    return (
        max(D // 12, 1) ** (-0.5),
        max(D // 16, 1) ** (-0.5),
        D ** (-0.5),
        max(FF // 64, 1) ** (-0.5),
        0.3,
    )


def tree_tables(segments, parents):
    seg_count = 1 + NBRANCH + NLEAF
    seg_ids = jnp.arange(seg_count, dtype=jnp.int32)
    member = (segments[:, None] == seg_ids[None, :]).astype(jnp.int32)
    seg_lengths = jnp.sum(member, axis=0)
    seg_starts = jnp.cumsum(seg_lengths) - seg_lengths
    branch_ids = jnp.arange(NBRANCH, dtype=jnp.int32)
    parent_pick = (parents[:, None] == branch_ids[None, :]).astype(jnp.int32)
    parent_len = jnp.sum(parent_pick * seg_lengths[1 : 1 + NBRANCH][None, :], axis=1)
    trunk_len = seg_lengths[0]
    base_depth = jnp.concatenate(
        [
            jnp.zeros((1,), jnp.int32),
            trunk_len * jnp.ones((NBRANCH,), jnp.int32),
            trunk_len + parent_len,
        ]
    )
    places = jnp.arange(segments.shape[0], dtype=jnp.int32)
    depth = places + jnp.sum(member * (base_depth - seg_starts)[None, :], axis=1)
    identity = (seg_ids[:, None] == seg_ids[None, :]).astype(jnp.int32)
    rooted = jnp.broadcast_to((seg_ids[None, :] == 0).astype(jnp.int32), (seg_count, seg_count))
    leaf_links = jnp.concatenate(
        [jnp.zeros((NLEAF, 1), jnp.int32), parent_pick, jnp.zeros((NLEAF, NLEAF), jnp.int32)],
        axis=1,
    )
    leaf_links = jnp.concatenate(
        [jnp.zeros((1 + NBRANCH, seg_count), jnp.int32), leaf_links], axis=0
    )
    ancestry = jnp.minimum(identity + rooted + leaf_links, 1)
    token_path = jnp.dot(member, ancestry)
    allowed = (jnp.dot(token_path, member.T) > 0) & (depth[None, :] <= depth[:, None])
    freqs = jnp.exp(jnp.arange(HD // 2, dtype=jnp.float32) * (-2.0 * math.log(rope_theta) / HD))
    angles = depth.astype(jnp.float32)[:, None] * freqs[None, :]
    return (allowed, jnp.cos(angles), jnp.sin(angles))


def rotate(vectors, cosines, sines):
    half_width = vectors.shape[-1] // 2
    first_half = vectors[..., :half_width]
    second_half = vectors[..., half_width:]
    return jnp.concatenate(
        [first_half * cosines - second_half * sines, second_half * cosines + first_half * sines],
        axis=-1,
    )


def normalize(values, gain):
    scaling = lax.rsqrt(jnp.mean(values * values, axis=-1, keepdims=True) + norm_eps)
    return (values * scaling * gain, scaling)


def norm_back(values, scaling, gain, upstream):
    scaled = upstream * gain
    gain_grad = jnp.sum(upstream * values * scaling, axis=0)
    inner = jnp.mean(scaled * values, axis=-1, keepdims=True)
    return (scaling * scaled - values * scaling * scaling * scaling * inner, gain_grad)


def gather_forward(values):
    return lax.all_gather(values, "col", axis=0, tiled=True)


def gather_backward(values):
    return lax.all_gather(values, "col", axis=0, tiled=True)


def sum_forward(term_fn, row_count):
    return lax.psum_scatter(
        term_fn(jnp.int32(0), lax.axis_size("col") * row_count).astype(jnp.bfloat16),
        "col",
        scatter_dimension=0,
        tiled=True,
    ).astype(jnp.float32)


def sum_backward(term_fn, row_count):
    return lax.psum_scatter(
        term_fn(jnp.int32(0), lax.axis_size("col") * row_count).astype(jnp.bfloat16),
        "col",
        scatter_dimension=0,
        tiled=True,
    ).astype(jnp.float32)


def adamw(master, moments, raw_grad, factor, step_rate):
    clipped = factor * raw_grad
    first_moment = beta_one * moments[0] + (1.0 - beta_one) * clipped
    second_moment = beta_two * moments[1] + (1.0 - beta_two) * clipped * clipped
    first_hat = first_moment / (1.0 - beta_one**STEP)
    second_hat = second_moment / (1.0 - beta_two**STEP)
    updated = master - step_rate * (
        first_hat / (jnp.sqrt(second_hat) + adam_eps) + weight_decay * master
    )
    return (updated, jnp.stack([first_moment, second_moment]))


def local(
    tokens,
    cotangent,
    segment_of,
    leaf_parent,
    w_qkv,
    mom_qkv,
    w_out,
    mom_out,
    w_gu,
    mom_gu,
    w_down,
    mom_down,
    gains,
    mom_gains,
):
    low_shards = (
        w_qkv.astype(jnp.bfloat16),
        w_out.astype(jnp.bfloat16),
        w_gu.astype(jnp.bfloat16),
        w_down.astype(jnp.bfloat16),
    )

    def fetch():
        return (
            lax.all_gather(low_shards[0], "row", axis=0, tiled=True),
            lax.all_gather(low_shards[1], "row", axis=1, tiled=True),
            lax.all_gather(low_shards[2], "row", axis=1, tiled=True),
            lax.all_gather(low_shards[3], "row", axis=1, tiled=True),
        )

    outputs = []
    input_grads = []
    owned = None
    unsummed = None
    gain_partial = None
    for batch_index in range(tokens.shape[0]):
        x_local = tokens[batch_index].astype(jnp.float32)
        row_count = x_local.shape[0]
        allowed, cosines, sines = tree_tables(segment_of[batch_index], leaf_parent[batch_index])
        w_a, w_b, w_c, w_d = fetch()
        normed_a, scale_a = normalize(x_local, gains[0])
        attn_in = gather_forward(normed_a.astype(jnp.bfloat16))
        projected = jnp.einsum("td,dkf->tkf", attn_in, w_a, preferred_element_type=jnp.float32)
        tree_len = projected.shape[0]
        groups = projected.shape[1]
        queries = rotate(
            projected[:, :, : GROUP * HD].reshape(tree_len, groups, GROUP, HD),
            cosines[:, None, None, :],
            sines[:, None, None, :],
        ).astype(jnp.bfloat16)
        key_heads = rotate(
            projected[:, :, GROUP * HD : (GROUP + 1) * HD], cosines[:, None, :], sines[:, None, :]
        ).astype(jnp.bfloat16)
        values = projected[:, :, (GROUP + 1) * HD :].astype(jnp.bfloat16)
        scores = jnp.einsum(
            "tkgh,skh->kgts", queries, key_heads, preferred_element_type=jnp.float32
        )
        logits = jnp.where(allowed, score_mult * scores, masked_value)
        row_peak = jnp.max(logits, axis=-1, keepdims=True)
        exp_terms = jnp.exp(logits - row_peak)
        exp_total = jnp.sum(exp_terms, axis=-1, keepdims=True)
        log_total = row_peak + jnp.log(exp_total)
        attn_probs = exp_terms / exp_total
        mixed_heads = (
            jnp.einsum(
                "kgts,skh->tkgh",
                attn_probs.astype(jnp.bfloat16),
                values,
                preferred_element_type=jnp.float32,
            )
            .astype(jnp.bfloat16)
            .reshape(tree_len, -1)
        )

        def out_terms(first_row, row_total):
            return jnp.dot(mixed_heads, w_b, preferred_element_type=jnp.float32)

        attn_sum = sum_forward(out_terms, row_count)
        residual_mid = x_local + residual_mult * attn_sum
        normed_b, scale_b = normalize(residual_mid, gains[1])
        ffn_in = gather_forward(normed_b.astype(jnp.bfloat16))
        gate_up = jnp.einsum("td,edf->tef", ffn_in, w_c, preferred_element_type=jnp.float32)
        gate_act = jax.nn.sigmoid(gate_up[:, 0])
        silu_gate = gate_up[:, 0] * gate_act
        hidden = (silu_gate * gate_up[:, 1]).astype(jnp.bfloat16)

        def down_terms(first_row, row_total):
            return jnp.dot(hidden, w_d, preferred_element_type=jnp.float32)

        mlp_sum = sum_forward(down_terms, row_count)
        outputs.append((residual_mid + residual_mult * mlp_sum).astype(jnp.bfloat16))
        w_a, w_b, w_c, w_d = fetch()
        cot_full = gather_backward(cotangent[batch_index])
        hidden_grad = residual_mult * jnp.einsum(
            "td,fd->tf", cot_full, w_d, preferred_element_type=jnp.float32
        )
        down_grad = residual_mult * jnp.einsum(
            "tf,td->fd", hidden, cot_full, preferred_element_type=jnp.float32
        )
        gate_grad = (
            hidden_grad * gate_up[:, 1] * gate_act * (1.0 + gate_up[:, 0] * (1.0 - gate_act))
        )
        up_grad = hidden_grad * silu_gate
        gate_up_grad = jnp.stack([gate_grad, up_grad], axis=1).astype(jnp.bfloat16)
        gu_grad = jnp.einsum(
            "td,tef->edf", ffn_in, gate_up_grad, preferred_element_type=jnp.float32
        )

        def ffn_back_terms(first_row, row_total):
            return jnp.einsum("tef,edf->td", gate_up_grad, w_c, preferred_element_type=jnp.float32)

        ffn_in_grad = sum_backward(ffn_back_terms, row_count)
        mid_norm_grad, gain_b_grad = norm_back(residual_mid, scale_b, gains[1], ffn_in_grad)
        mid_grad = cotangent[batch_index].astype(jnp.float32) + mid_norm_grad
        attn_out_grad = gather_backward((residual_mult * mid_grad).astype(jnp.bfloat16))
        out_grad = jnp.einsum(
            "tf,td->fd", mixed_heads, attn_out_grad, preferred_element_type=jnp.float32
        )
        heads_grad = (
            jnp.einsum("td,fd->tf", attn_out_grad, w_b, preferred_element_type=jnp.float32)
            .astype(jnp.bfloat16)
            .reshape(tree_len, groups, GROUP, HD)
        )
        attn_probs = jnp.exp(logits - log_total)
        prob_grad = jnp.einsum(
            "tkgh,skh->kgts", heads_grad, values, preferred_element_type=jnp.float32
        )
        row_inner = jnp.sum(prob_grad * attn_probs, axis=-1, keepdims=True)
        score_grad = (score_mult * attn_probs * (prob_grad - row_inner)).astype(jnp.bfloat16)
        query_grad = jnp.einsum(
            "kgts,skh->tkgh", score_grad, key_heads, preferred_element_type=jnp.float32
        )
        key_grad = jnp.einsum(
            "kgts,tkgh->skh", score_grad, queries, preferred_element_type=jnp.float32
        )
        value_grad = jnp.einsum(
            "kgts,tkgh->skh",
            attn_probs.astype(jnp.bfloat16),
            heads_grad,
            preferred_element_type=jnp.float32,
        )
        query_grad = rotate(query_grad, cosines[:, None, None, :], -sines[:, None, None, :])
        key_grad = rotate(key_grad, cosines[:, None, :], -sines[:, None, :])
        proj_grad = jnp.concatenate(
            [query_grad.reshape(tree_len, groups, GROUP * HD), key_grad, value_grad], axis=-1
        ).astype(jnp.bfloat16)
        qkv_grad = jnp.einsum("td,tkf->dkf", attn_in, proj_grad, preferred_element_type=jnp.float32)

        def attn_back_terms(first_row, row_total):
            return jnp.einsum("tkf,dkf->td", proj_grad, w_a, preferred_element_type=jnp.float32)

        attn_in_grad = sum_backward(attn_back_terms, row_count)
        input_norm_grad, gain_a_grad = norm_back(x_local, scale_a, gains[0], attn_in_grad)
        input_grads.append(mid_grad + input_norm_grad)
        gain_step = jnp.stack([gain_a_grad, gain_b_grad])
        gain_partial = gain_step if gain_partial is None else gain_partial + gain_step
        partials = (qkv_grad, out_grad, gu_grad, down_grad)
        unsummed = (
            partials
            if unsummed is None
            else tuple((running + addend for running, addend in zip(unsummed, partials)))
        )
    owned = (
        lax.psum_scatter(
            unsummed[0].astype(jnp.bfloat16), "row", scatter_dimension=0, tiled=True
        ).astype(jnp.float32),
        lax.psum_scatter(
            unsummed[1].astype(jnp.bfloat16), "row", scatter_dimension=1, tiled=True
        ).astype(jnp.float32),
        lax.psum_scatter(
            unsummed[2].astype(jnp.bfloat16), "row", scatter_dimension=1, tiled=True
        ).astype(jnp.float32),
        lax.psum_scatter(
            unsummed[3].astype(jnp.bfloat16), "row", scatter_dimension=1, tiled=True
        ).astype(jnp.float32),
    )
    local_squares = jnp.float32(0.0)
    for grad_piece in owned:
        local_squares = local_squares + jnp.sum(grad_piece * grad_piece)
    total_squares, gain_total = lax.psum((local_squares, gain_partial), ("row", "col"))
    grad_norm = jnp.sqrt(total_squares + jnp.sum(gain_total * gain_total))
    factor = jnp.minimum(1.0, clip_bound() / (grad_norm + 1e-06))
    rates = step_rates()
    masters = (w_qkv, w_out, w_gu, w_down)
    states = (mom_qkv, mom_out, mom_gu, mom_down)
    results = []
    for index_w in range(4):
        updated, moments = adamw(
            masters[index_w], states[index_w], owned[index_w], factor, rates[index_w]
        )
        results.append((updated, moments, updated.astype(jnp.bfloat16)))
    new_gains, moments_gains = adamw(gains, mom_gains, gain_total, factor, rates[4])
    mixed = jnp.stack(outputs, axis=0)
    d_tokens = jnp.stack(input_grads, axis=0)
    return (
        mixed,
        d_tokens,
        grad_norm,
        results[0][0],
        results[0][1],
        results[0][2],
        results[1][0],
        results[1][1],
        results[1][2],
        results[2][0],
        results[2][1],
        results[2][2],
        results[3][0],
        results[3][1],
        results[3][2],
        new_gains,
        moments_gains,
    )


def position_tables(segments, parents):
    seg_ids = jnp.arange(1 + NBRANCH + NLEAF, dtype=jnp.int32)
    member = (segments[:, None] == seg_ids[None, :]).astype(jnp.int32)
    seg_lengths = jnp.sum(member, axis=0)
    seg_starts = jnp.cumsum(seg_lengths) - seg_lengths
    parent_of = jnp.concatenate([jnp.full((1 + NBRANCH,), -1, jnp.int32), 1 + parents])
    branch_ids = jnp.arange(NBRANCH, dtype=jnp.int32)
    parent_pick = (parents[:, None] == branch_ids[None, :]).astype(jnp.int32)
    parent_len = jnp.sum(parent_pick * seg_lengths[1 : 1 + NBRANCH][None, :], axis=1)
    base_depth = jnp.concatenate(
        [
            jnp.zeros((1,), jnp.int32),
            seg_lengths[0] * jnp.ones((NBRANCH,), jnp.int32),
            seg_lengths[0] + parent_len,
        ]
    )
    places = jnp.arange(segments.shape[0], dtype=jnp.int32)
    depth = places + jnp.sum(member * (base_depth - seg_starts)[None, :], axis=1)
    parent = jnp.sum(member * parent_of[None, :], axis=1)
    freqs = jnp.exp(jnp.arange(HD // 2, dtype=jnp.float32) * (-2.0 * math.log(rope_theta) / HD))
    angles = depth.astype(jnp.float32)[:, None] * freqs[None, :]
    cosines, sines = jnp.cos(angles), jnp.sin(angles)
    return (
        jnp.concatenate([cosines] * 4, axis=1),
        jnp.concatenate([-sines, sines] * 2, axis=1),
        jnp.broadcast_to(segments[:, None].astype(jnp.float32), (segments.shape[0], 128)),
        jnp.broadcast_to(parent[:, None].astype(jnp.float32), (segments.shape[0], 128)),
        jnp.broadcast_to(segments[None, :].astype(jnp.float32), (8, segments.shape[0])),
    )

def dot_nn(a, b):
    return lax.dot_general(a, b, (((1,), (0,)), ((), ())), preferred_element_type=jnp.float32)


def dot_nt(a, b):
    return lax.dot_general(a, b, (((1,), (1,)), ((), ())), preferred_element_type=jnp.float32)


def dot_tn(a, b):
    return lax.dot_general(a, b, (((0,), (0,)), ((), ())), preferred_element_type=jnp.float32)


MICRO = 2
TREE = 1024
OWN = 256
WIDE = 2048
NX, NC, NZ, NY = 2, 2, 4, 2
SEG = 128
MESH = pl.DeviceIdType.MESH
HBM = pl.BlockSpec(memory_space=pl.ANY)


class Place:
    def __init__(self):
        row, col = lax.axis_index("row"), lax.axis_index("col")
        self.row, self.col = row, col
        self.z, self.y = row // NY, row % NY
        self.x, self.c = col // NC, col % NC
        self.own = col
        self.row_z = [lax.rem(row + NY * off, NZ * NY) for off in range(NZ)]
        self.row_y = self.z * NY + (1 - self.y)
        self.row_yz = [lax.rem(self.z + off, NZ) * NY + (1 - self.y) for off in range(NZ)]
        self.col_x = (1 - self.x) * NC + self.c
        self.col_c = self.x * NC + (1 - self.c)
        self.col_xc = (1 - self.x) * NC + (1 - self.c)
        self.at_z = [None] + [(self.row_z[off], col) for off in range(1, NZ)]
        self.at_up = (lax.rem(row + NY, NZ * NY), col)
        self.at_down = (lax.rem(row + (NZ - 1) * NY, NZ * NY), col)
        self.at_y = (self.row_y, col)
        self.at_x = (row, self.col_x)
        self.at_c = (row, self.col_c)

    def greet(self):
        barrier = pltpu.get_barrier_semaphore()
        partners = self.at_z[1:] + [self.at_y, self.at_x, self.at_c]
        for partner in partners:
            pl.semaphore_signal(barrier, inc=1, device_id=partner, device_id_type=MESH)
        pl.semaphore_wait(barrier, len(partners))


class Copies:
    def __init__(self):
        self.open_sends = []

    def send(self, src, dst, send_sem, recv_sem, device, when=True):
        copy = pltpu.make_async_remote_copy(
            src_ref=src, dst_ref=dst, send_sem=send_sem, recv_sem=recv_sem,
            device_id=device, device_id_type=MESH,
        )
        if when is True:
            copy.start()
        else:
            pl.when(when)(copy.start)
        self.open_sends.append((copy, when))
        return copy

    def arrive(self, dst, send_sem, recv_sem, device, when=True):
        copy = pltpu.make_async_remote_copy(
            src_ref=dst, dst_ref=dst, send_sem=send_sem, recv_sem=recv_sem,
            device_id=device, device_id_type=MESH,
        )
        if when is True:
            copy.wait_recv()
        else:
            pl.when(when)(copy.wait_recv)

    def local(self, src, dst, sem):
        copy = pltpu.make_async_copy(src, dst, sem)
        copy.start()
        return copy

    def close(self, some=None):
        left = []
        for copy, when in self.open_sends:
            if some is not None and not any(copy is one for one in some):
                left.append((copy, when))
            elif when is True:
                copy.wait_send()
            else:
                pl.when(when)(copy.wait_send)
        self.open_sends = left


def rows_of(index, size):
    return pl.ds(pl.multiple_of(index * size, size), size)


class WeightGather:
    def __init__(self, place, copies, own, full, view, send, recv, keep, over_y_first):
        self.place, self.copies, self.own, self.full, self.view = place, copies, own, full, view
        self.send, self.recv, self.keep = send, recv, keep
        self.sides = (place.y, 1 - place.y) if over_y_first else (place.y,)
        self.over_y_first = over_y_first

    def block(self, r):
        return self.view(self.full, r)

    def pass_on(self, src, r, up, down, over_y):
        p = self.place
        here = self.block(r)
        if up is not None:
            self.copies.send(src, here, self.send.at[0, r], self.recv.at[r], p.at_up, up)
        if down is not None:
            self.copies.send(src, here, self.send.at[1, r], self.recv.at[r], p.at_down, down)
        if over_y is not None:
            self.copies.send(src, here, self.send.at[2, r], self.recv.at[r], p.at_y, over_y)

    def start_y(self):
        p = self.place
        self.kept = self.copies.local(self.own, self.block(p.row), self.keep)
        self.pass_on(self.own, p.row, None, None, True)

    def start_z(self):
        p = self.place
        self.pass_on(self.own, p.row, p.z < NZ - 1, p.z > 0, None)

    def arrive(self, r, when=True):
        self.copies.arrive(self.block(r), self.send.at[2, r], self.recv.at[r], self.place.at_y, when)

    def relay_y(self):
        p = self.place
        self.arrive(p.row_y)
        self.pass_on(self.block(p.row_y), p.row_y, p.z < NZ - 1, p.z > 0, None)

    def relay(self, k):
        p = self.place
        for there, upward in ((p.z - k, True), (p.z + k, False)):
            came = there >= 0 if upward else there < NZ
            safe = lax.rem(there + NZ, NZ)
            for side in self.sides:
                r = safe * NY + side
                self.arrive(r, came)
                on = jnp.logical_and(came, p.z < NZ - 1) if upward else jnp.logical_and(came, p.z > 0)
                self.pass_on(
                    self.block(r), r, on if upward else None, None if upward else on, None if self.over_y_first else came
                )

    def finish(self):
        if not self.over_y_first:
            for off in range(NZ):
                self.arrive(self.place.row_yz[off])
        if self.kept is not None:
            self.keep_own()

    def keep_own(self):
        self.kept.wait()
        self.kept = None


class TokenGather:
    def __init__(self, place, copies, full, base, send, recv):
        self.place, self.copies, self.full, self.base = place, copies, full, base
        self.send, self.recv = send, recv

    def block(self, index):
        return self.full.at[pl.ds(pl.multiple_of(self.base + index * OWN, OWN), OWN), :]

    def start(self, own, keep):
        p = self.place
        here = self.block(p.own)
        self.kept = self.copies.local(own, here, keep)
        self.copies.send(own, here, self.send.at[0], self.recv.at[p.own], p.at_x)
        self.copies.send(own, here, self.send.at[1], self.recv.at[p.own], p.at_c)

    def relay(self):
        p = self.place
        block = self.block(p.col_x)
        self.copies.arrive(block, self.send.at[2], self.recv.at[p.col_x], p.at_c)
        self.copies.send(block, block, self.send.at[2], self.recv.at[p.col_x], p.at_c)

    def finish(self):
        p = self.place
        for index in (p.col_c, p.col_xc):
            self.copies.arrive(self.block(index), self.send.at[2], self.recv.at[index], p.at_c)
        self.kept.wait()


class TokenSum:
    def __init__(self, place, copies, blocks, away, mine, from_core, from_x, send, recv):
        self.place, self.copies, self.blocks, self.away, self.mine = place, copies, blocks, away, mine
        self.from_core, self.from_x, self.send, self.recv = from_core, from_x, send, recv

    def start(self):
        p = self.place
        self.sent = []
        for there in range(NX):
            self.sent.append(
                self.copies.send(
                    self.blocks(there * NC + (1 - p.c)), self.from_core.at[there],
                    self.send.at[there], self.recv.at[there], p.at_c,
                )
            )

    def middle(self):
        p = self.place
        for there in range(NX):
            self.copies.arrive(self.from_core.at[there], self.send.at[there], self.recv.at[there], p.at_c)
        other = 1 - p.x

        @pl.loop(0, OWN // 32)
        def _(i):
            rows = rows_of(i, 32)
            self.away[rows, :] = (
                self.away[rows, :].astype(jnp.float32) + self.from_core[other, rows, :].astype(jnp.float32)
            ).astype(jnp.bfloat16)

        self.sent.append(self.copies.send(self.away, self.from_x, self.send.at[2], self.recv.at[2], p.at_x))

    def arrive(self):
        p = self.place
        self.copies.arrive(self.from_x, self.send.at[2], self.recv.at[2], p.at_x)

    def rows(self, rows):
        p = self.place
        return (
            self.mine[rows, :].astype(jnp.float32)
            + self.from_core[p.x, rows, :].astype(jnp.float32)
            + self.from_x[rows, :].astype(jnp.float32)
        )


def swap_halves(tile):
    lane = lax.broadcasted_iota(jnp.int32, tile.shape, 1)
    return jnp.where(lane % HD < HD // 2, pltpu.roll(tile, 128 - HD // 2, 1), pltpu.roll(tile, HD // 2, 1))


def masked_parts(run, seg_col, parent_col, seg_row):
    rows = slice(run * SEG, (run + 1) * SEG)

    def causal():
        shape = (SEG, 2 * SEG)
        return lax.broadcasted_iota(jnp.int32, shape, 1) <= lax.broadcasted_iota(jnp.int32, shape, 0) + run * SEG

    def of_parent():
        return seg_row[0:1, 2 * SEG : 4 * SEG] == parent_col[rows, 0:1]

    def of_run():
        shape = (SEG, SEG)
        order = lax.broadcasted_iota(jnp.int32, shape, 1) <= lax.broadcasted_iota(jnp.int32, shape, 0)
        return order & (seg_row[0:1, rows] == seg_col[rows, 0:1])

    if run < 2:
        return [(slice(0, 2 * SEG), causal())]
    parts = [(slice(0, 2 * SEG), None)]
    if run >= 4:
        parts.append((slice(2 * SEG, 4 * SEG), of_parent()))
    parts.append((rows, of_run()))
    return parts


def softmax_parts(scores):
    peak = None
    for score in scores:
        top = jnp.max(score, axis=-1, keepdims=True)
        peak = top if peak is None else jnp.maximum(peak, top)
    peak = peak * score_mult
    exps = [jnp.exp(score * score_mult - peak) for score in scores]
    total = None
    for term in exps:
        part = jnp.sum(term, axis=-1, keepdims=True)
        total = part if total is None else total + part
    return exps, total, peak + jnp.log(total)


def stacked_pairs(tile_ref, rows):
    both = jnp.concatenate([tile_ref[rows, 0:128], tile_ref[rows, 128:256]], axis=0)
    lane = lax.broadcasted_iota(jnp.int32, both.shape, 1)
    zero = jnp.zeros_like(both)
    return jnp.concatenate([jnp.where(lane < HD, both, zero), jnp.where(lane < HD, zero, both)], axis=0)


def unstack_pairs(wide):
    half = wide.shape[0] // 2
    lane = lax.broadcasted_iota(jnp.int32, (half, 128), 1)
    return jnp.where(lane < HD, wide[:half], wide[half:])


def twice(kv):
    wide = kv.astype(jnp.float32)
    lane = lax.broadcasted_iota(jnp.int32, wide.shape, 1)
    other = pltpu.roll(wide, HD, 1)
    key = jnp.where(lane < HD, wide, other)
    value = jnp.where(lane < HD, other, wide)
    return key.astype(jnp.bfloat16), value.astype(jnp.bfloat16)


def score_parts(queries, keys, parts):
    scores = []
    for span, mask in parts:
        score = dot_nt(queries, keys[span])
        if mask is not None:
            score = jnp.where(jnp.concatenate([mask] * 4, axis=0), score, masked_value)
        scores.append(score)
    return scores


def attend(qkv_ref, seg_col_ref, parent_col_ref, seg_row_ref, heads_ref, log_ref):
    seg_row = seg_row_ref[...]
    keys, values = twice(qkv_ref[:, 256:384])
    for run in range(TREE // SEG):
        rows = slice(run * SEG, (run + 1) * SEG)
        parts = masked_parts(run, seg_col_ref, parent_col_ref, seg_row)
        exps, total, log_total = softmax_parts(score_parts(stacked_pairs(qkv_ref, rows), keys, parts))
        mixed = None
        for (span, _), term in zip(parts, exps):
            got = dot_nn(term.astype(jnp.bfloat16), values[span])
            mixed = got if mixed is None else mixed + got
        low = unstack_pairs(mixed * (1.0 / total)).astype(jnp.bfloat16)
        heads_ref[rows, 0:128] = low[0:SEG]
        heads_ref[rows, 128:256] = low[SEG:]
        log_ref[run * 4 * SEG : (run + 1) * 4 * SEG, :] = jnp.broadcast_to(log_total, (4 * SEG, 128))


def attend_back(
    key_sum, value_sum, grad_buf, back_ref, w_ref, heads_ref, log_ref, qkv_ref, cos_ref, sin_ref, seg_col_ref,
    parent_col_ref, seg_row_ref, out_ref,
):
    for part in range(TREE // OWN):
        rows = slice(part * OWN, (part + 1) * OWN)
        grad_buf[rows, :] = dot_nt(back_ref[rows, :], w_ref[...]).astype(jnp.bfloat16)
    seg_row = seg_row_ref[...]
    keys, values = twice(qkv_ref[:, 256:384])
    key_sum[...] = jnp.zeros_like(key_sum)
    value_sum[...] = jnp.zeros_like(value_sum)
    for run in range(TREE // SEG):
        rows = slice(run * SEG, (run + 1) * SEG)
        parts = masked_parts(run, seg_col_ref, parent_col_ref, seg_row)
        queries = stacked_pairs(qkv_ref, rows)
        upstream = stacked_pairs(grad_buf, rows)
        mixed = stacked_pairs(heads_ref, rows)
        inner = jnp.sum(upstream.astype(jnp.float32) * mixed.astype(jnp.float32), axis=-1, keepdims=True)
        log_total = log_ref[run * 4 * SEG : (run + 1) * 4 * SEG, 0:1]
        query_grad = None
        for (span, _), score in zip(parts, score_parts(queries, keys, parts)):
            prob = jnp.exp(score * score_mult - log_total)
            prob_grad = dot_nt(upstream, values[span])
            score_grad = (prob * (prob_grad - inner)).astype(jnp.bfloat16)
            term = dot_nn(score_grad, keys[span])
            query_grad = term if query_grad is None else query_grad + term
            key_sum[span, :] += dot_tn(score_grad, queries)
            value_sum[span, :] += dot_tn(prob.astype(jnp.bfloat16), upstream)
        pair_grad = unstack_pairs(query_grad) * score_mult
        cos, sin = cos_ref[rows, :], sin_ref[rows, :]
        for tile in range(2):
            part = pair_grad[tile * SEG : (tile + 1) * SEG]
            out_ref[rows, tile * 128 : (tile + 1) * 128] = (part * cos - swap_halves(part) * sin).astype(jnp.bfloat16)
    key_grad = key_sum[...] * score_mult
    key_grad = key_grad + pltpu.roll(key_grad, HD, 1)
    value_grad = value_sum[...]
    value_grad = value_grad + pltpu.roll(value_grad, HD, 1)
    turned = key_grad * cos_ref[...] - swap_halves(key_grad) * sin_ref[...]
    lane = lax.broadcasted_iota(jnp.int32, turned.shape, 1)
    out_ref[:, 256:384] = jnp.where(lane < HD, turned, value_grad).astype(jnp.bfloat16)


def forward_kernel(
    tokens, cot, own_qkv, own_out, own_gu, own_down, gain, cosines, sines, seg_col, parent_col, seg_row,
    w_qkv, w_out, w_gu, w_down, attn_in, cot_full, ffn_in, qkv, heads, log_sums, resid, gate, up, hidden, down_grad,
    down_out,
    partial, from_core, from_x, normed_buf, tokens_buf, cot_buf, near_buf, gain_buf,
    wide_qkv, wide_out, wide_gu, wide_down, low_qkv, low_out, low_gu, low_down,
    w_send, w_recv, w_keep, t_send, t_recv, t_keep, s_send, s_recv, l_sem,
):
    resid_buf = wide_gu
    place = Place()
    copies = Copies()
    pairs = (
        (own_qkv, wide_qkv), (tokens, tokens_buf), (gain, gain_buf), (own_out, wide_out),
        (own_gu, wide_gu), (cot, cot_buf), (own_down, wide_down),
    )
    loads = [copies.local(src, dst, l_sem.at[i]) for i, (src, dst) in enumerate(pairs)]
    place.greet()

    def row_block(full, r):
        return full.at[rows_of(r, OWN), :]

    def col_block(full, r):
        return full.at[:, rows_of(r, OWN)]

    def weight(index, own, full, view, over_y_first):
        return WeightGather(
            place, copies, own, full, view, w_send.at[index], w_recv.at[index], w_keep.at[index], over_y_first
        )

    g_qkv = weight(0, low_qkv, w_qkv, row_block, True)
    g_out = weight(1, low_out, w_out, col_block, True)
    g_gate = weight(2, low_gu.at[0], w_gu.at[0], row_block, False)
    g_up = weight(3, low_gu.at[1], w_gu.at[1], row_block, False)
    g_down = weight(4, low_down, w_down, col_block, False)

    def token_gather(index, full, m):
        return TokenGather(place, copies, full, m * TREE, t_send.at[index], t_recv.at[index])

    a_in = [token_gather(m, attn_in, m) for m in range(MICRO)]
    a_cot = [token_gather(2 + m, cot_full, m) for m in range(MICRO)]
    a_ffn = [token_gather(4 + m, ffn_in, m) for m in range(MICRO)]
    sums = [
        TokenSum(
            place, copies, functools.partial(lambda m, i: partial.at[m, i], m), partial.at[m, place.col_x],
            partial.at[m, place.own], from_core.at[m], from_x.at[m], s_send.at[m], s_recv.at[m],
        )
        for m in range(MICRO)
    ]

    def project(m):
        def body(a_ref, w_ref, cos_ref, sin_ref, out_ref):
            got = dot_nn(a_ref[...], w_ref[...])
            cos, sin = cos_ref[...], sin_ref[...]
            lane = lax.broadcasted_iota(jnp.int32, cos.shape, 1)
            cos_key = jnp.where(lane < HD, cos, 1.0)
            sin_key = jnp.where(lane < HD, sin, 0.0)
            for tile in range(got.shape[1] // 128):
                part = got[:, tile * 128 : (tile + 1) * 128]
                is_key = tile % 3 == 2
                turned = part * (cos_key if is_key else cos) + swap_halves(part) * (sin_key if is_key else sin)
                out_ref[:, tile * 128 : (tile + 1) * 128] = turned.astype(jnp.bfloat16)

        steps = TREE // OWN
        rows = pl.BlockSpec((OWN, D), lambda i: (m * steps + i, 0))
        table = pl.BlockSpec((OWN, 128), lambda i: (m * steps + i, 0))
        out = pl.BlockSpec((OWN, 768), lambda i: (m * steps + i, 0))
        whole = pl.BlockSpec((D, 768), lambda i: (0, 0))
        pltpu.emit_pipeline(body, grid=(steps,), in_specs=[rows, whole, table, table], out_specs=[out])(
            attn_in, w_qkv, cosines, sines, qkv
        )

    def attention(m):
        tree = pl.BlockSpec((TREE, 128), lambda g: (m, 0))
        pltpu.emit_pipeline(
            attend,
            grid=(2,),
            in_specs=[
                pl.BlockSpec((TREE, 384), lambda g: (m, g)),
                tree,
                tree,
                pl.BlockSpec((8, TREE), lambda g: (m, 0)),
            ],
            out_specs=[
                pl.BlockSpec((TREE, 256), lambda g: (m, g)),
                pl.BlockSpec((4 * TREE, 128), lambda g: (m * 2 + g, 0)),
            ],
        )(qkv, seg_col, parent_col, seg_row, heads, log_sums)

    def out_project(m):
        def body_at(step, a_ref, w_ref):
            partial[m, step.index[0]] = dot_nn(a_ref[...], w_ref[...]).astype(jnp.bfloat16)

        steps = TREE // OWN
        pltpu.emit_pipeline(
            body_at,
            grid=(steps,),
            in_specs=[
                pl.BlockSpec((OWN, 512), lambda i: (m * steps + i, 0)),
                pl.BlockSpec((512, D), lambda i: (0, 0)),
            ],
            out_specs=[],
            _explicit_indices=True,
        )(heads, w_out)

    def lower(wide, low):
        step = 64

        @pl.loop(0, wide.shape[0] // step)
        def _(i):
            rows = rows_of(i, step)
            low[rows, :] = wide[rows, :].astype(jnp.bfloat16)

    def first_norm(m):
        @pl.loop(0, OWN // 32)
        def _(i):
            rows = rows_of(i, 32)
            value = tokens_buf[m, rows, :].astype(jnp.float32)
            scale = lax.rsqrt(jnp.mean(value * value, axis=-1, keepdims=True) + norm_eps)
            near_buf[m, rows, :] = (value * scale * gain_buf[0:1, :]).astype(jnp.bfloat16)

        a_in[m].start(near_buf.at[m], t_keep.at[m])

    def middle_norm(m):
        sums[m].arrive()

        @pl.loop(0, OWN // 32)
        def _(i):
            rows = rows_of(i, 32)
            value = tokens_buf[m, rows, :].astype(jnp.float32) + residual_mult * sums[m].rows(rows)
            resid_buf[m, rows, :] = value
            scale = lax.rsqrt(jnp.mean(value * value, axis=-1, keepdims=True) + norm_eps)
            normed_buf[m, rows, :] = (value * scale * gain_buf[1:2, :]).astype(jnp.bfloat16)

        a_ffn[m].start(normed_buf.at[m], t_keep.at[4 + m])
        return copies.local(resid_buf.at[m], resid.at[m], l_sem.at[m])

    def gate_up(m):
        def body(a_ref, g_ref, u_ref, gate_ref, up_ref, hidden_ref):
            for part in range(TREE // OWN):
                rows = slice(part * OWN, (part + 1) * OWN)
                value = a_ref[rows, :]
                g = dot_nn(value, g_ref[0])
                u = dot_nn(value, u_ref[0])
                act = jax.nn.sigmoid(g)
                silu = g * act
                gate_ref[rows, :] = (u * act * (1.0 + g * (1.0 - act))).astype(jnp.bfloat16)
                up_ref[rows, :] = silu.astype(jnp.bfloat16)
                hidden_ref[rows, :] = (silu * u).astype(jnp.bfloat16)

        cols = pl.BlockSpec((TREE, 256), lambda j: (m, j))
        pltpu.emit_pipeline(
            body,
            grid=(WIDE // 256,),
            in_specs=[
                pl.BlockSpec((TREE, D), lambda j: (m, 0)),
                pl.BlockSpec((1, D, 256), lambda j: (0, 0, j)),
                pl.BlockSpec((1, D, 256), lambda j: (1, 0, j)),
            ],
            out_specs=[cols, cols, cols],
        )(ffn_in, w_gu, w_gu, gate, up, hidden)

    def grad_down():
        def body(h_ref, c_ref, out_ref):
            out_ref[...] = (residual_mult * dot_tn(h_ref[...], c_ref[...])).astype(jnp.bfloat16)

        pltpu.emit_pipeline(
            body,
            grid=(WIDE // 256,),
            in_specs=[
                pl.BlockSpec((MICRO * TREE, 256), lambda i: (0, i)),
                pl.BlockSpec((MICRO * TREE, D), lambda i: (0, 0)),
            ],
            out_specs=[pl.BlockSpec((256, D), lambda i: (i, 0))],
        )(hidden, cot_full, down_grad)

    def down(m, near):
        def body(h_ref, w_ref, out_ref):
            for part in range(TREE // OWN):
                rows = slice(part * OWN, (part + 1) * OWN)
                out_ref[rows, :] = dot_nn(h_ref[rows, :], w_ref[...]).astype(jnp.bfloat16)

        side = place.y if near else 1 - place.y
        pltpu.emit_pipeline(
            body,
            grid=(NZ,),
            in_specs=[
                pl.BlockSpec((TREE, WIDE), lambda j: (m, 0)),
                pl.BlockSpec((WIDE, OWN), lambda j: (0, j * NY + side)),
            ],
            out_specs=[pl.BlockSpec((TREE, OWN), lambda j: (m, j * NY + side))],
        )(hidden, w_down, down_out)

    g_qkv_load, tokens_load, gain_load, out_load, gu_load, cot_load, down_load = loads
    g_qkv_load.wait()
    lower(wide_qkv, low_qkv)
    g_qkv.start_y()
    g_qkv.start_z()
    out_load.wait()
    lower(wide_out, low_out)
    g_out.start_y()
    g_out.start_z()
    tokens_load.wait()
    gain_load.wait()
    for m in range(MICRO):
        first_norm(m)
    gu_load.wait()
    lower(wide_gu.at[0], low_gu.at[0])
    g_gate.start_y()
    g_qkv.relay_y()
    g_out.relay_y()
    lower(wide_gu.at[1], low_gu.at[1])
    g_up.start_y()
    cot_load.wait()
    for m in range(MICRO):
        a_cot[m].start(cot_buf.at[m], t_keep.at[2 + m])
    down_load.wait()
    lower(wide_down, low_down)
    g_down.start_y()
    a_in[0].relay()
    g_qkv.relay(1)
    g_out.relay(1)
    a_in[1].relay()
    g_qkv.relay(2)
    g_out.relay(2)
    g_gate.start_z()
    a_in[0].finish()
    a_in[1].finish()
    a_cot[0].relay()
    g_qkv.relay(3)
    g_qkv.finish()
    project(0)
    g_out.relay(3)
    g_out.finish()
    g_gate.relay(1)
    project(1)
    a_cot[1].relay()
    attention(0)
    g_gate.relay(2)
    g_up.start_z()
    out_project(0)
    sums[0].start()
    attention(1)
    sums[0].middle()
    out_project(1)
    sums[1].start()
    g_gate.relay(3)
    sums[1].middle()
    stored = [middle_norm(0)]
    g_up.relay(1)
    stored.append(middle_norm(1))
    a_ffn[0].relay()
    g_up.relay(2)
    g_down.start_z()
    a_ffn[1].relay()
    g_up.relay(3)
    g_down.relay(1)
    a_cot[0].finish()
    a_cot[1].finish()
    a_ffn[0].finish()
    g_gate.finish()
    g_up.finish()
    gate_up(0)
    g_down.relay(2)
    a_ffn[1].finish()
    gate_up(1)
    g_down.relay(3)
    g_down.keep_own()
    down(0, True)
    down(1, True)
    grad_down()
    g_down.finish()
    down(0, False)
    down(1, False)
    for copy in stored:
        copy.wait()
    copies.close()


def forward(tokens, cot, w_qkv, w_out, w_gu, w_down, gains, tables):
    low = jnp.bfloat16
    wide = jnp.float32
    shape = jax.ShapeDtypeStruct
    all_tokens = MICRO * TREE
    outs = [
        shape((D, 768), low), shape((512, D), low), shape((2, D, WIDE), low), shape((WIDE, D), low),
        shape((all_tokens, D), low), shape((all_tokens, D), low), shape((all_tokens, D), low),
        shape((all_tokens, 768), low), shape((all_tokens, 512), low), shape((2 * MICRO * 4 * TREE, 128), wide),
        shape((MICRO, OWN, D), wide),
        shape((all_tokens, WIDE), low), shape((all_tokens, WIDE), low), shape((all_tokens, WIDE), low),
        shape((WIDE, D), low), shape((all_tokens, D), low),
    ]
    dma = pltpu.SemaphoreType.DMA
    blocks = [(OWN, 768), (512, OWN), (2, OWN, WIDE), (WIDE, OWN)]
    scratch = [
        pltpu.VMEM((MICRO, NX * NC, OWN, D), low),
        pltpu.VMEM((MICRO, NX, OWN, D), low),
        pltpu.VMEM((MICRO, OWN, D), low),
        pltpu.VMEM((MICRO, OWN, D), low),
        pltpu.VMEM((MICRO, OWN, D), low),
        pltpu.VMEM((MICRO, OWN, D), low),
        pltpu.VMEM((MICRO, OWN, D), low),
        pltpu.VMEM((2, D), wide),
    ]
    scratch += [pltpu.VMEM(block, wide) for block in blocks]
    scratch += [pltpu.VMEM(block, low) for block in blocks]
    scratch += [
        dma((5, 3, NZ * NY)), dma((5, NZ * NY)), dma((5,)),
        dma((6, 3)), dma((6, NX * NC)), dma((6,)),
        dma((MICRO, 3)), dma((MICRO, 3)), dma((7,)),
    ]
    return pl.pallas_call(
        forward_kernel,
        out_shape=outs,
        in_specs=[HBM] * 12,
        out_specs=[HBM] * len(outs),
        scratch_shapes=scratch,
        compiler_params=pltpu.CompilerParams(
            collective_id=0, has_side_effects=True, vmem_limit_bytes=63 * 1024 * 1024
        ),
        cost_estimate=pl.CostEstimate(flops=90 * 10**9, bytes_accessed=2 * 10**8, transcendentals=10**7),
        name="forward",
    )(tokens, cot, w_qkv.reshape(OWN, 768), w_out, w_gu, w_down, gains, *tables)


class GradSum:
    ENDS = (3, 2, 1)
    MIDDLES = (3, 2, 0)

    def __init__(self, place, copies, full, view, from_y, from_z, owned, squares, sems):
        self.place, self.copies, self.full, self.view = place, copies, full, view
        self.from_y, self.from_z, self.owned = from_y, from_z, owned
        self.squares = squares
        self.y_send, self.y_recv, self.z_send, self.z_recv = sems
        h, odd = place.z // 2, place.z % 2
        self.h = h
        self.inner = odd + h - 2 * odd * h
        self.at_end, self.at_middle = self.inner == 0, self.inner == 1
        inward = place.row + NY * (1 - 2 * h)
        outward = place.row - NY * (1 - 2 * h)
        size = NZ * NY
        self.inward = (lax.rem(inward + size, size), place.col)
        self.outward = (lax.rem(outward + size, size), place.col)
        self.end_slot = (3 - 3 * h, 2 - h, 1 + 3 * h)
        self.middle_slot = (3 - 3 * h, 2 + 2 * h, 4 - h)
        self.middle_from = (3 - 3 * h, 2 - h, 3 * h)
        rows, cols = owned.shape
        self.grid = 2
        self.spec = pl.BlockSpec((rows // 2, cols), lambda i: (i, 0))

    def z_of(self, base):
        return base + self.h * (3 - 2 * base)

    def add(self, out, *terms, wide=1):
        def body(*refs):
            total = refs[0][...].astype(jnp.float32)
            for ref in refs[1:-1]:
                total = total + ref[...].astype(jnp.float32)
            refs[-1][...] = total.astype(jnp.bfloat16)

        rows, cols = self.owned.shape
        spec = pl.BlockSpec((rows // 2, wide * cols), lambda i: (i, 0))
        pltpu.emit_pipeline(body, grid=(2,), in_specs=[spec] * len(terms), out_specs=[spec])(*terms, out)

    def last_add(self, *terms):
        def body(*refs):
            total = refs[0][...].astype(jnp.float32)
            for ref in refs[1:-1]:
                total = total + ref[...].astype(jnp.float32)
            refs[-1][...] = total
            cols = total.shape[1]
            self.squares[0:1, 0:cols] += jnp.sum(total * total, axis=0, keepdims=True)

        pltpu.emit_pipeline(body, grid=(self.grid,), in_specs=[self.spec] * len(terms), out_specs=[self.spec])(
            *terms, self.owned
        )

    def got_z(self, slot, side=0):
        land = self.landing(slot, side)
        self.copies.arrive(land, self.z_send.at[0, side], self.z_recv.at[slot, side], self.place.at_up)


class FarGradSum(GradSum):
    def landing(self, slot, side):
        return self.from_z.at[slot]

    def turn_z(self, turn):
        base = (3, 2, 1 - self.inner, self.inner)[turn]
        return base + self.h * (3 - 2 * base)

    def start(self):
        p = self.place
        for turn in range(NZ):
            self.copies.send(
                self.view(self.full, self.turn_z(turn) * NY + (1 - p.y)), self.from_y.at[turn],
                self.y_send.at[turn], self.y_recv.at[turn], p.at_y,
            )

    def got_y(self, turn):
        self.copies.arrive(self.from_y.at[turn], self.y_send.at[turn], self.y_recv.at[turn], self.place.at_y)

    def hook(self, step):
        p = self.place
        if step < 3:

            @pl.when(self.at_end)
            def _():
                self.got_y(step)
                mine = self.view(self.full, self.z_of(self.ENDS[step]) * NY + p.y)
                self.add(self.from_y.at[step], mine, self.from_y.at[step])

            slot = self.end_slot[step]
            self.copies.send(
                self.from_y.at[step], self.from_z.at[slot], self.z_send.at[step, 0], self.z_recv.at[slot, 0],
                self.inward, self.at_end,
            )
        if step > 0:
            turn = step - 1

            @pl.when(self.at_middle)
            def _():
                self.got_y(turn)
                self.got_z(self.middle_from[turn])
                mine = self.view(self.full, self.z_of(self.MIDDLES[turn]) * NY + p.y)
                self.add(self.from_y.at[turn], mine, self.from_y.at[turn], self.from_z.at[self.middle_from[turn]])

            slot = self.middle_slot[turn]
            self.copies.send(
                self.from_y.at[turn], self.from_z.at[slot], self.z_send.at[turn, 1], self.z_recv.at[slot, 0],
                self.inward if turn < 2 else self.outward, self.at_middle,
            )

    def end(self):
        p = self.place
        self.got_y(3)
        mine = self.view(self.full, p.row)

        @pl.when(self.at_end)
        def _():
            self.got_z(4 - self.h)
            self.last_add(mine, self.from_y.at[3], self.from_z.at[4 - self.h])

        @pl.when(self.at_middle)
        def _():
            self.got_z(1 + self.h)
            self.got_z(4)
            self.last_add(mine, self.from_y.at[3], self.from_z.at[1 + self.h], self.from_z.at[4])


class NearGradSum(GradSum):
    def landing(self, slot, side):
        return self.from_z.at[slot] if side is None else self.from_z.at[slot, :, rows_of(side, OWN)]

    def pair(self, base):
        return self.full.at[:, rows_of(self.z_of(base), NY * OWN)]

    def got_pair(self, slot):
        self.copies.arrive(self.from_z.at[slot], self.z_send.at[0, 0], self.z_recv.at[slot, 0], self.place.at_up)

    def hook(self, step):
        if step < 3:
            slot = self.end_slot[step]
            self.copies.send(
                self.pair(self.ENDS[step]), self.from_z.at[slot], self.z_send.at[step, 0], self.z_recv.at[slot, 0],
                self.inward, self.at_end,
            )
        if step > 0:
            turn = step - 1
            here, slot = self.middle_from[turn], self.middle_slot[turn]

            @pl.when(self.at_middle)
            def _():
                self.got_pair(here)
                self.add(self.from_z.at[here], self.pair(self.MIDDLES[turn]), self.from_z.at[here], wide=NY)

            self.copies.send(
                self.from_z.at[here], self.from_z.at[slot], self.z_send.at[turn, 1], self.z_recv.at[slot, 0],
                self.inward if turn < 2 else self.outward, self.at_middle,
            )

    def cross(self):
        p = self.place
        side = 1 - p.y
        mine = self.view(self.full, p.row_y)

        @pl.when(self.at_end)
        def _():
            land = self.landing(4 - self.h, side)
            self.got_pair(4 - self.h)
            self.add(land, mine, land)

        @pl.when(self.at_middle)
        def _():
            land = self.landing(4, side)
            self.got_pair(1 + self.h)
            self.got_pair(4)
            self.add(land, mine, land, self.landing(1 + self.h, side))

        for slot, when in ((4 - self.h, self.at_end), (4, self.at_middle)):
            self.copies.send(
                self.landing(slot, side), self.from_y.at[0], self.y_send.at[0], self.y_recv.at[0], p.at_y, when
            )

    def end(self):
        p = self.place
        self.copies.arrive(self.from_y.at[0], self.y_send.at[0], self.y_recv.at[0], p.at_y)
        mine = self.view(self.full, p.row)

        @pl.when(self.at_end)
        def _():
            self.last_add(mine, self.from_y.at[0], self.landing(4 - self.h, p.y))

        @pl.when(self.at_middle)
        def _():
            self.last_add(mine, self.from_y.at[0], self.landing(1 + self.h, p.y), self.landing(4, p.y))


def backward_kernel(
    w_qkv, w_out, w_gu, w_down, attn_in, cot_full, ffn_in, qkv, heads, log_sums, resid, gate, up, hidden, down_grad,
    down_out, tokens, cot, gain, cosines, sines, seg_col, parent_col, seg_row,
    mixed, d_tokens, own_qkv, own_out, own_gu, own_down, totals_out,
    gate_grad, up_grad, out_back, proj_grad, gu_grad, out_grad, qkv_grad,
    y_qkv, y_out, y_gate, y_up, y_far, y_near, z_qkv, z_out, z_gate, z_up, z_far, z_near,
    partial, away, mine, from_core, from_x, mid, wide_buf, low_buf, near_buf, gain_buf, gain_sum, squares,
    key_sum, value_sum, grad_buf, stage, came, z_came, totals,
    r_ysend, r_yrecv, r_zsend, r_zrecv, t_send, t_recv, t_keep, u_send, u_recv, l_sem, n_send, n_recv,
):
    place = Place()
    copies = Copies()
    place.greet()

    def row_block(full, r):
        return full.at[rows_of(r, OWN), :]

    def col_block(full, r):
        return full.at[:, rows_of(r, OWN)]

    def grad_sum(kind, index, full, view, *refs):
        sems = (r_ysend.at[index], r_yrecv.at[index], r_zsend.at[index], r_zrecv.at[index])
        return kind(place, copies, full, view, *refs, squares, sems)

    half = WIDE // 2
    low_half, high_half = pl.ds(0, half), pl.ds(half, half)
    r_qkv = grad_sum(FarGradSum, 0, qkv_grad, row_block, y_qkv, z_qkv, own_qkv)
    r_out = grad_sum(FarGradSum, 1, out_grad, col_block, y_out, z_out, own_out)
    r_gate = grad_sum(FarGradSum, 2, gu_grad.at[0], row_block, y_gate, z_gate, own_gu.at[0])
    r_up = grad_sum(FarGradSum, 3, gu_grad.at[1], row_block, y_up, z_up, own_gu.at[1])
    r_far = grad_sum(FarGradSum, 4, down_grad.at[low_half, :], col_block, y_far, z_far, own_down.at[low_half, :])
    r_near = grad_sum(NearGradSum, 5, down_grad.at[high_half, :], col_block, y_near, z_near, own_down.at[high_half, :])
    a_back = [
        TokenGather(place, copies, out_back, m * TREE, t_send.at[m], t_recv.at[m]) for m in range(MICRO)
    ]

    def token_sum(turn, m):
        if turn == 1:
            blocks = lambda i: down_out.at[pl.ds(pl.multiple_of(m * TREE + i * OWN, OWN), OWN), :]
            far, near = away.at[m], mine.at[m]
        else:
            blocks = lambda i: partial.at[m, i]
            far, near = partial.at[m, place.col_x], partial.at[m, place.own]
        lands = 1 if turn == 1 else 0
        return TokenSum(
            place, copies, blocks, far, near, from_core.at[lands, m], from_x.at[lands, m], u_send.at[turn, m],
            u_recv.at[turn, m],
        )

    ffn_sum = [token_sum(0, m) for m in range(MICRO)]
    mlp_sum = [token_sum(1, m) for m in range(MICRO)]
    attn_sum = [token_sum(2, m) for m in range(MICRO)]

    def grad_hidden():
        def body(c_ref, w_ref, gate_ref, up_ref, gate_out, up_out):
            for part in range(WIDE // 512):
                cols = slice(part * 512, (part + 1) * 512)
                back = residual_mult * dot_nt(c_ref[...], w_ref[cols, :])
                gate_out[:, cols] = (back * gate_ref[:, cols].astype(jnp.float32)).astype(jnp.bfloat16)
                up_out[:, cols] = (back * up_ref[:, cols].astype(jnp.float32)).astype(jnp.bfloat16)

        rows = pl.BlockSpec((OWN, WIDE), lambda i: (i, 0))
        pltpu.emit_pipeline(
            body,
            grid=(MICRO * TREE // OWN,),
            in_specs=[rows, pl.BlockSpec((WIDE, D), lambda i: (0, 0)), rows, rows],
            out_specs=[rows, rows],
        )(cot_full, w_down, gate, up, gate_grad, up_grad)

    def grad_weight(near_all, far_all, out, near_cols, far_cols, side=None):
        def body(a_ref, b_ref, out_ref):
            out_ref[...] = dot_tn(a_ref[...], b_ref[...]).astype(jnp.bfloat16)

        def block(j):
            return j if side is None else j * NY + side

        pltpu.emit_pipeline(
            body,
            grid=(near_cols // OWN if side is None else NZ,),
            in_specs=[
                pl.BlockSpec((MICRO * TREE, OWN), lambda j: (0, block(j))),
                pl.BlockSpec((MICRO * TREE, far_cols), lambda j: (0, 0)),
            ],
            out_specs=[pl.BlockSpec((OWN, far_cols), lambda j: (block(j), 0))],
        )(near_all, far_all, out)

    def back_ffn(m):
        def body(step, g_ref, u_ref, wg_ref, wu_ref):
            for part in range(TREE // OWN):
                rows = slice(part * OWN, (part + 1) * OWN)
                value = dot_nt(g_ref[rows, :], wg_ref[0]) + dot_nt(u_ref[rows, :], wu_ref[0])
                partial[m, part, :, pl.ds(pl.multiple_of(step.index[0] * 256, 256), 256)] = value.astype(jnp.bfloat16)

        tree = pl.BlockSpec((TREE, WIDE), lambda j: (m, 0))
        pltpu.emit_pipeline(
            body,
            grid=(D // 256,),
            in_specs=[
                tree,
                tree,
                pl.BlockSpec((1, 256, WIDE), lambda j: (0, j, 0)),
                pl.BlockSpec((1, 256, WIDE), lambda j: (1, j, 0)),
            ],
            out_specs=[],
            _explicit_indices=True,
        )(gate_grad, up_grad, w_gu, w_gu)

    def back_attention(m):
        tree = pl.BlockSpec((TREE, 128), lambda g: (m, 0))
        group = pl.BlockSpec((TREE, 384), lambda g: (m, g))
        pltpu.emit_pipeline(
            functools.partial(attend_back, key_sum, value_sum, grad_buf),
            grid=(2,),
            in_specs=[
                pl.BlockSpec((TREE, D), lambda g: (m, 0)),
                pl.BlockSpec((256, D), lambda g: (g, 0)),
                pl.BlockSpec((TREE, 256), lambda g: (m, g)),
                pl.BlockSpec((4 * TREE, 128), lambda g: (m * 2 + g, 0)),
                group,
                tree,
                tree,
                tree,
                tree,
                pl.BlockSpec((8, TREE), lambda g: (m, 0)),
            ],
            out_specs=[group],
        )(out_back, w_out, heads, log_sums, qkv, cosines, sines, seg_col, parent_col, seg_row, proj_grad)

    def back_project(m):
        def body(step, a_ref, w_ref):
            partial[m, step.index[0]] = dot_nt(a_ref[...], w_ref[...]).astype(jnp.bfloat16)

        steps = TREE // OWN
        pltpu.emit_pipeline(
            body,
            grid=(steps,),
            in_specs=[
                pl.BlockSpec((OWN, 768), lambda i: (m * steps + i, 0)),
                pl.BlockSpec((D, 768), lambda i: (0, 0)),
            ],
            out_specs=[],
            _explicit_indices=True,
        )(proj_grad, w_qkv)

    def norm_back_rows(value, upstream, which):
        row_gain = gain_buf[which : which + 1, :]
        scale = lax.rsqrt(jnp.mean(value * value, axis=-1, keepdims=True) + norm_eps)
        scaled = upstream * row_gain
        inner = jnp.mean(scaled * value, axis=-1, keepdims=True)
        gain_sum[which : which + 1, :] += jnp.sum(upstream * value * scale, axis=0, keepdims=True)
        return scale * scaled - value * (scale * scale * scale * inner)

    def middle_back(m):
        ffn_sum[m].arrive()
        load = copies.local(resid.at[m], wide_buf, l_sem.at[0])
        load_low = copies.local(cot.at[m], low_buf, l_sem.at[1])
        load.wait()
        load_low.wait()

        @pl.loop(0, OWN // 16)
        def _(i):
            rows = rows_of(i, 16)
            back = norm_back_rows(wide_buf[rows, :], ffn_sum[m].rows(rows), 1)
            value = low_buf[rows, :].astype(jnp.float32) + back
            mid[m, rows, :] = value
            near_buf[m, rows, :] = (residual_mult * value).astype(jnp.bfloat16)

        a_back[m].start(near_buf.at[m], t_keep.at[m])

    def finish_mixed(m):
        mlp_sum[m].arrive()
        load = copies.local(resid.at[m], wide_buf, l_sem.at[0])
        load.wait()

        @pl.loop(0, OWN // 16)
        def _(i):
            rows = rows_of(i, 16)
            low_buf[rows, :] = (wide_buf[rows, :] + residual_mult * mlp_sum[m].rows(rows)).astype(jnp.bfloat16)

        copies.local(low_buf, mixed.at[m], l_sem.at[1]).wait()

    def finish_tokens(m):
        attn_sum[m].arrive()
        copies.local(tokens.at[m], low_buf, l_sem.at[1]).wait()

        @pl.loop(0, OWN // 16)
        def _(i):
            rows = rows_of(i, 16)
            back = norm_back_rows(low_buf[rows, :].astype(jnp.float32), attn_sum[m].rows(rows), 0)
            mid[m, rows, :] = mid[m, rows, :] + back

        return copies.local(mid.at[m], d_tokens.at[m], l_sem.at[2 + m])

    def sent(part):
        copies.close(part.sent)

    def sum_everywhere():
        stage[0] = jnp.zeros_like(stage[0])
        stage[0, 0:2, :] = gain_sum[0:2, :]
        stage[0, 2:3, :] = squares[0:1, :]
        for k, partner in enumerate((place.at_c, place.at_x, place.at_y)):
            copies.send(stage.at[k], came.at[k], n_send.at[k], n_recv.at[k], partner)
            copies.arrive(came.at[k], n_send.at[k], n_recv.at[k], partner)
            stage[k + 1] = stage[k] + came[k]
        last = stage.at[3]
        for off in range(1, NZ):
            copies.send(last, z_came.at[place.z], n_send.at[2 + off], n_recv.at[3 + place.z], place.at_z[off])
        z_came[place.z] = stage[3]
        for off in range(1, NZ):
            there = lax.rem(place.z + off, NZ)
            copies.arrive(z_came.at[there], n_send.at[2 + off], n_recv.at[3 + there], place.at_z[off])
        total = z_came[0]
        for there in range(1, NZ):
            total = total + z_came[there]
        gains_total = total[0:2]
        norm = jnp.sqrt(
            jnp.sum(total[2:3], axis=(0, 1), keepdims=True) + jnp.sum(gains_total * gains_total, axis=(0, 1), keepdims=True)
        )
        factor = jnp.minimum(1.0, clip_bound() / (norm + 1e-06))
        totals[...] = jnp.zeros_like(totals)
        totals[0:2, :] = gains_total
        totals[2:3, :] = jnp.broadcast_to(factor, (1, D))
        totals[3:4, :] = jnp.broadcast_to(norm, (1, D))

    def load_partial(m):
        return [
            copies.local(mlp_sum[m].blocks(place.col_x), away.at[m], l_sem.at[2 + 2 * m]),
            copies.local(mlp_sum[m].blocks(place.own), mine.at[m], l_sem.at[3 + 2 * m]),
        ]

    r_far.start()
    r_near.hook(0)
    mlp_sum[0].start()
    mlp_sum[1].start()
    load_gain = copies.local(gain, gain_buf, l_sem.at[0])
    parts = load_partial(0) + load_partial(1)
    gain_sum[...] = jnp.zeros_like(gain_sum)
    squares[...] = jnp.zeros_like(squares)
    load_gain.wait()
    for copy in parts:
        copy.wait()
    mlp_sum[0].middle()
    mlp_sum[1].middle()
    r_near.hook(1)
    r_far.hook(0)
    grad_hidden()
    grad_weight(ffn_in, gate_grad, gu_grad.at[0], D, WIDE)
    r_gate.start()
    r_far.hook(1)
    r_near.hook(2)
    r_far.hook(2)
    back_ffn(0)
    ffn_sum[0].start()
    r_near.hook(3)
    r_far.hook(3)
    back_ffn(1)
    ffn_sum[1].start()
    ffn_sum[0].middle()
    r_near.cross()
    r_gate.hook(0)
    grad_weight(ffn_in, up_grad, gu_grad.at[1], D, WIDE)
    r_up.start()
    ffn_sum[1].middle()
    r_gate.hook(1)
    middle_back(0)
    r_gate.hook(2)
    middle_back(1)
    finish_mixed(0)
    finish_mixed(1)
    a_back[0].relay()
    r_gate.hook(3)
    a_back[0].finish()
    back_attention(0)
    a_back[1].relay()
    r_up.hook(0)
    sent(ffn_sum[0])
    back_project(0)
    attn_sum[0].start()
    a_back[1].finish()
    grad_weight(heads, out_back, out_grad, 512, D)
    r_out.start()
    r_up.hook(1)
    back_attention(1)
    attn_sum[0].middle()
    r_up.hook(2)
    grad_weight(attn_in, proj_grad, qkv_grad, D, 768)
    r_qkv.start()
    r_up.hook(3)
    sent(ffn_sum[1])
    back_project(1)
    attn_sum[1].start()
    r_far.end()
    r_near.end()
    r_gate.end()
    attn_sum[1].middle()
    r_out.hook(0)
    r_out.hook(1)
    r_out.hook(2)
    r_out.hook(3)
    stores = [finish_tokens(0)]
    r_qkv.hook(0)
    r_qkv.hook(1)
    stores.append(finish_tokens(1))
    r_qkv.hook(2)
    r_qkv.hook(3)
    r_up.end()
    r_out.end()
    r_qkv.end()
    sum_everywhere()
    stores.append(copies.local(totals, totals_out, l_sem.at[1]))
    for copy in stores:
        copy.wait()
    copies.close()


def backward(saved, tokens, cot, gains, tables):
    low = jnp.bfloat16
    wide = jnp.float32
    shape = jax.ShapeDtypeStruct
    all_tokens = MICRO * TREE
    half = (WIDE // 2, OWN)
    blocks = [(OWN, 768), (512, OWN), (OWN, WIDE), (OWN, WIDE), half, half]
    outs = [shape((MICRO, OWN, D), low), shape((MICRO, OWN, D), wide)]
    outs += [shape(block, wide) for block in ((OWN, 768), (512, OWN), (2, OWN, WIDE), (WIDE, OWN))]
    outs += [shape((8, D), wide)]
    outs += [
        shape((all_tokens, WIDE), low), shape((all_tokens, WIDE), low), shape((all_tokens, D), low),
        shape((all_tokens, 768), low),
        shape((2, D, WIDE), low), shape((512, D), low), shape((D, 768), low),
    ]
    outs += [shape((NZ,) + block, low) for block in blocks[:5]]
    outs += [shape((1,) + blocks[5], low)]
    outs += [shape((NZ + 1,) + block, low) for block in blocks[:5]]
    outs += [shape((NZ + 1, WIDE // 2, NY * OWN), low)]
    dma = pltpu.SemaphoreType.DMA
    args = (*saved, tokens, cot, gains, *tables)
    return pl.pallas_call(
        backward_kernel,
        out_shape=outs,
        in_specs=[HBM] * len(args),
        out_specs=[HBM] * len(outs),
        scratch_shapes=[
            pltpu.VMEM((MICRO, NX * NC, OWN, D), low),
            pltpu.VMEM((MICRO, OWN, D), low),
            pltpu.VMEM((MICRO, OWN, D), low),
            pltpu.VMEM((2, MICRO, NX, OWN, D), low),
            pltpu.VMEM((2, MICRO, OWN, D), low),
            pltpu.VMEM((MICRO, OWN, D), wide),
            pltpu.VMEM((OWN, D), wide),
            pltpu.VMEM((OWN, D), low),
            pltpu.VMEM((MICRO, OWN, D), low),
            pltpu.VMEM((2, D), wide),
            pltpu.VMEM((8, D), wide),
            pltpu.VMEM((8, D), wide),
            pltpu.VMEM((TREE, 128), wide),
            pltpu.VMEM((TREE, 128), wide),
            pltpu.VMEM((TREE, 256), low),
            pltpu.VMEM((4, 8, D), wide),
            pltpu.VMEM((3, 8, D), wide),
            pltpu.VMEM((NZ, 8, D), wide),
            pltpu.VMEM((8, D), wide),
            dma((6, NZ)), dma((6, NZ)), dma((6, 3, 2)), dma((6, NZ + 1, 2)),
            dma((MICRO, 3)), dma((MICRO, NX * NC)), dma((MICRO,)),
            dma((3, MICRO, 3)), dma((3, MICRO, 3)), dma((6,)), dma((6,)), dma((3 + NZ,)),
        ],
        input_output_aliases={11: 7, 12: 8},
        compiler_params=pltpu.CompilerParams(
            collective_id=1, has_side_effects=True, vmem_limit_bytes=63 * 1024 * 1024
        ),
        cost_estimate=pl.CostEstimate(flops=140 * 10**9, bytes_accessed=5 * 10**8, transcendentals=10**7),
        name="backward",
    )(*args)


def update_kernel(
    g_qkv, g_out, g_gu, g_down, w_qkv, w_out, w_gu, w_down, mom_qkv, mom_out, mom_gu, mom_down, gains, mom_gains, totals,
    new_qkv, new_out, new_gu, new_down, moments_qkv, moments_out, moments_gu, moments_down,
    copy_qkv, copy_out, copy_gu, copy_down, new_gains, moments_gains,
):
    rates = step_rates()

    def step_of(grad, master, first, second, rate):
        clipped = totals[2:3, 0:1].reshape((1,) * grad.ndim) * grad
        first = beta_one * first + (1.0 - beta_one) * clipped
        second = beta_two * second + (1.0 - beta_two) * clipped * clipped
        first_hat = first / (1.0 - beta_one**STEP)
        second_hat = second / (1.0 - beta_two**STEP)
        updated = master - rate * (first_hat / (jnp.sqrt(second_hat) + adam_eps) + weight_decay * master)
        return updated, first, second

    def weight(rate, rows, grad, master, moments, new, new_moments, new_copy):
        def body(g_ref, w_ref, m_ref, new_ref, mom_ref, low_ref):
            updated, first, second = step_of(g_ref[...], w_ref[...], m_ref[0], m_ref[1], rate)
            new_ref[...] = updated
            mom_ref[0] = first
            mom_ref[1] = second
            low_ref[...] = updated.astype(jnp.bfloat16)

        rest = master.shape[1:]
        zeros = (0,) * len(rest)
        one = pl.BlockSpec((rows,) + rest, lambda i: (i,) + zeros)
        two = pl.BlockSpec((2, rows) + rest, lambda i: (0, i) + zeros)
        pltpu.emit_pipeline(
            body, grid=(master.shape[0] // rows,), in_specs=[one, one, two], out_specs=[one, two, one]
        )(grad, master, moments, new, new_moments, new_copy)

    weight(rates[2], 64, g_gu, w_gu, mom_gu, new_gu, moments_gu, copy_gu)
    weight(rates[3], 512, g_down, w_down, mom_down, new_down, moments_down, copy_down)
    weight(rates[1], 256, g_out, w_out, mom_out, new_out, moments_out, copy_out)
    weight(rates[0], 64, g_qkv, w_qkv, mom_qkv, new_qkv, moments_qkv, copy_qkv)
    updated, first, second = step_of(totals[0:2, :], gains[...], mom_gains[0], mom_gains[1], rates[4])
    new_gains[...] = updated
    moments_gains[0] = first
    moments_gains[1] = second


def update(grads, masters, states, gains, mom_gains, totals):
    shape = jax.ShapeDtypeStruct
    outs = [shape(master.shape, jnp.float32) for master in masters]
    outs += [shape(state.shape, jnp.float32) for state in states]
    outs += [shape(master.shape, jnp.bfloat16) for master in masters]
    outs += [shape(gains.shape, jnp.float32), shape(mom_gains.shape, jnp.float32)]
    whole = pl.BlockSpec(memory_space=pltpu.VMEM)
    return pl.pallas_call(
        update_kernel,
        out_shape=outs,
        in_specs=[HBM] * 12 + [whole] * 3,
        out_specs=[HBM] * 12 + [whole] * 2,
        compiler_params=pltpu.CompilerParams(vmem_limit_bytes=63 * 1024 * 1024),
        cost_estimate=pl.CostEstimate(flops=60 * 10**6, bytes_accessed=58 * 10**6, transcendentals=4 * 10**6),
        name="update",
    )(*grads, *masters, *states, gains, mom_gains, totals)


def fast_local(
    tokens,
    cotangent,
    segment_of,
    leaf_parent,
    w_qkv,
    mom_qkv,
    w_out,
    mom_out,
    w_gu,
    mom_gu,
    w_down,
    mom_down,
    gains,
    mom_gains,
):
    tables = [position_tables(segment_of[m], leaf_parent[m]) for m in range(MICRO)]
    tables = [jnp.concatenate([table[i] for table in tables], axis=0) for i in range(5)]
    saved = forward(tokens, cotangent, w_qkv, w_out, w_gu, w_down, gains, tables)
    mixed, d_tokens, g_qkv, g_out, g_gu, g_down, totals = backward(saved, tokens, cotangent, gains, tables)[:7]

    def flat(value, lead):
        return value.reshape(value.shape[:lead] + (-1, WIDE))

    masters = (w_qkv, w_out, flat(w_gu, 0), w_down)
    states = (mom_qkv, mom_out, flat(mom_gu, 1), mom_down)
    done = update(
        (g_qkv.reshape(w_qkv.shape), g_out, flat(g_gu, 0), g_down), masters, states, gains, mom_gains, totals
    )
    new, moments, copies = list(done[:4]), list(done[4:8]), list(done[8:12])
    new[2] = new[2].reshape(w_gu.shape)
    moments[2] = moments[2].reshape(mom_gu.shape)
    copies[2] = copies[2].reshape(w_gu.shape)
    results = []
    for i in range(4):
        results += [new[i], moments[i], copies[i]]
    return (mixed, d_tokens, totals[3, 0], *results, done[12], done[13])


def solution(mesh):
    placed = (
        P(None, ("row", "col"), None),
        P(None, ("row", "col"), None),
        P(None, "row"),
        P(None, "row"),
        P("row", "col", None),
        P(None, "row", "col", None),
        P("col", "row"),
        P(None, "col", "row"),
        P(None, "row", "col"),
        P(None, None, "row", "col"),
        P("col", "row"),
        P(None, "col", "row"),
        P(),
        P(),
    )
    sizes = dict(mesh.shape)
    fits = sizes == {"row": NZ * NY, "col": NX * NC}
    return jax.shard_map(
        fast_local if fits else local,
        mesh=mesh,
        in_specs=placed,
        out_specs=(
            P(None, ("row", "col"), None),
            P(None, ("row", "col"), None),
            P(),
            P("row", "col", None),
            P(None, "row", "col", None),
            P("row", "col", None),
            P("col", "row"),
            P(None, "col", "row"),
            P("col", "row"),
            P(None, "row", "col"),
            P(None, None, "row", "col"),
            P(None, "row", "col"),
            P("col", "row"),
            P(None, "col", "row"),
            P("col", "row"),
            P(),
            P(),
        ),
        check_vma=False,
    )
```

```python
import functools
import math

import jax
import jax.numpy as jnp
from jax import lax
from jax.experimental import pallas as pl
from jax.experimental.pallas import tpu as pltpu
from jax.sharding import PartitionSpec as P

D = 2048
FF = 8192
HD = 64
KVH = 8
GROUP = 4
NBRANCH = 4
NLEAF = 8
STEP = 7


norm_eps = 1e-05
residual_mult = 0.22
score_mult = 0.015625
rope_theta = 10000000.0
beta_one = 0.5
beta_two = 0.55
adam_eps = 1e-08
weight_decay = 0.1
masked_value = -1e30


def param_count():
    return D * KVH * (GROUP + 2) * HD + KVH * GROUP * HD * D + 3 * D * FF + 2 * D


def clip_bound():
    return math.sqrt(param_count())


def step_rates():
    return (
        max(D // 12, 1) ** (-0.5),
        max(D // 16, 1) ** (-0.5),
        D ** (-0.5),
        max(FF // 64, 1) ** (-0.5),
        0.3,
    )


def tree_tables(segments, parents):
    seg_count = 1 + NBRANCH + NLEAF
    seg_ids = jnp.arange(seg_count, dtype=jnp.int32)
    member = (segments[:, None] == seg_ids[None, :]).astype(jnp.int32)
    seg_lengths = jnp.sum(member, axis=0)
    seg_starts = jnp.cumsum(seg_lengths) - seg_lengths
    branch_ids = jnp.arange(NBRANCH, dtype=jnp.int32)
    parent_pick = (parents[:, None] == branch_ids[None, :]).astype(jnp.int32)
    parent_len = jnp.sum(parent_pick * seg_lengths[1 : 1 + NBRANCH][None, :], axis=1)
    trunk_len = seg_lengths[0]
    base_depth = jnp.concatenate(
        [
            jnp.zeros((1,), jnp.int32),
            trunk_len * jnp.ones((NBRANCH,), jnp.int32),
            trunk_len + parent_len,
        ]
    )
    places = jnp.arange(segments.shape[0], dtype=jnp.int32)
    depth = places + jnp.sum(member * (base_depth - seg_starts)[None, :], axis=1)
    identity = (seg_ids[:, None] == seg_ids[None, :]).astype(jnp.int32)
    rooted = jnp.broadcast_to((seg_ids[None, :] == 0).astype(jnp.int32), (seg_count, seg_count))
    leaf_links = jnp.concatenate(
        [jnp.zeros((NLEAF, 1), jnp.int32), parent_pick, jnp.zeros((NLEAF, NLEAF), jnp.int32)],
        axis=1,
    )
    leaf_links = jnp.concatenate(
        [jnp.zeros((1 + NBRANCH, seg_count), jnp.int32), leaf_links], axis=0
    )
    ancestry = jnp.minimum(identity + rooted + leaf_links, 1)
    token_path = jnp.dot(member, ancestry)
    allowed = (jnp.dot(token_path, member.T) > 0) & (depth[None, :] <= depth[:, None])
    freqs = jnp.exp(jnp.arange(HD // 2, dtype=jnp.float32) * (-2.0 * math.log(rope_theta) / HD))
    angles = depth.astype(jnp.float32)[:, None] * freqs[None, :]
    return (allowed, jnp.cos(angles), jnp.sin(angles))


def rotate(vectors, cosines, sines):
    half_width = vectors.shape[-1] // 2
    first_half = vectors[..., :half_width]
    second_half = vectors[..., half_width:]
    return jnp.concatenate(
        [first_half * cosines - second_half * sines, second_half * cosines + first_half * sines],
        axis=-1,
    )


def normalize(values, gain):
    scaling = lax.rsqrt(jnp.mean(values * values, axis=-1, keepdims=True) + norm_eps)
    return (values * scaling * gain, scaling)


def norm_back(values, scaling, gain, upstream):
    scaled = upstream * gain
    gain_grad = jnp.sum(upstream * values * scaling, axis=0)
    inner = jnp.mean(scaled * values, axis=-1, keepdims=True)
    return (scaling * scaled - values * scaling * scaling * scaling * inner, gain_grad)


def gather_forward(values):
    return lax.all_gather(values, "col", axis=0, tiled=True)


def gather_backward(values):
    return lax.all_gather(values, "col", axis=0, tiled=True)


def sum_forward(term_fn, row_count):
    return lax.psum_scatter(
        term_fn(jnp.int32(0), lax.axis_size("col") * row_count).astype(jnp.bfloat16),
        "col",
        scatter_dimension=0,
        tiled=True,
    ).astype(jnp.float32)


def sum_backward(term_fn, row_count):
    return lax.psum_scatter(
        term_fn(jnp.int32(0), lax.axis_size("col") * row_count).astype(jnp.bfloat16),
        "col",
        scatter_dimension=0,
        tiled=True,
    ).astype(jnp.float32)


def adamw(master, moments, raw_grad, factor, step_rate):
    clipped = factor * raw_grad
    first_moment = beta_one * moments[0] + (1.0 - beta_one) * clipped
    second_moment = beta_two * moments[1] + (1.0 - beta_two) * clipped * clipped
    first_hat = first_moment / (1.0 - beta_one**STEP)
    second_hat = second_moment / (1.0 - beta_two**STEP)
    updated = master - step_rate * (
        first_hat / (jnp.sqrt(second_hat) + adam_eps) + weight_decay * master
    )
    return (updated, jnp.stack([first_moment, second_moment]))


def local(
    tokens,
    cotangent,
    segment_of,
    leaf_parent,
    w_qkv,
    mom_qkv,
    w_out,
    mom_out,
    w_gu,
    mom_gu,
    w_down,
    mom_down,
    gains,
    mom_gains,
):
    low_shards = (
        w_qkv.astype(jnp.bfloat16),
        w_out.astype(jnp.bfloat16),
        w_gu.astype(jnp.bfloat16),
        w_down.astype(jnp.bfloat16),
    )

    def fetch():
        return (
            lax.all_gather(low_shards[0], "row", axis=0, tiled=True),
            lax.all_gather(low_shards[1], "row", axis=1, tiled=True),
            lax.all_gather(low_shards[2], "row", axis=1, tiled=True),
            lax.all_gather(low_shards[3], "row", axis=1, tiled=True),
        )

    outputs = []
    input_grads = []
    owned = None
    unsummed = None
    gain_partial = None
    for batch_index in range(tokens.shape[0]):
        x_local = tokens[batch_index].astype(jnp.float32)
        row_count = x_local.shape[0]
        allowed, cosines, sines = tree_tables(segment_of[batch_index], leaf_parent[batch_index])
        w_a, w_b, w_c, w_d = fetch()
        normed_a, scale_a = normalize(x_local, gains[0])
        attn_in = gather_forward(normed_a.astype(jnp.bfloat16))
        projected = jnp.einsum("td,dkf->tkf", attn_in, w_a, preferred_element_type=jnp.float32)
        tree_len = projected.shape[0]
        groups = projected.shape[1]
        queries = rotate(
            projected[:, :, : GROUP * HD].reshape(tree_len, groups, GROUP, HD),
            cosines[:, None, None, :],
            sines[:, None, None, :],
        ).astype(jnp.bfloat16)
        key_heads = rotate(
            projected[:, :, GROUP * HD : (GROUP + 1) * HD], cosines[:, None, :], sines[:, None, :]
        ).astype(jnp.bfloat16)
        values = projected[:, :, (GROUP + 1) * HD :].astype(jnp.bfloat16)
        scores = jnp.einsum(
            "tkgh,skh->kgts", queries, key_heads, preferred_element_type=jnp.float32
        )
        logits = jnp.where(allowed, score_mult * scores, masked_value)
        row_peak = jnp.max(logits, axis=-1, keepdims=True)
        exp_terms = jnp.exp(logits - row_peak)
        exp_total = jnp.sum(exp_terms, axis=-1, keepdims=True)
        log_total = row_peak + jnp.log(exp_total)
        attn_probs = exp_terms / exp_total
        mixed_heads = (
            jnp.einsum(
                "kgts,skh->tkgh",
                attn_probs.astype(jnp.bfloat16),
                values,
                preferred_element_type=jnp.float32,
            )
            .astype(jnp.bfloat16)
            .reshape(tree_len, -1)
        )

        def out_terms(first_row, row_total):
            return jnp.dot(mixed_heads, w_b, preferred_element_type=jnp.float32)

        attn_sum = sum_forward(out_terms, row_count)
        residual_mid = x_local + residual_mult * attn_sum
        normed_b, scale_b = normalize(residual_mid, gains[1])
        ffn_in = gather_forward(normed_b.astype(jnp.bfloat16))
        gate_up = jnp.einsum("td,edf->tef", ffn_in, w_c, preferred_element_type=jnp.float32)
        gate_act = jax.nn.sigmoid(gate_up[:, 0])
        silu_gate = gate_up[:, 0] * gate_act
        hidden = (silu_gate * gate_up[:, 1]).astype(jnp.bfloat16)

        def down_terms(first_row, row_total):
            return jnp.dot(hidden, w_d, preferred_element_type=jnp.float32)

        mlp_sum = sum_forward(down_terms, row_count)
        outputs.append((residual_mid + residual_mult * mlp_sum).astype(jnp.bfloat16))
        w_a, w_b, w_c, w_d = fetch()
        cot_full = gather_backward(cotangent[batch_index])
        hidden_grad = residual_mult * jnp.einsum(
            "td,fd->tf", cot_full, w_d, preferred_element_type=jnp.float32
        )
        down_grad = residual_mult * jnp.einsum(
            "tf,td->fd", hidden, cot_full, preferred_element_type=jnp.float32
        )
        gate_grad = (
            hidden_grad * gate_up[:, 1] * gate_act * (1.0 + gate_up[:, 0] * (1.0 - gate_act))
        )
        up_grad = hidden_grad * silu_gate
        gate_up_grad = jnp.stack([gate_grad, up_grad], axis=1).astype(jnp.bfloat16)
        gu_grad = jnp.einsum(
            "td,tef->edf", ffn_in, gate_up_grad, preferred_element_type=jnp.float32
        )

        def ffn_back_terms(first_row, row_total):
            return jnp.einsum("tef,edf->td", gate_up_grad, w_c, preferred_element_type=jnp.float32)

        ffn_in_grad = sum_backward(ffn_back_terms, row_count)
        mid_norm_grad, gain_b_grad = norm_back(residual_mid, scale_b, gains[1], ffn_in_grad)
        mid_grad = cotangent[batch_index].astype(jnp.float32) + mid_norm_grad
        attn_out_grad = gather_backward((residual_mult * mid_grad).astype(jnp.bfloat16))
        out_grad = jnp.einsum(
            "tf,td->fd", mixed_heads, attn_out_grad, preferred_element_type=jnp.float32
        )
        heads_grad = (
            jnp.einsum("td,fd->tf", attn_out_grad, w_b, preferred_element_type=jnp.float32)
            .astype(jnp.bfloat16)
            .reshape(tree_len, groups, GROUP, HD)
        )
        attn_probs = jnp.exp(logits - log_total)
        prob_grad = jnp.einsum(
            "tkgh,skh->kgts", heads_grad, values, preferred_element_type=jnp.float32
        )
        row_inner = jnp.sum(prob_grad * attn_probs, axis=-1, keepdims=True)
        score_grad = (score_mult * attn_probs * (prob_grad - row_inner)).astype(jnp.bfloat16)
        query_grad = jnp.einsum(
            "kgts,skh->tkgh", score_grad, key_heads, preferred_element_type=jnp.float32
        )
        key_grad = jnp.einsum(
            "kgts,tkgh->skh", score_grad, queries, preferred_element_type=jnp.float32
        )
        value_grad = jnp.einsum(
            "kgts,tkgh->skh",
            attn_probs.astype(jnp.bfloat16),
            heads_grad,
            preferred_element_type=jnp.float32,
        )
        query_grad = rotate(query_grad, cosines[:, None, None, :], -sines[:, None, None, :])
        key_grad = rotate(key_grad, cosines[:, None, :], -sines[:, None, :])
        proj_grad = jnp.concatenate(
            [query_grad.reshape(tree_len, groups, GROUP * HD), key_grad, value_grad], axis=-1
        ).astype(jnp.bfloat16)
        qkv_grad = jnp.einsum("td,tkf->dkf", attn_in, proj_grad, preferred_element_type=jnp.float32)

        def attn_back_terms(first_row, row_total):
            return jnp.einsum("tkf,dkf->td", proj_grad, w_a, preferred_element_type=jnp.float32)

        attn_in_grad = sum_backward(attn_back_terms, row_count)
        input_norm_grad, gain_a_grad = norm_back(x_local, scale_a, gains[0], attn_in_grad)
        input_grads.append(mid_grad + input_norm_grad)
        gain_step = jnp.stack([gain_a_grad, gain_b_grad])
        gain_partial = gain_step if gain_partial is None else gain_partial + gain_step
        partials = (qkv_grad, out_grad, gu_grad, down_grad)
        unsummed = (
            partials
            if unsummed is None
            else tuple((running + addend for running, addend in zip(unsummed, partials)))
        )
    owned = (
        lax.psum_scatter(
            unsummed[0].astype(jnp.bfloat16), "row", scatter_dimension=0, tiled=True
        ).astype(jnp.float32),
        lax.psum_scatter(
            unsummed[1].astype(jnp.bfloat16), "row", scatter_dimension=1, tiled=True
        ).astype(jnp.float32),
        lax.psum_scatter(
            unsummed[2].astype(jnp.bfloat16), "row", scatter_dimension=1, tiled=True
        ).astype(jnp.float32),
        lax.psum_scatter(
            unsummed[3].astype(jnp.bfloat16), "row", scatter_dimension=1, tiled=True
        ).astype(jnp.float32),
    )
    local_squares = jnp.float32(0.0)
    for grad_piece in owned:
        local_squares = local_squares + jnp.sum(grad_piece * grad_piece)
    total_squares, gain_total = lax.psum((local_squares, gain_partial), ("row", "col"))
    grad_norm = jnp.sqrt(total_squares + jnp.sum(gain_total * gain_total))
    factor = jnp.minimum(1.0, clip_bound() / (grad_norm + 1e-06))
    rates = step_rates()
    masters = (w_qkv, w_out, w_gu, w_down)
    states = (mom_qkv, mom_out, mom_gu, mom_down)
    results = []
    for index_w in range(4):
        updated, moments = adamw(
            masters[index_w], states[index_w], owned[index_w], factor, rates[index_w]
        )
        results.append((updated, moments, updated.astype(jnp.bfloat16)))
    new_gains, moments_gains = adamw(gains, mom_gains, gain_total, factor, rates[4])
    mixed = jnp.stack(outputs, axis=0)
    d_tokens = jnp.stack(input_grads, axis=0)
    return (
        mixed,
        d_tokens,
        grad_norm,
        results[0][0],
        results[0][1],
        results[0][2],
        results[1][0],
        results[1][1],
        results[1][2],
        results[2][0],
        results[2][1],
        results[2][2],
        results[3][0],
        results[3][1],
        results[3][2],
        new_gains,
        moments_gains,
    )


def position_tables(segments, parents):
    seg_ids = jnp.arange(1 + NBRANCH + NLEAF, dtype=jnp.int32)
    member = (segments[:, None] == seg_ids[None, :]).astype(jnp.int32)
    seg_lengths = jnp.sum(member, axis=0)
    seg_starts = jnp.cumsum(seg_lengths) - seg_lengths
    parent_of = jnp.concatenate([jnp.full((1 + NBRANCH,), -1, jnp.int32), 1 + parents])
    branch_ids = jnp.arange(NBRANCH, dtype=jnp.int32)
    parent_pick = (parents[:, None] == branch_ids[None, :]).astype(jnp.int32)
    parent_len = jnp.sum(parent_pick * seg_lengths[1 : 1 + NBRANCH][None, :], axis=1)
    base_depth = jnp.concatenate(
        [
            jnp.zeros((1,), jnp.int32),
            seg_lengths[0] * jnp.ones((NBRANCH,), jnp.int32),
            seg_lengths[0] + parent_len,
        ]
    )
    places = jnp.arange(segments.shape[0], dtype=jnp.int32)
    depth = places + jnp.sum(member * (base_depth - seg_starts)[None, :], axis=1)
    parent = jnp.sum(member * parent_of[None, :], axis=1)
    freqs = jnp.exp(jnp.arange(HD // 2, dtype=jnp.float32) * (-2.0 * math.log(rope_theta) / HD))
    angles = depth.astype(jnp.float32)[:, None] * freqs[None, :]
    cosines, sines = jnp.cos(angles), jnp.sin(angles)
    return (
        jnp.concatenate([cosines] * 4, axis=1),
        jnp.concatenate([-sines, sines] * 2, axis=1),
        jnp.broadcast_to(segments[:, None].astype(jnp.float32), (segments.shape[0], 128)),
        jnp.broadcast_to(parent[:, None].astype(jnp.float32), (segments.shape[0], 128)),
        jnp.broadcast_to(segments[None, :].astype(jnp.float32), (8, segments.shape[0])),
    )

def dot_nn(a, b):
    return lax.dot_general(a, b, (((1,), (0,)), ((), ())), preferred_element_type=jnp.float32)


def dot_nt(a, b):
    return lax.dot_general(a, b, (((1,), (1,)), ((), ())), preferred_element_type=jnp.float32)


def dot_tn(a, b):
    return lax.dot_general(a, b, (((0,), (0,)), ((), ())), preferred_element_type=jnp.float32)


MICRO = 2
TREE = 1024
OWN = 256
WIDE = 2048
NX, NC, NZ, NY = 2, 2, 4, 2
SEG = 128
MESH = pl.DeviceIdType.MESH
HBM = pl.BlockSpec(memory_space=pl.ANY)


class Place:
    def __init__(self):
        row, col = lax.axis_index("row"), lax.axis_index("col")
        self.row, self.col = row, col
        self.z, self.y = row // NY, row % NY
        self.x, self.c = col // NC, col % NC
        self.own = col
        self.row_z = [lax.rem(row + NY * off, NZ * NY) for off in range(NZ)]
        self.row_y = self.z * NY + (1 - self.y)
        self.row_yz = [lax.rem(self.z + off, NZ) * NY + (1 - self.y) for off in range(NZ)]
        self.col_x = (1 - self.x) * NC + self.c
        self.col_c = self.x * NC + (1 - self.c)
        self.col_xc = (1 - self.x) * NC + (1 - self.c)
        self.at_z = [None] + [(self.row_z[off], col) for off in range(1, NZ)]
        self.at_up = (lax.rem(row + NY, NZ * NY), col)
        self.at_down = (lax.rem(row + (NZ - 1) * NY, NZ * NY), col)
        self.at_y = (self.row_y, col)
        self.at_x = (row, self.col_x)
        self.at_c = (row, self.col_c)

    def greet(self):
        barrier = pltpu.get_barrier_semaphore()
        partners = self.at_z[1:] + [self.at_y, self.at_x, self.at_c]
        for partner in partners:
            pl.semaphore_signal(barrier, inc=1, device_id=partner, device_id_type=MESH)
        pl.semaphore_wait(barrier, len(partners))


class Copies:
    def __init__(self):
        self.open_sends = []

    def send(self, src, dst, send_sem, recv_sem, device, when=True):
        copy = pltpu.make_async_remote_copy(
            src_ref=src, dst_ref=dst, send_sem=send_sem, recv_sem=recv_sem,
            device_id=device, device_id_type=MESH,
        )
        if when is True:
            copy.start()
        else:
            pl.when(when)(copy.start)
        self.open_sends.append((copy, when))
        return copy

    def arrive(self, dst, send_sem, recv_sem, device, when=True):
        copy = pltpu.make_async_remote_copy(
            src_ref=dst, dst_ref=dst, send_sem=send_sem, recv_sem=recv_sem,
            device_id=device, device_id_type=MESH,
        )
        if when is True:
            copy.wait_recv()
        else:
            pl.when(when)(copy.wait_recv)

    def local(self, src, dst, sem):
        copy = pltpu.make_async_copy(src, dst, sem)
        copy.start()
        return copy

    def close(self, some=None):
        left = []
        for copy, when in self.open_sends:
            if some is not None and not any(copy is one for one in some):
                left.append((copy, when))
            elif when is True:
                copy.wait_send()
            else:
                pl.when(when)(copy.wait_send)
        self.open_sends = left


def rows_of(index, size):
    return pl.ds(pl.multiple_of(index * size, size), size)


class WeightGather:
    def __init__(self, place, copies, own, full, view, send, recv, keep, over_y_first):
        self.place, self.copies, self.own, self.full, self.view = place, copies, own, full, view
        self.send, self.recv, self.keep = send, recv, keep
        self.sides = (place.y, 1 - place.y) if over_y_first else (place.y,)
        self.over_y_first = over_y_first

    def block(self, r):
        return self.view(self.full, r)

    def pass_on(self, src, r, up, down, over_y):
        p = self.place
        here = self.block(r)
        if up is not None:
            self.copies.send(src, here, self.send.at[0, r], self.recv.at[r], p.at_up, up)
        if down is not None:
            self.copies.send(src, here, self.send.at[1, r], self.recv.at[r], p.at_down, down)
        if over_y is not None:
            self.copies.send(src, here, self.send.at[2, r], self.recv.at[r], p.at_y, over_y)

    def start_y(self):
        p = self.place
        self.kept = self.copies.local(self.own, self.block(p.row), self.keep)
        self.pass_on(self.own, p.row, None, None, True)

    def start_z(self):
        p = self.place
        self.pass_on(self.own, p.row, p.z < NZ - 1, p.z > 0, None)

    def arrive(self, r, when=True):
        self.copies.arrive(self.block(r), self.send.at[2, r], self.recv.at[r], self.place.at_y, when)

    def relay_y(self):
        p = self.place
        self.arrive(p.row_y)
        self.pass_on(self.block(p.row_y), p.row_y, p.z < NZ - 1, p.z > 0, None)

    def relay(self, k):
        p = self.place
        for there, upward in ((p.z - k, True), (p.z + k, False)):
            came = there >= 0 if upward else there < NZ
            safe = lax.rem(there + NZ, NZ)
            for side in self.sides:
                r = safe * NY + side
                self.arrive(r, came)
                on = jnp.logical_and(came, p.z < NZ - 1) if upward else jnp.logical_and(came, p.z > 0)
                self.pass_on(
                    self.block(r), r, on if upward else None, None if upward else on, None if self.over_y_first else came
                )

    def finish(self):
        if not self.over_y_first:
            for off in range(NZ):
                self.arrive(self.place.row_yz[off])
        if self.kept is not None:
            self.keep_own()

    def keep_own(self):
        self.kept.wait()
        self.kept = None


class TokenGather:
    def __init__(self, place, copies, full, base, send, recv):
        self.place, self.copies, self.full, self.base = place, copies, full, base
        self.send, self.recv = send, recv

    def block(self, index):
        return self.full.at[pl.ds(pl.multiple_of(self.base + index * OWN, OWN), OWN), :]

    def start(self, own, keep):
        p = self.place
        here = self.block(p.own)
        self.kept = self.copies.local(own, here, keep)
        self.copies.send(own, here, self.send.at[0], self.recv.at[p.own], p.at_x)
        self.copies.send(own, here, self.send.at[1], self.recv.at[p.own], p.at_c)

    def relay(self):
        p = self.place
        block = self.block(p.col_x)
        self.copies.arrive(block, self.send.at[2], self.recv.at[p.col_x], p.at_c)
        self.copies.send(block, block, self.send.at[2], self.recv.at[p.col_x], p.at_c)

    def finish(self):
        p = self.place
        for index in (p.col_c, p.col_xc):
            self.copies.arrive(self.block(index), self.send.at[2], self.recv.at[index], p.at_c)
        self.kept.wait()


class TokenSum:
    def __init__(self, place, copies, blocks, away, mine, from_core, from_x, send, recv):
        self.place, self.copies, self.blocks, self.away, self.mine = place, copies, blocks, away, mine
        self.from_core, self.from_x, self.send, self.recv = from_core, from_x, send, recv

    def start(self):
        p = self.place
        self.sent = []
        for there in range(NX):
            self.sent.append(
                self.copies.send(
                    self.blocks(there * NC + (1 - p.c)), self.from_core.at[there],
                    self.send.at[there], self.recv.at[there], p.at_c,
                )
            )

    def middle(self):
        p = self.place
        for there in range(NX):
            self.copies.arrive(self.from_core.at[there], self.send.at[there], self.recv.at[there], p.at_c)
        other = 1 - p.x

        @pl.loop(0, OWN // 32)
        def _(i):
            rows = rows_of(i, 32)
            self.away[rows, :] = (
                self.away[rows, :].astype(jnp.float32) + self.from_core[other, rows, :].astype(jnp.float32)
            ).astype(jnp.bfloat16)

        self.sent.append(self.copies.send(self.away, self.from_x, self.send.at[2], self.recv.at[2], p.at_x))

    def arrive(self):
        p = self.place
        self.copies.arrive(self.from_x, self.send.at[2], self.recv.at[2], p.at_x)

    def rows(self, rows):
        p = self.place
        return (
            self.mine[rows, :].astype(jnp.float32)
            + self.from_core[p.x, rows, :].astype(jnp.float32)
            + self.from_x[rows, :].astype(jnp.float32)
        )


def swap_halves(tile):
    lane = lax.broadcasted_iota(jnp.int32, tile.shape, 1)
    return jnp.where(lane % HD < HD // 2, pltpu.roll(tile, 128 - HD // 2, 1), pltpu.roll(tile, HD // 2, 1))


def masked_parts(run, seg_col, parent_col, seg_row):
    rows = slice(run * SEG, (run + 1) * SEG)

    def causal():
        shape = (SEG, 2 * SEG)
        return lax.broadcasted_iota(jnp.int32, shape, 1) <= lax.broadcasted_iota(jnp.int32, shape, 0) + run * SEG

    def of_parent():
        return seg_row[0:1, 2 * SEG : 4 * SEG] == parent_col[rows, 0:1]

    def of_run():
        shape = (SEG, SEG)
        order = lax.broadcasted_iota(jnp.int32, shape, 1) <= lax.broadcasted_iota(jnp.int32, shape, 0)
        return order & (seg_row[0:1, rows] == seg_col[rows, 0:1])

    if run < 2:
        return [(slice(0, 2 * SEG), causal())]
    parts = [(slice(0, 2 * SEG), None)]
    if run >= 4:
        parts.append((slice(2 * SEG, 4 * SEG), of_parent()))
    parts.append((rows, of_run()))
    return parts


def softmax_parts(scores):
    peak = None
    for score in scores:
        top = jnp.max(score, axis=-1, keepdims=True)
        peak = top if peak is None else jnp.maximum(peak, top)
    peak = peak * score_mult
    exps = [jnp.exp(score * score_mult - peak) for score in scores]
    total = None
    for term in exps:
        part = jnp.sum(term, axis=-1, keepdims=True)
        total = part if total is None else total + part
    return exps, total, peak + jnp.log(total)


def stacked_pairs(tile_ref, rows):
    both = jnp.concatenate([tile_ref[rows, 0:128], tile_ref[rows, 128:256]], axis=0)
    lane = lax.broadcasted_iota(jnp.int32, both.shape, 1)
    zero = jnp.zeros_like(both)
    return jnp.concatenate([jnp.where(lane < HD, both, zero), jnp.where(lane < HD, zero, both)], axis=0)


def unstack_pairs(wide):
    half = wide.shape[0] // 2
    lane = lax.broadcasted_iota(jnp.int32, (half, 128), 1)
    return jnp.where(lane < HD, wide[:half], wide[half:])


def twice(kv):
    wide = kv.astype(jnp.float32)
    lane = lax.broadcasted_iota(jnp.int32, wide.shape, 1)
    other = pltpu.roll(wide, HD, 1)
    key = jnp.where(lane < HD, wide, other)
    value = jnp.where(lane < HD, other, wide)
    return key.astype(jnp.bfloat16), value.astype(jnp.bfloat16)


def score_parts(queries, keys, parts):
    scores = []
    for span, mask in parts:
        score = dot_nt(queries, keys[span])
        if mask is not None:
            score = jnp.where(jnp.concatenate([mask] * 4, axis=0), score, masked_value)
        scores.append(score)
    return scores


def attend(qkv_ref, seg_col_ref, parent_col_ref, seg_row_ref, heads_ref, log_ref):
    seg_row = seg_row_ref[...]
    keys, values = twice(qkv_ref[:, 256:384])
    for run in range(TREE // SEG):
        rows = slice(run * SEG, (run + 1) * SEG)
        parts = masked_parts(run, seg_col_ref, parent_col_ref, seg_row)
        exps, total, log_total = softmax_parts(score_parts(stacked_pairs(qkv_ref, rows), keys, parts))
        mixed = None
        for (span, _), term in zip(parts, exps):
            got = dot_nn(term.astype(jnp.bfloat16), values[span])
            mixed = got if mixed is None else mixed + got
        low = unstack_pairs(mixed * (1.0 / total)).astype(jnp.bfloat16)
        heads_ref[rows, 0:128] = low[0:SEG]
        heads_ref[rows, 128:256] = low[SEG:]
        log_ref[run * 4 * SEG : (run + 1) * 4 * SEG, :] = jnp.broadcast_to(log_total, (4 * SEG, 128))


def attend_back(
    key_sum, value_sum, grad_buf, back_ref, w_ref, heads_ref, log_ref, qkv_ref, cos_ref, sin_ref, seg_col_ref,
    parent_col_ref, seg_row_ref, out_ref,
):
    for part in range(TREE // OWN):
        rows = slice(part * OWN, (part + 1) * OWN)
        grad_buf[rows, :] = dot_nt(back_ref[rows, :], w_ref[...]).astype(jnp.bfloat16)
    seg_row = seg_row_ref[...]
    keys, values = twice(qkv_ref[:, 256:384])
    key_sum[...] = jnp.zeros_like(key_sum)
    value_sum[...] = jnp.zeros_like(value_sum)
    for run in range(TREE // SEG):
        rows = slice(run * SEG, (run + 1) * SEG)
        parts = masked_parts(run, seg_col_ref, parent_col_ref, seg_row)
        queries = stacked_pairs(qkv_ref, rows)
        upstream = stacked_pairs(grad_buf, rows)
        mixed = stacked_pairs(heads_ref, rows)
        inner = jnp.sum(upstream.astype(jnp.float32) * mixed.astype(jnp.float32), axis=-1, keepdims=True)
        log_total = log_ref[run * 4 * SEG : (run + 1) * 4 * SEG, 0:1]
        query_grad = None
        for (span, _), score in zip(parts, score_parts(queries, keys, parts)):
            prob = jnp.exp(score * score_mult - log_total)
            prob_grad = dot_nt(upstream, values[span])
            score_grad = (prob * (prob_grad - inner)).astype(jnp.bfloat16)
            term = dot_nn(score_grad, keys[span])
            query_grad = term if query_grad is None else query_grad + term
            key_sum[span, :] += dot_tn(score_grad, queries)
            value_sum[span, :] += dot_tn(prob.astype(jnp.bfloat16), upstream)
        pair_grad = unstack_pairs(query_grad) * score_mult
        cos, sin = cos_ref[rows, :], sin_ref[rows, :]
        for tile in range(2):
            part = pair_grad[tile * SEG : (tile + 1) * SEG]
            out_ref[rows, tile * 128 : (tile + 1) * 128] = (part * cos - swap_halves(part) * sin).astype(jnp.bfloat16)
    key_grad = key_sum[...] * score_mult
    key_grad = key_grad + pltpu.roll(key_grad, HD, 1)
    value_grad = value_sum[...]
    value_grad = value_grad + pltpu.roll(value_grad, HD, 1)
    turned = key_grad * cos_ref[...] - swap_halves(key_grad) * sin_ref[...]
    lane = lax.broadcasted_iota(jnp.int32, turned.shape, 1)
    out_ref[:, 256:384] = jnp.where(lane < HD, turned, value_grad).astype(jnp.bfloat16)


def forward_kernel(
    tokens, cot, own_qkv, own_out, own_gu, own_down, gain, cosines, sines, seg_col, parent_col, seg_row,
    w_qkv, w_out, w_gu, w_down, attn_in, cot_full, ffn_in, qkv, heads, log_sums, resid, gate, up, hidden, down_grad,
    down_out,
    partial, from_core, from_x, normed_buf, tokens_buf, cot_buf, near_buf, gain_buf,
    wide_qkv, wide_out, wide_gu, wide_down, low_qkv, low_out, low_gu, low_down,
    w_send, w_recv, w_keep, t_send, t_recv, t_keep, s_send, s_recv, l_sem,
):
    resid_buf = wide_gu
    place = Place()
    copies = Copies()
    pairs = (
        (own_qkv, wide_qkv), (tokens, tokens_buf), (gain, gain_buf), (own_out, wide_out),
        (own_gu, wide_gu), (cot, cot_buf), (own_down, wide_down),
    )
    loads = [copies.local(src, dst, l_sem.at[i]) for i, (src, dst) in enumerate(pairs)]
    place.greet()

    def row_block(full, r):
        return full.at[rows_of(r, OWN), :]

    def col_block(full, r):
        return full.at[:, rows_of(r, OWN)]

    def weight(index, own, full, view, over_y_first):
        return WeightGather(
            place, copies, own, full, view, w_send.at[index], w_recv.at[index], w_keep.at[index], over_y_first
        )

    g_qkv = weight(0, low_qkv, w_qkv, row_block, True)
    g_out = weight(1, low_out, w_out, col_block, True)
    g_gate = weight(2, low_gu.at[0], w_gu.at[0], row_block, False)
    g_up = weight(3, low_gu.at[1], w_gu.at[1], row_block, False)
    g_down = weight(4, low_down, w_down, col_block, False)

    def token_gather(index, full, m):
        return TokenGather(place, copies, full, m * TREE, t_send.at[index], t_recv.at[index])

    a_in = [token_gather(m, attn_in, m) for m in range(MICRO)]
    a_cot = [token_gather(2 + m, cot_full, m) for m in range(MICRO)]
    a_ffn = [token_gather(4 + m, ffn_in, m) for m in range(MICRO)]
    sums = [
        TokenSum(
            place, copies, functools.partial(lambda m, i: partial.at[m, i], m), partial.at[m, place.col_x],
            partial.at[m, place.own], from_core.at[m], from_x.at[m], s_send.at[m], s_recv.at[m],
        )
        for m in range(MICRO)
    ]

    def project(m):
        def body(a_ref, w_ref, cos_ref, sin_ref, out_ref):
            got = dot_nn(a_ref[...], w_ref[...])
            cos, sin = cos_ref[...], sin_ref[...]
            lane = lax.broadcasted_iota(jnp.int32, cos.shape, 1)
            cos_key = jnp.where(lane < HD, cos, 1.0)
            sin_key = jnp.where(lane < HD, sin, 0.0)
            for tile in range(got.shape[1] // 128):
                part = got[:, tile * 128 : (tile + 1) * 128]
                is_key = tile % 3 == 2
                turned = part * (cos_key if is_key else cos) + swap_halves(part) * (sin_key if is_key else sin)
                out_ref[:, tile * 128 : (tile + 1) * 128] = turned.astype(jnp.bfloat16)

        steps = TREE // OWN
        rows = pl.BlockSpec((OWN, D), lambda i: (m * steps + i, 0))
        table = pl.BlockSpec((OWN, 128), lambda i: (m * steps + i, 0))
        out = pl.BlockSpec((OWN, 768), lambda i: (m * steps + i, 0))
        whole = pl.BlockSpec((D, 768), lambda i: (0, 0))
        pltpu.emit_pipeline(body, grid=(steps,), in_specs=[rows, whole, table, table], out_specs=[out])(
            attn_in, w_qkv, cosines, sines, qkv
        )

    def attention(m):
        tree = pl.BlockSpec((TREE, 128), lambda g: (m, 0))
        pltpu.emit_pipeline(
            attend,
            grid=(2,),
            in_specs=[
                pl.BlockSpec((TREE, 384), lambda g: (m, g)),
                tree,
                tree,
                pl.BlockSpec((8, TREE), lambda g: (m, 0)),
            ],
            out_specs=[
                pl.BlockSpec((TREE, 256), lambda g: (m, g)),
                pl.BlockSpec((4 * TREE, 128), lambda g: (m * 2 + g, 0)),
            ],
        )(qkv, seg_col, parent_col, seg_row, heads, log_sums)

    def out_project(m):
        def body_at(step, a_ref, w_ref):
            partial[m, step.index[0]] = dot_nn(a_ref[...], w_ref[...]).astype(jnp.bfloat16)

        steps = TREE // OWN
        pltpu.emit_pipeline(
            body_at,
            grid=(steps,),
            in_specs=[
                pl.BlockSpec((OWN, 512), lambda i: (m * steps + i, 0)),
                pl.BlockSpec((512, D), lambda i: (0, 0)),
            ],
            out_specs=[],
            _explicit_indices=True,
        )(heads, w_out)

    def lower(wide, low):
        step = 64

        @pl.loop(0, wide.shape[0] // step)
        def _(i):
            rows = rows_of(i, step)
            low[rows, :] = wide[rows, :].astype(jnp.bfloat16)

    def first_norm(m):
        @pl.loop(0, OWN // 32)
        def _(i):
            rows = rows_of(i, 32)
            value = tokens_buf[m, rows, :].astype(jnp.float32)
            scale = lax.rsqrt(jnp.mean(value * value, axis=-1, keepdims=True) + norm_eps)
            near_buf[m, rows, :] = (value * scale * gain_buf[0:1, :]).astype(jnp.bfloat16)

        a_in[m].start(near_buf.at[m], t_keep.at[m])

    def middle_norm(m):
        sums[m].arrive()

        @pl.loop(0, OWN // 32)
        def _(i):
            rows = rows_of(i, 32)
            value = tokens_buf[m, rows, :].astype(jnp.float32) + residual_mult * sums[m].rows(rows)
            resid_buf[m, rows, :] = value
            scale = lax.rsqrt(jnp.mean(value * value, axis=-1, keepdims=True) + norm_eps)
            normed_buf[m, rows, :] = (value * scale * gain_buf[1:2, :]).astype(jnp.bfloat16)

        a_ffn[m].start(normed_buf.at[m], t_keep.at[4 + m])
        return copies.local(resid_buf.at[m], resid.at[m], l_sem.at[m])

    def project_gate(m):
        def body(a_ref, g_ref, gate_ref):
            for part in range(TREE // OWN):
                rows = slice(part * OWN, (part + 1) * OWN)
                gate_ref[rows, :] = dot_nn(a_ref[rows, :], g_ref[0]).astype(jnp.bfloat16)

        pltpu.emit_pipeline(
            body,
            grid=(WIDE // 256,),
            in_specs=[
                pl.BlockSpec((TREE, D), lambda j: (m, 0)),
                pl.BlockSpec((1, D, 256), lambda j: (0, 0, j)),
            ],
            out_specs=[pl.BlockSpec((TREE, 256), lambda j: (m, j))],
        )(ffn_in, w_gu, gate)

    def project_up(m):
        def body(a_ref, u_ref, g_ref, gate_ref, up_ref, hidden_ref):
            for part in range(TREE // OWN):
                rows = slice(part * OWN, (part + 1) * OWN)
                u = dot_nn(a_ref[rows, :], u_ref[0])
                g = g_ref[rows, :].astype(jnp.float32)
                act = jax.nn.sigmoid(g)
                silu = g * act
                gate_ref[rows, :] = (u * act * (1.0 + g * (1.0 - act))).astype(jnp.bfloat16)
                up_ref[rows, :] = silu.astype(jnp.bfloat16)
                hidden_ref[rows, :] = (silu * u).astype(jnp.bfloat16)

        cols = pl.BlockSpec((TREE, 256), lambda j: (m, j))
        pltpu.emit_pipeline(
            body,
            grid=(WIDE // 256,),
            in_specs=[
                pl.BlockSpec((TREE, D), lambda j: (m, 0)),
                pl.BlockSpec((1, D, 256), lambda j: (1, 0, j)),
                cols,
            ],
            out_specs=[cols, cols, cols],
        )(ffn_in, w_gu, gate, gate, up, hidden)

    def grad_down():
        def body(h_ref, c_ref, out_ref):
            out_ref[...] = (residual_mult * dot_tn(h_ref[...], c_ref[...])).astype(jnp.bfloat16)

        pltpu.emit_pipeline(
            body,
            grid=(WIDE // 256,),
            in_specs=[
                pl.BlockSpec((MICRO * TREE, 256), lambda i: (0, i)),
                pl.BlockSpec((MICRO * TREE, D), lambda i: (0, 0)),
            ],
            out_specs=[pl.BlockSpec((256, D), lambda i: (i, 0))],
        )(hidden, cot_full, down_grad)

    def down(m, near):
        def body(h_ref, w_ref, out_ref):
            for part in range(TREE // OWN):
                rows = slice(part * OWN, (part + 1) * OWN)
                out_ref[rows, :] = dot_nn(h_ref[rows, :], w_ref[...]).astype(jnp.bfloat16)

        side = place.y if near else 1 - place.y
        pltpu.emit_pipeline(
            body,
            grid=(NZ,),
            in_specs=[
                pl.BlockSpec((TREE, WIDE), lambda j: (m, 0)),
                pl.BlockSpec((WIDE, OWN), lambda j: (0, j * NY + side)),
            ],
            out_specs=[pl.BlockSpec((TREE, OWN), lambda j: (m, j * NY + side))],
        )(hidden, w_down, down_out)

    g_qkv_load, tokens_load, gain_load, out_load, gu_load, cot_load, down_load = loads
    g_qkv_load.wait()
    lower(wide_qkv, low_qkv)
    g_qkv.start_y()
    g_qkv.start_z()
    out_load.wait()
    lower(wide_out, low_out)
    g_out.start_y()
    g_out.start_z()
    tokens_load.wait()
    gain_load.wait()
    for m in range(MICRO):
        first_norm(m)
    gu_load.wait()
    lower(wide_gu.at[0], low_gu.at[0])
    g_gate.start_y()
    g_qkv.relay_y()
    g_out.relay_y()
    lower(wide_gu.at[1], low_gu.at[1])
    g_up.start_y()
    cot_load.wait()
    for m in range(MICRO):
        a_cot[m].start(cot_buf.at[m], t_keep.at[2 + m])
    down_load.wait()
    lower(wide_down, low_down)
    g_down.start_y()
    a_in[0].relay()
    g_qkv.relay(1)
    g_out.relay(1)
    a_in[1].relay()
    g_qkv.relay(2)
    g_out.relay(2)
    g_gate.start_z()
    a_in[0].finish()
    a_in[1].finish()
    a_cot[0].relay()
    g_qkv.relay(3)
    g_qkv.finish()
    project(0)
    g_out.relay(3)
    g_out.finish()
    g_gate.relay(1)
    project(1)
    a_cot[1].relay()
    attention(0)
    g_gate.relay(2)
    g_up.start_z()
    out_project(0)
    sums[0].start()
    attention(1)
    sums[0].middle()
    out_project(1)
    sums[1].start()
    g_gate.relay(3)
    sums[1].middle()
    stored = [middle_norm(0)]
    g_up.relay(1)
    stored.append(middle_norm(1))
    a_ffn[0].relay()
    g_up.relay(2)
    g_down.start_z()
    g_gate.finish()
    a_ffn[0].finish()
    project_gate(0)
    a_ffn[1].relay()
    g_up.relay(3)
    g_down.relay(1)
    a_ffn[1].finish()
    project_gate(1)
    a_cot[0].finish()
    a_cot[1].finish()
    g_up.finish()
    project_up(0)
    g_down.relay(2)
    project_up(1)
    g_down.relay(3)
    g_down.keep_own()
    down(0, True)
    down(1, True)
    grad_down()
    g_down.finish()
    down(0, False)
    down(1, False)
    for copy in stored:
        copy.wait()
    copies.close()


def forward(tokens, cot, w_qkv, w_out, w_gu, w_down, gains, tables):
    low = jnp.bfloat16
    wide = jnp.float32
    shape = jax.ShapeDtypeStruct
    all_tokens = MICRO * TREE
    outs = [
        shape((D, 768), low), shape((512, D), low), shape((2, D, WIDE), low), shape((WIDE, D), low),
        shape((all_tokens, D), low), shape((all_tokens, D), low), shape((all_tokens, D), low),
        shape((all_tokens, 768), low), shape((all_tokens, 512), low), shape((2 * MICRO * 4 * TREE, 128), wide),
        shape((MICRO, OWN, D), wide),
        shape((all_tokens, WIDE), low), shape((all_tokens, WIDE), low), shape((all_tokens, WIDE), low),
        shape((WIDE, D), low), shape((all_tokens, D), low),
    ]
    dma = pltpu.SemaphoreType.DMA
    blocks = [(OWN, 768), (512, OWN), (2, OWN, WIDE), (WIDE, OWN)]
    scratch = [
        pltpu.VMEM((MICRO, NX * NC, OWN, D), low),
        pltpu.VMEM((MICRO, NX, OWN, D), low),
        pltpu.VMEM((MICRO, OWN, D), low),
        pltpu.VMEM((MICRO, OWN, D), low),
        pltpu.VMEM((MICRO, OWN, D), low),
        pltpu.VMEM((MICRO, OWN, D), low),
        pltpu.VMEM((MICRO, OWN, D), low),
        pltpu.VMEM((2, D), wide),
    ]
    scratch += [pltpu.VMEM(block, wide) for block in blocks]
    scratch += [pltpu.VMEM(block, low) for block in blocks]
    scratch += [
        dma((5, 3, NZ * NY)), dma((5, NZ * NY)), dma((5,)),
        dma((6, 3)), dma((6, NX * NC)), dma((6,)),
        dma((MICRO, 3)), dma((MICRO, 3)), dma((7,)),
    ]
    return pl.pallas_call(
        forward_kernel,
        out_shape=outs,
        in_specs=[HBM] * 12,
        out_specs=[HBM] * len(outs),
        scratch_shapes=scratch,
        compiler_params=pltpu.CompilerParams(
            collective_id=0, has_side_effects=True, vmem_limit_bytes=63 * 1024 * 1024
        ),
        cost_estimate=pl.CostEstimate(flops=90 * 10**9, bytes_accessed=2 * 10**8, transcendentals=10**7),
        name="forward",
    )(tokens, cot, w_qkv.reshape(OWN, 768), w_out, w_gu, w_down, gains, *tables)


class GradSum:
    ENDS = (3, 2, 1)
    MIDDLES = (3, 2, 0)

    def __init__(self, place, copies, full, view, from_y, from_z, owned, squares, sems):
        self.place, self.copies, self.full, self.view = place, copies, full, view
        self.from_y, self.from_z, self.owned = from_y, from_z, owned
        self.squares = squares
        self.y_send, self.y_recv, self.z_send, self.z_recv = sems
        h, odd = place.z // 2, place.z % 2
        self.h = h
        self.inner = odd + h - 2 * odd * h
        self.at_end, self.at_middle = self.inner == 0, self.inner == 1
        inward = place.row + NY * (1 - 2 * h)
        outward = place.row - NY * (1 - 2 * h)
        size = NZ * NY
        self.inward = (lax.rem(inward + size, size), place.col)
        self.outward = (lax.rem(outward + size, size), place.col)
        self.end_slot = (3 - 3 * h, 2 - h, 1 + 3 * h)
        self.middle_slot = (3 - 3 * h, 2 + 2 * h, 4 - h)
        self.middle_from = (3 - 3 * h, 2 - h, 3 * h)
        rows, cols = owned.shape
        self.grid = 2
        self.spec = pl.BlockSpec((rows // 2, cols), lambda i: (i, 0))

    def z_of(self, base):
        return base + self.h * (3 - 2 * base)

    def add(self, out, *terms, wide=1):
        def body(*refs):
            total = refs[0][...].astype(jnp.float32)
            for ref in refs[1:-1]:
                total = total + ref[...].astype(jnp.float32)
            refs[-1][...] = total.astype(jnp.bfloat16)

        rows, cols = self.owned.shape
        spec = pl.BlockSpec((rows // 2, wide * cols), lambda i: (i, 0))
        pltpu.emit_pipeline(body, grid=(2,), in_specs=[spec] * len(terms), out_specs=[spec])(*terms, out)

    def last_add(self, *terms):
        def body(*refs):
            total = refs[0][...].astype(jnp.float32)
            for ref in refs[1:-1]:
                total = total + ref[...].astype(jnp.float32)
            refs[-1][...] = total
            cols = total.shape[1]
            self.squares[0:1, 0:cols] += jnp.sum(total * total, axis=0, keepdims=True)

        pltpu.emit_pipeline(body, grid=(self.grid,), in_specs=[self.spec] * len(terms), out_specs=[self.spec])(
            *terms, self.owned
        )

    def got_z(self, slot, side=0):
        land = self.landing(slot, side)
        self.copies.arrive(land, self.z_send.at[0, side], self.z_recv.at[slot, side], self.place.at_up)


class FarGradSum(GradSum):
    def landing(self, slot, side):
        return self.from_z.at[slot]

    def turn_z(self, turn):
        base = (3, 2, 1 - self.inner, self.inner)[turn]
        return base + self.h * (3 - 2 * base)

    def start(self):
        p = self.place
        for turn in range(NZ):
            self.copies.send(
                self.view(self.full, self.turn_z(turn) * NY + (1 - p.y)), self.from_y.at[turn],
                self.y_send.at[turn], self.y_recv.at[turn], p.at_y,
            )

    def got_y(self, turn):
        self.copies.arrive(self.from_y.at[turn], self.y_send.at[turn], self.y_recv.at[turn], self.place.at_y)

    def hook(self, step):
        p = self.place
        if step < 3:

            @pl.when(self.at_end)
            def _():
                self.got_y(step)
                mine = self.view(self.full, self.z_of(self.ENDS[step]) * NY + p.y)
                self.add(self.from_y.at[step], mine, self.from_y.at[step])

            slot = self.end_slot[step]
            self.copies.send(
                self.from_y.at[step], self.from_z.at[slot], self.z_send.at[step, 0], self.z_recv.at[slot, 0],
                self.inward, self.at_end,
            )
        if step > 0:
            turn = step - 1

            @pl.when(self.at_middle)
            def _():
                self.got_y(turn)
                self.got_z(self.middle_from[turn])
                mine = self.view(self.full, self.z_of(self.MIDDLES[turn]) * NY + p.y)
                self.add(self.from_y.at[turn], mine, self.from_y.at[turn], self.from_z.at[self.middle_from[turn]])

            slot = self.middle_slot[turn]
            self.copies.send(
                self.from_y.at[turn], self.from_z.at[slot], self.z_send.at[turn, 1], self.z_recv.at[slot, 0],
                self.inward if turn < 2 else self.outward, self.at_middle,
            )

    def end(self):
        p = self.place
        self.got_y(3)
        mine = self.view(self.full, p.row)

        @pl.when(self.at_end)
        def _():
            self.got_z(4 - self.h)
            self.last_add(mine, self.from_y.at[3], self.from_z.at[4 - self.h])

        @pl.when(self.at_middle)
        def _():
            self.got_z(1 + self.h)
            self.got_z(4)
            self.last_add(mine, self.from_y.at[3], self.from_z.at[1 + self.h], self.from_z.at[4])


class NearGradSum(GradSum):
    def landing(self, slot, side):
        return self.from_z.at[slot] if side is None else self.from_z.at[slot, :, rows_of(side, OWN)]

    def pair(self, base):
        return self.full.at[:, rows_of(self.z_of(base), NY * OWN)]

    def got_pair(self, slot):
        self.copies.arrive(self.from_z.at[slot], self.z_send.at[0, 0], self.z_recv.at[slot, 0], self.place.at_up)

    def hook(self, step):
        if step < 3:
            slot = self.end_slot[step]
            self.copies.send(
                self.pair(self.ENDS[step]), self.from_z.at[slot], self.z_send.at[step, 0], self.z_recv.at[slot, 0],
                self.inward, self.at_end,
            )
        if step > 0:
            turn = step - 1
            here, slot = self.middle_from[turn], self.middle_slot[turn]

            @pl.when(self.at_middle)
            def _():
                self.got_pair(here)
                self.add(self.from_z.at[here], self.pair(self.MIDDLES[turn]), self.from_z.at[here], wide=NY)

            self.copies.send(
                self.from_z.at[here], self.from_z.at[slot], self.z_send.at[turn, 1], self.z_recv.at[slot, 0],
                self.inward if turn < 2 else self.outward, self.at_middle,
            )

    def cross(self):
        p = self.place
        side = 1 - p.y
        mine = self.view(self.full, p.row_y)

        @pl.when(self.at_end)
        def _():
            land = self.landing(4 - self.h, side)
            self.got_pair(4 - self.h)
            self.add(land, mine, land)

        @pl.when(self.at_middle)
        def _():
            land = self.landing(4, side)
            self.got_pair(1 + self.h)
            self.got_pair(4)
            self.add(land, mine, land, self.landing(1 + self.h, side))

        for slot, when in ((4 - self.h, self.at_end), (4, self.at_middle)):
            self.copies.send(
                self.landing(slot, side), self.from_y.at[0], self.y_send.at[0], self.y_recv.at[0], p.at_y, when
            )

    def end(self):
        p = self.place
        self.copies.arrive(self.from_y.at[0], self.y_send.at[0], self.y_recv.at[0], p.at_y)
        mine = self.view(self.full, p.row)

        @pl.when(self.at_end)
        def _():
            self.last_add(mine, self.from_y.at[0], self.landing(4 - self.h, p.y))

        @pl.when(self.at_middle)
        def _():
            self.last_add(mine, self.from_y.at[0], self.landing(1 + self.h, p.y), self.landing(4, p.y))


def backward_kernel(
    w_qkv, w_out, w_gu, w_down, attn_in, cot_full, ffn_in, qkv, heads, log_sums, resid, gate, up, hidden, down_grad,
    down_out, tokens, cot, gain, cosines, sines, seg_col, parent_col, seg_row,
    mixed, d_tokens, own_qkv, own_out, own_gu, own_down, totals_out,
    gate_grad, up_grad, out_back, proj_grad, gu_grad, out_grad, qkv_grad,
    y_qkv, y_out, y_gate, y_up, y_far, y_near, z_qkv, z_out, z_gate, z_up, z_far, z_near,
    partial, away, mine, from_core, from_x, mid, wide_buf, low_buf, near_buf, gain_buf, gain_sum, squares,
    key_sum, value_sum, grad_buf, stage, came, z_came, totals,
    r_ysend, r_yrecv, r_zsend, r_zrecv, t_send, t_recv, t_keep, u_send, u_recv, l_sem, n_send, n_recv,
):
    place = Place()
    copies = Copies()
    place.greet()

    def row_block(full, r):
        return full.at[rows_of(r, OWN), :]

    def col_block(full, r):
        return full.at[:, rows_of(r, OWN)]

    def grad_sum(kind, index, full, view, *refs):
        sems = (r_ysend.at[index], r_yrecv.at[index], r_zsend.at[index], r_zrecv.at[index])
        return kind(place, copies, full, view, *refs, squares, sems)

    half = WIDE // 2
    low_half, high_half = pl.ds(0, half), pl.ds(half, half)
    r_qkv = grad_sum(FarGradSum, 0, qkv_grad, row_block, y_qkv, z_qkv, own_qkv)
    r_out = grad_sum(FarGradSum, 1, out_grad, col_block, y_out, z_out, own_out)
    r_gate = grad_sum(FarGradSum, 2, gu_grad.at[0], row_block, y_gate, z_gate, own_gu.at[0])
    r_up = grad_sum(FarGradSum, 3, gu_grad.at[1], row_block, y_up, z_up, own_gu.at[1])
    r_far = grad_sum(FarGradSum, 4, down_grad.at[low_half, :], col_block, y_far, z_far, own_down.at[low_half, :])
    r_near = grad_sum(NearGradSum, 5, down_grad.at[high_half, :], col_block, y_near, z_near, own_down.at[high_half, :])
    a_back = [
        TokenGather(place, copies, out_back, m * TREE, t_send.at[m], t_recv.at[m]) for m in range(MICRO)
    ]

    def token_sum(turn, m):
        if turn == 1:
            blocks = lambda i: down_out.at[pl.ds(pl.multiple_of(m * TREE + i * OWN, OWN), OWN), :]
            far, near = away.at[m], mine.at[m]
        else:
            blocks = lambda i: partial.at[m, i]
            far, near = partial.at[m, place.col_x], partial.at[m, place.own]
        lands = 1 if turn == 1 else 0
        return TokenSum(
            place, copies, blocks, far, near, from_core.at[lands, m], from_x.at[lands, m], u_send.at[turn, m],
            u_recv.at[turn, m],
        )

    ffn_sum = [token_sum(0, m) for m in range(MICRO)]
    mlp_sum = [token_sum(1, m) for m in range(MICRO)]
    attn_sum = [token_sum(2, m) for m in range(MICRO)]

    def grad_hidden():
        def body(c_ref, w_ref, gate_ref, up_ref, gate_out, up_out):
            for part in range(WIDE // 512):
                cols = slice(part * 512, (part + 1) * 512)
                back = residual_mult * dot_nt(c_ref[...], w_ref[cols, :])
                gate_out[:, cols] = (back * gate_ref[:, cols].astype(jnp.float32)).astype(jnp.bfloat16)
                up_out[:, cols] = (back * up_ref[:, cols].astype(jnp.float32)).astype(jnp.bfloat16)

        rows = pl.BlockSpec((OWN, WIDE), lambda i: (i, 0))
        pltpu.emit_pipeline(
            body,
            grid=(MICRO * TREE // OWN,),
            in_specs=[rows, pl.BlockSpec((WIDE, D), lambda i: (0, 0)), rows, rows],
            out_specs=[rows, rows],
        )(cot_full, w_down, gate, up, gate_grad, up_grad)

    def grad_weight(near_all, far_all, out, near_cols, far_cols, side=None):
        def body(a_ref, b_ref, out_ref):
            out_ref[...] = dot_tn(a_ref[...], b_ref[...]).astype(jnp.bfloat16)

        def block(j):
            return j if side is None else j * NY + side

        pltpu.emit_pipeline(
            body,
            grid=(near_cols // OWN if side is None else NZ,),
            in_specs=[
                pl.BlockSpec((MICRO * TREE, OWN), lambda j: (0, block(j))),
                pl.BlockSpec((MICRO * TREE, far_cols), lambda j: (0, 0)),
            ],
            out_specs=[pl.BlockSpec((OWN, far_cols), lambda j: (block(j), 0))],
        )(near_all, far_all, out)

    def back_ffn(m):
        def body(step, g_ref, u_ref, wg_ref, wu_ref):
            for part in range(TREE // OWN):
                rows = slice(part * OWN, (part + 1) * OWN)
                value = dot_nt(g_ref[rows, :], wg_ref[0]) + dot_nt(u_ref[rows, :], wu_ref[0])
                partial[m, part, :, pl.ds(pl.multiple_of(step.index[0] * 256, 256), 256)] = value.astype(jnp.bfloat16)

        tree = pl.BlockSpec((TREE, WIDE), lambda j: (m, 0))
        pltpu.emit_pipeline(
            body,
            grid=(D // 256,),
            in_specs=[
                tree,
                tree,
                pl.BlockSpec((1, 256, WIDE), lambda j: (0, j, 0)),
                pl.BlockSpec((1, 256, WIDE), lambda j: (1, j, 0)),
            ],
            out_specs=[],
            _explicit_indices=True,
        )(gate_grad, up_grad, w_gu, w_gu)

    def back_attention(m):
        tree = pl.BlockSpec((TREE, 128), lambda g: (m, 0))
        group = pl.BlockSpec((TREE, 384), lambda g: (m, g))
        pltpu.emit_pipeline(
            functools.partial(attend_back, key_sum, value_sum, grad_buf),
            grid=(2,),
            in_specs=[
                pl.BlockSpec((TREE, D), lambda g: (m, 0)),
                pl.BlockSpec((256, D), lambda g: (g, 0)),
                pl.BlockSpec((TREE, 256), lambda g: (m, g)),
                pl.BlockSpec((4 * TREE, 128), lambda g: (m * 2 + g, 0)),
                group,
                tree,
                tree,
                tree,
                tree,
                pl.BlockSpec((8, TREE), lambda g: (m, 0)),
            ],
            out_specs=[group],
        )(out_back, w_out, heads, log_sums, qkv, cosines, sines, seg_col, parent_col, seg_row, proj_grad)

    def back_project(m):
        def body(step, a_ref, w_ref):
            partial[m, step.index[0]] = dot_nt(a_ref[...], w_ref[...]).astype(jnp.bfloat16)

        steps = TREE // OWN
        pltpu.emit_pipeline(
            body,
            grid=(steps,),
            in_specs=[
                pl.BlockSpec((OWN, 768), lambda i: (m * steps + i, 0)),
                pl.BlockSpec((D, 768), lambda i: (0, 0)),
            ],
            out_specs=[],
            _explicit_indices=True,
        )(proj_grad, w_qkv)

    def norm_back_rows(value, upstream, which):
        row_gain = gain_buf[which : which + 1, :]
        scale = lax.rsqrt(jnp.mean(value * value, axis=-1, keepdims=True) + norm_eps)
        scaled = upstream * row_gain
        inner = jnp.mean(scaled * value, axis=-1, keepdims=True)
        gain_sum[which : which + 1, :] += jnp.sum(upstream * value * scale, axis=0, keepdims=True)
        return scale * scaled - value * (scale * scale * scale * inner)

    def middle_back(m):
        ffn_sum[m].arrive()
        load = copies.local(resid.at[m], wide_buf, l_sem.at[0])
        load_low = copies.local(cot.at[m], low_buf, l_sem.at[1])
        load.wait()
        load_low.wait()

        @pl.loop(0, OWN // 16)
        def _(i):
            rows = rows_of(i, 16)
            back = norm_back_rows(wide_buf[rows, :], ffn_sum[m].rows(rows), 1)
            value = low_buf[rows, :].astype(jnp.float32) + back
            mid[m, rows, :] = value
            near_buf[m, rows, :] = (residual_mult * value).astype(jnp.bfloat16)

        a_back[m].start(near_buf.at[m], t_keep.at[m])

    def finish_mixed(m):
        mlp_sum[m].arrive()
        load = copies.local(resid.at[m], wide_buf, l_sem.at[0])
        load.wait()

        @pl.loop(0, OWN // 16)
        def _(i):
            rows = rows_of(i, 16)
            low_buf[rows, :] = (wide_buf[rows, :] + residual_mult * mlp_sum[m].rows(rows)).astype(jnp.bfloat16)

        copies.local(low_buf, mixed.at[m], l_sem.at[1]).wait()

    def finish_tokens(m):
        attn_sum[m].arrive()
        copies.local(tokens.at[m], low_buf, l_sem.at[1]).wait()

        @pl.loop(0, OWN // 16)
        def _(i):
            rows = rows_of(i, 16)
            back = norm_back_rows(low_buf[rows, :].astype(jnp.float32), attn_sum[m].rows(rows), 0)
            mid[m, rows, :] = mid[m, rows, :] + back

        return copies.local(mid.at[m], d_tokens.at[m], l_sem.at[2 + m])

    def sent(part):
        copies.close(part.sent)

    def sum_everywhere():
        stage[0] = jnp.zeros_like(stage[0])
        stage[0, 0:2, :] = gain_sum[0:2, :]
        stage[0, 2:3, :] = squares[0:1, :]
        for k, partner in enumerate((place.at_c, place.at_x, place.at_y)):
            copies.send(stage.at[k], came.at[k], n_send.at[k], n_recv.at[k], partner)
            copies.arrive(came.at[k], n_send.at[k], n_recv.at[k], partner)
            stage[k + 1] = stage[k] + came[k]
        last = stage.at[3]
        for off in range(1, NZ):
            copies.send(last, z_came.at[place.z], n_send.at[2 + off], n_recv.at[3 + place.z], place.at_z[off])
        z_came[place.z] = stage[3]
        for off in range(1, NZ):
            there = lax.rem(place.z + off, NZ)
            copies.arrive(z_came.at[there], n_send.at[2 + off], n_recv.at[3 + there], place.at_z[off])
        total = z_came[0]
        for there in range(1, NZ):
            total = total + z_came[there]
        gains_total = total[0:2]
        norm = jnp.sqrt(
            jnp.sum(total[2:3], axis=(0, 1), keepdims=True) + jnp.sum(gains_total * gains_total, axis=(0, 1), keepdims=True)
        )
        factor = jnp.minimum(1.0, clip_bound() / (norm + 1e-06))
        totals[...] = jnp.zeros_like(totals)
        totals[0:2, :] = gains_total
        totals[2:3, :] = jnp.broadcast_to(factor, (1, D))
        totals[3:4, :] = jnp.broadcast_to(norm, (1, D))

    def load_partial(m):
        return [
            copies.local(mlp_sum[m].blocks(place.col_x), away.at[m], l_sem.at[2 + 2 * m]),
            copies.local(mlp_sum[m].blocks(place.own), mine.at[m], l_sem.at[3 + 2 * m]),
        ]

    r_far.start()
    r_near.hook(0)
    mlp_sum[0].start()
    mlp_sum[1].start()
    load_gain = copies.local(gain, gain_buf, l_sem.at[0])
    parts = load_partial(0) + load_partial(1)
    gain_sum[...] = jnp.zeros_like(gain_sum)
    squares[...] = jnp.zeros_like(squares)
    load_gain.wait()
    for copy in parts:
        copy.wait()
    mlp_sum[0].middle()
    mlp_sum[1].middle()
    r_near.hook(1)
    r_far.hook(0)
    grad_hidden()
    grad_weight(ffn_in, gate_grad, gu_grad.at[0], D, WIDE)
    r_gate.start()
    r_far.hook(1)
    r_near.hook(2)
    r_far.hook(2)
    back_ffn(0)
    ffn_sum[0].start()
    r_near.hook(3)
    r_far.hook(3)
    back_ffn(1)
    ffn_sum[1].start()
    ffn_sum[0].middle()
    r_near.cross()
    r_gate.hook(0)
    grad_weight(ffn_in, up_grad, gu_grad.at[1], D, WIDE)
    r_up.start()
    ffn_sum[1].middle()
    r_gate.hook(1)
    middle_back(0)
    r_gate.hook(2)
    middle_back(1)
    finish_mixed(0)
    finish_mixed(1)
    a_back[0].relay()
    r_gate.hook(3)
    a_back[0].finish()
    back_attention(0)
    a_back[1].relay()
    r_up.hook(0)
    sent(ffn_sum[0])
    back_project(0)
    attn_sum[0].start()
    a_back[1].finish()
    grad_weight(heads, out_back, out_grad, 512, D)
    r_out.start()
    r_up.hook(1)
    back_attention(1)
    attn_sum[0].middle()
    r_up.hook(2)
    grad_weight(attn_in, proj_grad, qkv_grad, D, 768)
    r_qkv.start()
    r_up.hook(3)
    sent(ffn_sum[1])
    back_project(1)
    attn_sum[1].start()
    r_far.end()
    r_near.end()
    r_gate.end()
    attn_sum[1].middle()
    r_out.hook(0)
    r_out.hook(1)
    r_out.hook(2)
    r_out.hook(3)
    stores = [finish_tokens(0)]
    r_qkv.hook(0)
    r_qkv.hook(1)
    stores.append(finish_tokens(1))
    r_qkv.hook(2)
    r_qkv.hook(3)
    r_up.end()
    r_out.end()
    r_qkv.end()
    sum_everywhere()
    stores.append(copies.local(totals, totals_out, l_sem.at[1]))
    for copy in stores:
        copy.wait()
    copies.close()


def backward(saved, tokens, cot, gains, tables):
    low = jnp.bfloat16
    wide = jnp.float32
    shape = jax.ShapeDtypeStruct
    all_tokens = MICRO * TREE
    half = (WIDE // 2, OWN)
    blocks = [(OWN, 768), (512, OWN), (OWN, WIDE), (OWN, WIDE), half, half]
    outs = [shape((MICRO, OWN, D), low), shape((MICRO, OWN, D), wide)]
    outs += [shape(block, wide) for block in ((OWN, 768), (512, OWN), (2, OWN, WIDE), (WIDE, OWN))]
    outs += [shape((8, D), wide)]
    outs += [
        shape((all_tokens, WIDE), low), shape((all_tokens, WIDE), low), shape((all_tokens, D), low),
        shape((all_tokens, 768), low),
        shape((2, D, WIDE), low), shape((512, D), low), shape((D, 768), low),
    ]
    outs += [shape((NZ,) + block, low) for block in blocks[:5]]
    outs += [shape((1,) + blocks[5], low)]
    outs += [shape((NZ + 1,) + block, low) for block in blocks[:5]]
    outs += [shape((NZ + 1, WIDE // 2, NY * OWN), low)]
    dma = pltpu.SemaphoreType.DMA
    args = (*saved, tokens, cot, gains, *tables)
    return pl.pallas_call(
        backward_kernel,
        out_shape=outs,
        in_specs=[HBM] * len(args),
        out_specs=[HBM] * len(outs),
        scratch_shapes=[
            pltpu.VMEM((MICRO, NX * NC, OWN, D), low),
            pltpu.VMEM((MICRO, OWN, D), low),
            pltpu.VMEM((MICRO, OWN, D), low),
            pltpu.VMEM((2, MICRO, NX, OWN, D), low),
            pltpu.VMEM((2, MICRO, OWN, D), low),
            pltpu.VMEM((MICRO, OWN, D), wide),
            pltpu.VMEM((OWN, D), wide),
            pltpu.VMEM((OWN, D), low),
            pltpu.VMEM((MICRO, OWN, D), low),
            pltpu.VMEM((2, D), wide),
            pltpu.VMEM((8, D), wide),
            pltpu.VMEM((8, D), wide),
            pltpu.VMEM((TREE, 128), wide),
            pltpu.VMEM((TREE, 128), wide),
            pltpu.VMEM((TREE, 256), low),
            pltpu.VMEM((4, 8, D), wide),
            pltpu.VMEM((3, 8, D), wide),
            pltpu.VMEM((NZ, 8, D), wide),
            pltpu.VMEM((8, D), wide),
            dma((6, NZ)), dma((6, NZ)), dma((6, 3, 2)), dma((6, NZ + 1, 2)),
            dma((MICRO, 3)), dma((MICRO, NX * NC)), dma((MICRO,)),
            dma((3, MICRO, 3)), dma((3, MICRO, 3)), dma((6,)), dma((6,)), dma((3 + NZ,)),
        ],
        input_output_aliases={11: 7, 12: 8},
        compiler_params=pltpu.CompilerParams(
            collective_id=1, has_side_effects=True, vmem_limit_bytes=63 * 1024 * 1024
        ),
        cost_estimate=pl.CostEstimate(flops=140 * 10**9, bytes_accessed=5 * 10**8, transcendentals=10**7),
        name="backward",
    )(*args)


def update_kernel(
    g_qkv, g_out, g_gu, g_down, w_qkv, w_out, w_gu, w_down, mom_qkv, mom_out, mom_gu, mom_down, gains, mom_gains, totals,
    new_qkv, new_out, new_gu, new_down, moments_qkv, moments_out, moments_gu, moments_down,
    copy_qkv, copy_out, copy_gu, copy_down, new_gains, moments_gains,
):
    rates = step_rates()

    def step_of(grad, master, first, second, rate):
        clipped = totals[2:3, 0:1].reshape((1,) * grad.ndim) * grad
        first = beta_one * first + (1.0 - beta_one) * clipped
        second = beta_two * second + (1.0 - beta_two) * clipped * clipped
        first_hat = first / (1.0 - beta_one**STEP)
        second_hat = second / (1.0 - beta_two**STEP)
        updated = master - rate * (first_hat / (jnp.sqrt(second_hat) + adam_eps) + weight_decay * master)
        return updated, first, second

    def weight(rate, rows, grad, master, moments, new, new_moments, new_copy):
        def body(g_ref, w_ref, m_ref, new_ref, mom_ref, low_ref):
            updated, first, second = step_of(g_ref[...], w_ref[...], m_ref[0], m_ref[1], rate)
            new_ref[...] = updated
            mom_ref[0] = first
            mom_ref[1] = second
            low_ref[...] = updated.astype(jnp.bfloat16)

        rest = master.shape[1:]
        zeros = (0,) * len(rest)
        one = pl.BlockSpec((rows,) + rest, lambda i: (i,) + zeros)
        two = pl.BlockSpec((2, rows) + rest, lambda i: (0, i) + zeros)
        pltpu.emit_pipeline(
            body, grid=(master.shape[0] // rows,), in_specs=[one, one, two], out_specs=[one, two, one]
        )(grad, master, moments, new, new_moments, new_copy)

    weight(rates[2], 64, g_gu, w_gu, mom_gu, new_gu, moments_gu, copy_gu)
    weight(rates[3], 512, g_down, w_down, mom_down, new_down, moments_down, copy_down)
    weight(rates[1], 256, g_out, w_out, mom_out, new_out, moments_out, copy_out)
    weight(rates[0], 64, g_qkv, w_qkv, mom_qkv, new_qkv, moments_qkv, copy_qkv)
    updated, first, second = step_of(totals[0:2, :], gains[...], mom_gains[0], mom_gains[1], rates[4])
    new_gains[...] = updated
    moments_gains[0] = first
    moments_gains[1] = second


def update(grads, masters, states, gains, mom_gains, totals):
    shape = jax.ShapeDtypeStruct
    outs = [shape(master.shape, jnp.float32) for master in masters]
    outs += [shape(state.shape, jnp.float32) for state in states]
    outs += [shape(master.shape, jnp.bfloat16) for master in masters]
    outs += [shape(gains.shape, jnp.float32), shape(mom_gains.shape, jnp.float32)]
    whole = pl.BlockSpec(memory_space=pltpu.VMEM)
    return pl.pallas_call(
        update_kernel,
        out_shape=outs,
        in_specs=[HBM] * 12 + [whole] * 3,
        out_specs=[HBM] * 12 + [whole] * 2,
        compiler_params=pltpu.CompilerParams(vmem_limit_bytes=63 * 1024 * 1024),
        cost_estimate=pl.CostEstimate(flops=60 * 10**6, bytes_accessed=58 * 10**6, transcendentals=4 * 10**6),
        name="update",
    )(*grads, *masters, *states, gains, mom_gains, totals)


def fast_local(
    tokens,
    cotangent,
    segment_of,
    leaf_parent,
    w_qkv,
    mom_qkv,
    w_out,
    mom_out,
    w_gu,
    mom_gu,
    w_down,
    mom_down,
    gains,
    mom_gains,
):
    tables = [position_tables(segment_of[m], leaf_parent[m]) for m in range(MICRO)]
    tables = [jnp.concatenate([table[i] for table in tables], axis=0) for i in range(5)]
    saved = forward(tokens, cotangent, w_qkv, w_out, w_gu, w_down, gains, tables)
    mixed, d_tokens, g_qkv, g_out, g_gu, g_down, totals = backward(saved, tokens, cotangent, gains, tables)[:7]

    def flat(value, lead):
        return value.reshape(value.shape[:lead] + (-1, WIDE))

    masters = (w_qkv, w_out, flat(w_gu, 0), w_down)
    states = (mom_qkv, mom_out, flat(mom_gu, 1), mom_down)
    done = update(
        (g_qkv.reshape(w_qkv.shape), g_out, flat(g_gu, 0), g_down), masters, states, gains, mom_gains, totals
    )
    new, moments, copies = list(done[:4]), list(done[4:8]), list(done[8:12])
    new[2] = new[2].reshape(w_gu.shape)
    moments[2] = moments[2].reshape(mom_gu.shape)
    copies[2] = copies[2].reshape(w_gu.shape)
    results = []
    for i in range(4):
        results += [new[i], moments[i], copies[i]]
    return (mixed, d_tokens, totals[3, 0], *results, done[12], done[13])


def solution(mesh):
    placed = (
        P(None, ("row", "col"), None),
        P(None, ("row", "col"), None),
        P(None, "row"),
        P(None, "row"),
        P("row", "col", None),
        P(None, "row", "col", None),
        P("col", "row"),
        P(None, "col", "row"),
        P(None, "row", "col"),
        P(None, None, "row", "col"),
        P("col", "row"),
        P(None, "col", "row"),
        P(),
        P(),
    )
    sizes = dict(mesh.shape)
    fits = sizes == {"row": NZ * NY, "col": NX * NC}
    return jax.shard_map(
        fast_local if fits else local,
        mesh=mesh,
        in_specs=placed,
        out_specs=(
            P(None, ("row", "col"), None),
            P(None, ("row", "col"), None),
            P(),
            P("row", "col", None),
            P(None, "row", "col", None),
            P("row", "col", None),
            P("col", "row"),
            P(None, "col", "row"),
            P("col", "row"),
            P(None, "row", "col"),
            P(None, None, "row", "col"),
            P(None, "row", "col"),
            P("col", "row"),
            P(None, "col", "row"),
            P("col", "row"),
            P(),
            P(),
        ),
        check_vma=False,
    )
```
